256 devices in a mesh: tm: 8 (over x, z_lo), space: 32 (over y, z_hi, core).
Axes of the slice: x: 4, y: 4, z: 8 (z_hi: 4, z_lo: 2; z = z_hi * 2 + z_lo), core: 2. Of those that a mesh axis runs over, the one named last changes fastest.
Arguments:
- vectors: bfloat16 [8, 96, 2, 3, 4096], P('tm', None, None, None, 'space'), may hold values from -3 to 3
- gauge_links: bfloat16 [8, 3, 2, 3, 3, 4096], P('tm', None, None, None, None, 'space'), may hold values from -2.6875 to 2.6875
- momentum: int32 [3], replicated, may hold values from -2 to 2
- direction: int32 [8], P('tm'), may hold values from 0 to 2, as said below
Outputs:
- elementals: float32 [96, 8, 2, 9216], P('space', None, None, 'tm')
The draws below stay inside these ranges and needn't reach their ends.
Inputs may be any that keep to these rules, and one draw needn't show every extreme that they name: `direction`: entry t is 2 for even t; for odd t the entries alternate between 0 and 1 with a drawn first value.
All inputs are finite; a program needn't handle non-finite values.
Results may differ from the reference program's by a relative error of at most 0.0041.
Values may be sent and summed in bfloat16 or wider, within the bound.
No kernel may reach another device: no remote copies, remote signals or barrier semaphores. Data moves between devices by JAX's collectives and lax.ppermute only.
A program may use at most 128 MiB of HBM per device.

```python
import math
import jax
import jax.numpy as jnp
from jax import lax

NEV = 96
LX = 16
LY = 8
NT = 8
NZ = 32
VOLUME = 4096


def draw_direction(key, part):
    key = jax.random.fold_in(key, 7)
    first_value = jax.random.randint(key, (), 0, 2, dtype=jnp.int32)
    slice_index = jnp.arange(NT, dtype=jnp.int32)
    alternating = (first_value + slice_index // 2) % 2
    return jnp.where(slice_index % 2 == 0, 2, alternating).astype(jnp.int32)


def shard_levels(rng, shape, split, low, high):
    def one(axis_at, blocks):
        draws = jax.random.uniform(jax.random.fold_in(jax.random.fold_in(rng, 6), axis_at), (blocks,), jnp.float32, low / len(split), high / len(split))
        return jnp.repeat(jnp.exp(draws), shape[axis_at] // blocks).reshape((-1,) + (1,) * (len(shape) - axis_at - 1))

    factor_of = one(*split[0])
    for cut in split[1:]:
        factor_of = factor_of * one(*cut)
    return factor_of


def centred(stream_key, dims, spread, limit, cuts=(), kind=jnp.bfloat16):
    loudness = shard_levels(stream_key, dims, cuts, -0.22, 0.18) if cuts else 1.0
    result = jax.random.normal(stream_key, dims, jnp.float32) * spread * loudness
    return jnp.minimum(jnp.maximum(result, -limit), limit).astype(kind)


def setup_inputs(seed: int = 0) -> dict:
    seeds = jax.random.split(jax.random.key(seed), 5)
    vectors = centred(seeds[0], (NT, NEV, 2, 3, VOLUME), 0.5, 3.0, ((0, 8), (4, 32)))
    gauge_links = centred(seeds[1], (NT, 3, 2, 3, 3, VOLUME), 0.45, 2.6875, ((0, 8), (5, 32)))
    momentum = jax.random.randint(seeds[2], (3,), -2, 3).astype(jnp.int32)
    direction = draw_direction(jax.random.fold_in(seeds[4], 71), 0)
    return {"vectors": vectors, "gauge_links": gauge_links, "momentum": momentum, "direction": direction}


def select_axis(direction, options):
    shaped = direction.reshape((-1,) + (1,) * (options[0].ndim - 1))
    return jnp.where(shaped == 0, options[0], jnp.where(shaped == 1, options[1], options[2]))

def forward_x(site_field, x_coord):
    return jnp.where(x_coord == LX - 1, jnp.roll(site_field, LX - 1, -1), jnp.roll(site_field, -1, -1))

def backward_x(site_field, x_coord):
    return jnp.where(x_coord == 0, jnp.roll(site_field, 1 - LX, -1), jnp.roll(site_field, 1, -1))

def forward_y(site_field, y_coord):
    return jnp.where(y_coord == LY - 1, jnp.roll(site_field, (LY - 1) * LX, -1), jnp.roll(site_field, -LX, -1))

def backward_y(site_field, y_coord):
    return jnp.where(y_coord == 0, jnp.roll(site_field, (1 - LY) * LX, -1), jnp.roll(site_field, LX, -1))

def phase_table(momentum, z_first, z_extent, site_count):
    site_index = jnp.arange(site_count, dtype=jnp.int32)
    x_coord = site_index % LX
    y_coord = site_index // LX % LY
    z_coord = z_first + site_index // (LX * LY)
    full_turn = 2.0 * math.pi
    angle_x = full_turn * (jnp.mod(momentum[0] * x_coord, LX).astype(jnp.float32) / LX)
    angle_y = full_turn * (jnp.mod(momentum[1] * y_coord, LY).astype(jnp.float32) / LY)
    angle_z = full_turn * (jnp.mod(momentum[2] * z_coord, z_extent).astype(jnp.float32) / z_extent)
    phase_angle = angle_x + angle_y + angle_z
    return (jnp.cos(phase_angle), -jnp.sin(phase_angle))

def displace(vectors, gauge_links, lower_plane, upper_plane, lower_link, direction, cos_part, sin_part):
    site_count = vectors.shape[-1]
    plane_size = LX * LY
    site_index = jnp.arange(site_count, dtype=jnp.int32)
    x_coord = site_index % LX
    y_coord = site_index // LX % LY
    ahead_z = jnp.concatenate([vectors[..., plane_size:], upper_plane], -1)
    behind_z = jnp.concatenate([lower_plane, vectors[..., :site_count - plane_size]], -1)
    vector_ahead = select_axis(direction, (forward_x(vectors, x_coord), forward_y(vectors, y_coord), ahead_z)).astype(jnp.float32)
    vector_behind = select_axis(direction, (backward_x(vectors, x_coord), backward_y(vectors, y_coord), behind_z)).astype(jnp.float32)
    link_here = select_axis(direction, (gauge_links[:, 0], gauge_links[:, 1], gauge_links[:, 2])).astype(jnp.float32)
    link_z_back = jnp.concatenate([lower_link, gauge_links[:, 2, ..., :site_count - plane_size]], -1)
    link_back = select_axis(direction, (backward_x(gauge_links[:, 0], x_coord), backward_y(gauge_links[:, 1], y_coord), link_z_back)).astype(jnp.float32)
    here_re = link_here[:, 0][:, None]
    here_im = link_here[:, 1][:, None]
    ahead_re = vector_ahead[:, :, 0][:, :, None]
    ahead_im = vector_ahead[:, :, 1][:, :, None]
    front_re = lax.optimization_barrier(jnp.sum(here_re * ahead_re - here_im * ahead_im, axis=3))
    front_im = lax.optimization_barrier(jnp.sum(here_re * ahead_im + here_im * ahead_re, axis=3))
    dagger_re = jnp.swapaxes(link_back[:, 0], 1, 2)[:, None]
    dagger_im = jnp.swapaxes(link_back[:, 1], 1, 2)[:, None]
    behind_re = vector_behind[:, :, 0][:, :, None]
    behind_im = vector_behind[:, :, 1][:, :, None]
    rear_re = lax.optimization_barrier(jnp.sum(dagger_re * behind_re + dagger_im * behind_im, axis=3))
    rear_im = lax.optimization_barrier(jnp.sum(dagger_re * behind_im - dagger_im * behind_re, axis=3))
    moved_re = front_re - rear_re
    moved_im = front_im - rear_im
    phased_re = cos_part * moved_re - sin_part * moved_im
    phased_im = cos_part * moved_im + sin_part * moved_re
    return jnp.stack((phased_re, phased_im), axis=2).astype(jnp.bfloat16)

def left_operand(phased):
    phased_re = phased[:, :, 0]
    phased_im = phased[:, :, 1]
    upper_rows = jnp.stack((phased_re, -phased_im), axis=2)
    lower_rows = jnp.stack((phased_im, phased_re), axis=2)
    return jnp.stack((upper_rows, lower_rows), axis=1)

def cross_rows(row_vectors, all_vectors):
    left_float = row_vectors.astype(jnp.float32)[:, :, None]
    right_float = all_vectors.astype(jnp.float32)[:, None]
    real_parts = []
    imag_parts = []
    for colour in range(3):
        second_colour = (colour + 1) % 3
        third_colour = (colour + 2) % 3
        one_re = left_float[:, :, :, 0, second_colour] * right_float[:, :, :, 0, third_colour] - left_float[:, :, :, 1, second_colour] * right_float[:, :, :, 1, third_colour]
        one_im = left_float[:, :, :, 0, second_colour] * right_float[:, :, :, 1, third_colour] + left_float[:, :, :, 1, second_colour] * right_float[:, :, :, 0, third_colour]
        two_re = left_float[:, :, :, 0, third_colour] * right_float[:, :, :, 0, second_colour] - left_float[:, :, :, 1, third_colour] * right_float[:, :, :, 1, second_colour]
        two_im = left_float[:, :, :, 0, third_colour] * right_float[:, :, :, 1, second_colour] + left_float[:, :, :, 1, third_colour] * right_float[:, :, :, 0, second_colour]
        real_parts.append(one_re - two_re)
        imag_parts.append(one_im - two_im)
    return jnp.stack((jnp.stack(real_parts, 3), jnp.stack(imag_parts, 3)), 3).astype(jnp.bfloat16)

def reference(vectors, gauge_links, momentum, direction):
    slice_count = vectors.shape[0]
    site_count = vectors.shape[-1]
    plane_size = LX * LY
    cos_part, sin_part = phase_table(momentum, 0, NZ, site_count)
    block_rows = math.gcd(NEV, 8)

    def one_slice(slice_index):
        slice_vectors = lax.dynamic_slice_in_dim(vectors, slice_index, 1, 0)
        slice_links = lax.dynamic_slice_in_dim(gauge_links, slice_index, 1, 0)
        slice_direction = lax.dynamic_slice_in_dim(direction, slice_index, 1, 0)
        phased = displace(slice_vectors, slice_links, slice_vectors[..., site_count - plane_size:], slice_vectors[..., :plane_size], slice_links[:, 2, :, :, :, site_count - plane_size:], slice_direction, cos_part, sin_part)
        left_part = left_operand(phased).astype(jnp.float32)

        def one_block(block_index):
            block_vectors = lax.dynamic_slice_in_dim(slice_vectors, block_index * block_rows, block_rows, 1)
            crossed = cross_rows(block_vectors, slice_vectors).astype(jnp.float32)
            product = jnp.einsum('tcirax,tjkrax->jtcik', left_part, crossed, precision=lax.Precision.HIGHEST)
            return product.reshape(block_rows, 2, NEV * NEV)
        blocks_out = lax.map(one_block, jnp.arange(NEV // block_rows, dtype=jnp.int32))
        return blocks_out.reshape(NEV, 2, NEV * NEV)
    stacked = lax.map(one_slice, jnp.arange(slice_count, dtype=jnp.int32))
    normaliser = 1.0 / math.sqrt(LX * LY * NZ)
    return jnp.transpose(stacked, (1, 0, 2, 3)) * normaliser
```

```python
import math

import jax
import jax.numpy as jnp
from jax import lax
from jax.experimental import pallas as pl
from jax.experimental.pallas import tpu as pltpu
from jax.sharding import Mesh
from jax.sharding import PartitionSpec as P

NEV = 96
LX = 16
LY = 8
LZ = 32
SITES = 128
AXES = ("x", "zl", "y", "zh", "c")
SIZES = (4, 2, 4, 4, 2)
DEPTH = 6 * SITES


def ring_pairs(target):
    pairs = []
    for x in range(4):
        for zl in range(2):
            for s in range(32):
                to = target(zl, s)
                if to is not None:
                    head = (x * 2 + zl) * 32
                    pairs.append((head + s, head + to))
    return pairs


def outer_plane(zl, s):
    if zl == 1:
        return None
    return (s + 1) % 32 if s % 2 == 1 else (s - 1) % 32


def next_plane(zl, s):
    return (s + 1) % 32 if zl == 0 else None


def phased_kernel(scalars, own, other, outer, links, back, out, field, ahead, behind, rows):
    direction = scalars[3]
    plane = scalars[4]
    core = scalars[5]
    lane = lax.broadcasted_iota(jnp.int32, (1, SITES), 1)
    x_coord = lane % LX
    y_coord = lane // LX
    turns = (
        2 * jnp.bitwise_and(scalars[0] * x_coord, LX - 1)
        + 4 * jnp.bitwise_and(scalars[1] * y_coord, LY - 1)
        + jnp.bitwise_and(scalars[2] * plane, LZ - 1)
    )
    angle = (2.0 * math.pi / LZ) * jnp.bitwise_and(turns, LZ - 1).astype(jnp.float32)
    cos_part = jnp.cos(angle)
    sin_part = -jnp.sin(angle)

    @pl.when(direction == 2)
    def _():
        for comp in range(6):
            near = other[comp].astype(jnp.float32)
            far = outer[comp].astype(jnp.float32)
            ahead[comp] = jnp.where(core == 0, near, far)
            behind[comp] = jnp.where(core == 0, far, near)

    @pl.when(direction != 2)
    def _():
        step = jnp.where(direction == 0, 1, LX)
        last = jnp.logical_and(x_coord == LX - 1, direction == 0)
        first = jnp.logical_and(x_coord == 0, direction == 0)
        for comp in range(6):
            here = own[comp].astype(jnp.float32)
            ahead[comp] = jnp.where(
                last, pltpu.roll(here, LX - 1, 1), pltpu.roll(here, SITES - step, 1)
            )
            behind[comp] = jnp.where(
                first, pltpu.roll(here, SITES - LX + 1, 1), pltpu.roll(here, step, 1)
            )

    link = [links[d].astype(jnp.float32) for d in range(3)]
    here_link = jnp.where(
        direction == 0, link[0], jnp.where(direction == 1, link[1], link[2])
    )
    x_back = jnp.where(
        x_coord == 0, pltpu.roll(link[0], SITES - LX + 1, 1), pltpu.roll(link[0], 1, 1)
    )
    y_back = pltpu.roll(link[1], LX, 1)
    back_link = jnp.where(
        direction == 0,
        x_back,
        jnp.where(direction == 1, y_back, back[...].astype(jnp.float32)),
    )

    def matrix(table, part, row, column):
        at = part * 9 + row * 3 + column
        return table[at : at + 1]

    for a in range(3):
        front_re = front_im = rear_re = rear_im = 0.0
        for b in range(3):
            u_re, u_im = matrix(here_link, 0, a, b), matrix(here_link, 1, a, b)
            v_re, v_im = ahead[b], ahead[3 + b]
            front_re += u_re * v_re - u_im * v_im
            front_im += u_re * v_im + u_im * v_re
            w_re, w_im = matrix(back_link, 0, b, a), matrix(back_link, 1, b, a)
            v_re, v_im = behind[b], behind[3 + b]
            rear_re += w_re * v_re + w_im * v_im
            rear_im += w_re * v_im - w_im * v_re
        moved_re = front_re - rear_re
        moved_im = front_im - rear_im
        field[a] = cos_part * moved_re - sin_part * moved_im
        field[3 + a] = cos_part * moved_im + sin_part * moved_re

    for comp in range(6):
        for group in range(8):
            rows[pl.ds(24 * group, 12), :] = (
                field[comp, pl.ds(12 * group, 12), :]
                if comp < 3
                else -field[comp, pl.ds(12 * group, 12), :]
            )
            rows[pl.ds(24 * group + 12, 12), :] = field[
                (comp + 3) % 6, pl.ds(12 * group, 12), :
            ]
        out[:, comp * SITES : (comp + 1) * SITES] = rows[...].astype(jnp.bfloat16)


def product_kernel(scalars, own, other, left_own, left_other, out, vectors, left, crossed):
    step = pl.program_id(0)
    core = scalars[5]

    @pl.when(step == 0)
    def _():
        for comp in range(6):
            vectors[comp] = own[comp].astype(jnp.float32)
            vectors[6 + comp] = other[comp].astype(jnp.float32)
        left[:, :DEPTH] = left_own[...]
        left[:, DEPTH:] = left_other[...]

    def one_row(index, carry):
        high = index // 3
        low = index % 3
        j = 24 * step + 6 * high + 3 * core + low
        main = pl.multiple_of(256 * high + 96 * low, 32)
        tail = pl.multiple_of(jnp.where(low == 2, 1024 + 32 * high, main + 64), 32)
        for plane in range(2):
            mine = [vectors[6 * plane + comp, pl.ds(j, 1), :] for comp in range(6)]
            mine = [jnp.broadcast_to(m, (16, SITES)) for m in mine]
            for chunk in range(6):
                them = [
                    vectors[6 * plane + comp, 16 * chunk : 16 * chunk + 16, :]
                    for comp in range(6)
                ]
                if chunk < 4:
                    at = pl.multiple_of(main + 16 * chunk, 16)
                else:
                    at = pl.multiple_of(tail + 16 * (chunk - 4), 16)
                for a in range(3):
                    b = (a + 1) % 3
                    c = (a + 2) % 3
                    one_re = mine[b] * them[c] - mine[3 + b] * them[3 + c]
                    one_im = mine[b] * them[3 + c] + mine[3 + b] * them[c]
                    two_re = mine[c] * them[b] - mine[3 + c] * them[3 + b]
                    two_im = mine[c] * them[3 + b] + mine[3 + c] * them[b]
                    column = (6 * plane + a) * SITES
                    crossed[pl.ds(at, 16), column : column + SITES] = (
                        one_re - two_re
                    ).astype(jnp.bfloat16)
                    column += 3 * SITES
                    crossed[pl.ds(at, 16), column : column + SITES] = (
                        one_im - two_im
                    ).astype(jnp.bfloat16)
        return carry

    lax.fori_loop(0, 12, one_row, 0)
    for part in range(3):
        lanes = slice(384 * part, 384 * part + 384)
        product = lax.dot_general(
            left[...],
            crossed[lanes, :],
            (((1,), (1,)), ((), ())),
            preferred_element_type=jnp.float32,
        )
        for x in range(4):
            out[x, 0, :, lanes] = product[48 * x : 48 * x + 48].astype(jnp.bfloat16)


def plane_sum_kernel(parts, out):
    lane = lax.broadcasted_iota(jnp.int32, (24, SITES), 1)
    for zl in range(2):
        tails = []
        for x in range(4):
            total = parts[4 * x, 24 * zl : 24 * zl + 24, :].astype(jnp.float32)
            for y in range(1, 4):
                total += parts[4 * x + y, 24 * zl : 24 * zl + 24, :].astype(jnp.float32)
            for zh in range(4):
                for half in range(2):
                    lanes = 256 * zh + 128 * half
                    out[2 * zh + zl, 96 * half + 24 * x : 96 * half + 24 * x + 24, :] = total[
                        :, lanes : lanes + SITES
                    ].astype(jnp.bfloat16)
            tails.append(total[:, 1024:1152])
        for zh in range(4):
            joined = jnp.zeros((24, SITES), jnp.float32)
            for x in range(4):
                moved = pltpu.roll(tails[x], (32 * (x - zh)) % SITES, 1)
                joined = jnp.where(lane // 32 == x, moved, joined)
            out[2 * zh + zl, 192:216, :] = joined.astype(jnp.bfloat16)


def final_kernel(parts, out, rows):
    scale = 1.0 / math.sqrt(LX * LY * LZ)
    for zl in range(2):
        total = parts[zl].astype(jnp.float32)
        for zh in range(1, 4):
            total += parts[2 * zh + zl].astype(jnp.float32)
        total *= scale
        for x in range(4):
            t = 2 * x + zl
            rows[0, pl.ds(t, 24, 8), :] = total[24 * x : 24 * x + 24]
            rows[1, pl.ds(t, 24, 8), :] = total[96 + 24 * x : 96 + 24 * x + 24]
            tail = total[192:216]
            if x:
                tail = pltpu.roll(tail, SITES - 32 * x, 1)
            rows[2, pl.ds(t, 24, 8), :] = tail
    for ri in range(2):
        pieces = [[], [], []]
        for i in range(12):
            at = 8 * (12 * ri + i)
            one, two, three = (rows[part, at : at + 8, :] for part in range(3))
            pieces[0].append(one[:, :96])
            pieces[1].append(one[:, 96:])
            pieces[1].append(two[:, :64])
            pieces[2].append(two[:, 64:])
            pieces[2].append(three[:, :32])
        for r in range(3):
            out[r, ri] = jnp.concatenate(pieces[r], axis=1)


def vmem():
    return pl.BlockSpec(memory_space=pltpu.VMEM)


def smem():
    return pl.BlockSpec(memory_space=pltpu.SMEM)


def on_device(vectors, gauge_links, momentum, direction):
    core = lax.axis_index("c")
    plane = (lax.axis_index("y") * 4 + lax.axis_index("zh")) * 2 + core
    scalars = jnp.concatenate(
        [momentum, direction, jnp.stack([plane, core]).astype(jnp.int32)]
    )
    own = jnp.transpose(vectors[0], (1, 2, 0, 3)).reshape(6, NEV, SITES)
    links = gauge_links[0].reshape(3, 18, SITES)
    swap = [(0, 1), (1, 0)]
    outer = lax.ppermute(own, AXES, ring_pairs(outer_plane))
    back = lax.ppermute(links[2], AXES, ring_pairs(next_plane))
    other = lax.ppermute(own, "c", swap)
    f32 = jnp.float32
    bf16 = jnp.bfloat16
    left_own = pl.pallas_call(
        phased_kernel,
        out_shape=jax.ShapeDtypeStruct((192, DEPTH), bf16),
        in_specs=[smem(), vmem(), vmem(), vmem(), vmem(), vmem()],
        out_specs=vmem(),
        scratch_shapes=[
            pltpu.VMEM((6, NEV, SITES), f32),
            pltpu.VMEM((6, NEV, SITES), f32),
            pltpu.VMEM((6, NEV, SITES), f32),
            pltpu.VMEM((192, SITES), f32),
        ],
        compiler_params=pltpu.CompilerParams(vmem_limit_bytes=24 << 20),
    )(scalars, own, other, outer, links, back)
    left_other = lax.ppermute(left_own, "c", swap)
    partial = pl.pallas_call(
        product_kernel,
        grid=(4,),
        out_shape=jax.ShapeDtypeStruct((4, 4, 48, 1152), bf16),
        in_specs=[smem(), vmem(), vmem(), vmem(), vmem()],
        out_specs=pl.BlockSpec((4, 1, 48, 1152), lambda y: (0, y, 0, 0)),
        scratch_shapes=[
            pltpu.VMEM((12, NEV, SITES), f32),
            pltpu.VMEM((192, 2 * DEPTH), bf16),
            pltpu.VMEM((1152, 2 * DEPTH), bf16),
        ],
        compiler_params=pltpu.CompilerParams(vmem_limit_bytes=32 << 20),
    )(scalars, own, other, left_own, left_other)
    partial = lax.all_to_all(partial.reshape(16, 48, 1152), ("x", "y"), 0, 0, tiled=True)
    summed = pl.pallas_call(
        plane_sum_kernel,
        out_shape=jax.ShapeDtypeStruct((8, 216, SITES), bf16),
        in_specs=[vmem()],
        out_specs=vmem(),
        compiler_params=pltpu.CompilerParams(vmem_limit_bytes=24 << 20),
    )(partial)
    summed = lax.all_to_all(summed, ("zh", "zl"), 0, 0, tiled=True)
    result = pl.pallas_call(
        final_kernel,
        out_shape=jax.ShapeDtypeStruct((3, 2, 8, 12 * NEV), f32),
        in_specs=[vmem()],
        out_specs=vmem(),
        scratch_shapes=[pltpu.VMEM((3, 192, SITES), f32)],
        compiler_params=pltpu.CompilerParams(vmem_limit_bytes=24 << 20),
    )(summed)
    return jnp.transpose(result, (0, 2, 1, 3))


def solution(mesh):
    cut = Mesh(mesh.devices.reshape(SIZES), AXES)
    return jax.shard_map(
        on_device,
        mesh=cut,
        in_specs=(
            P(("x", "zl"), None, None, None, ("y", "zh", "c")),
            P(("x", "zl"), None, None, None, None, ("y", "zh", "c")),
            P(),
            P(("x", "zl")),
        ),
        out_specs=P(("y", "zh", "c"), None, None, ("x", "zl")),
        check_vma=False,
    )
```

```python
import math

import jax
import jax.numpy as jnp
from jax import lax
from jax.experimental import pallas as pl
from jax.experimental.pallas import tpu as pltpu
from jax.sharding import Mesh
from jax.sharding import PartitionSpec as P

NEV = 96
LX = 16
LY = 8
LZ = 32
SITES = 128
AXES = ("x", "zl", "y", "zh", "c")
SIZES = (4, 2, 4, 4, 2)
DEPTH = 6 * SITES


def ring_pairs(target):
    pairs = []
    for x in range(4):
        for zl in range(2):
            for s in range(32):
                to = target(zl, s)
                if to is not None:
                    head = (x * 2 + zl) * 32
                    pairs.append((head + s, head + to))
    return pairs


def outer_plane(zl, s):
    if zl == 1:
        return None
    return (s + 1) % 32 if s % 2 == 1 else (s - 1) % 32


def next_plane(zl, s):
    return (s + 1) % 32 if zl == 0 else None


def phased_kernel(momentum, direction_ref, own, other, outer, links, back, out, field, ahead, behind):
    direction = direction_ref[0]
    core = lax.axis_index("c")
    plane = (lax.axis_index("y") * 4 + lax.axis_index("zh")) * 2 + core
    lane = lax.broadcasted_iota(jnp.int32, (1, SITES), 1)
    x_coord = lane % LX
    y_coord = lane // LX
    turns = (
        2 * jnp.bitwise_and(momentum[0] * x_coord, LX - 1)
        + 4 * jnp.bitwise_and(momentum[1] * y_coord, LY - 1)
        + jnp.bitwise_and(momentum[2] * plane, LZ - 1)
    )
    angle = (2.0 * math.pi / LZ) * jnp.bitwise_and(turns, LZ - 1).astype(jnp.float32)
    cos_part = jnp.cos(angle)
    sin_part = -jnp.sin(angle)

    @pl.when(direction == 2)
    def _():
        for comp in range(6):
            near = other[comp].astype(jnp.float32)
            far = outer[comp].astype(jnp.float32)
            ahead[comp] = jnp.where(core == 0, near, far)
            behind[comp] = jnp.where(core == 0, far, near)

    @pl.when(direction != 2)
    def _():
        step = jnp.where(direction == 0, 1, LX)
        last = jnp.logical_and(x_coord == LX - 1, direction == 0)
        first = jnp.logical_and(x_coord == 0, direction == 0)
        for comp in range(6):
            here = own[comp].astype(jnp.float32)
            ahead[comp] = jnp.where(
                last, pltpu.roll(here, LX - 1, 1), pltpu.roll(here, SITES - step, 1)
            )
            behind[comp] = jnp.where(
                first, pltpu.roll(here, SITES - LX + 1, 1), pltpu.roll(here, step, 1)
            )

    link = [links[d].astype(jnp.float32) for d in range(3)]
    here_link = jnp.where(
        direction == 0, link[0], jnp.where(direction == 1, link[1], link[2])
    )
    x_back = jnp.where(
        x_coord == 0, pltpu.roll(link[0], SITES - LX + 1, 1), pltpu.roll(link[0], 1, 1)
    )
    y_back = pltpu.roll(link[1], LX, 1)
    back_link = jnp.where(
        direction == 0,
        x_back,
        jnp.where(direction == 1, y_back, back[...].astype(jnp.float32)),
    )

    def matrix(table, part, row, column):
        at = part * 9 + row * 3 + column
        return table[at : at + 1]

    for a in range(3):
        front_re = front_im = rear_re = rear_im = 0.0
        for b in range(3):
            u_re, u_im = matrix(here_link, 0, a, b), matrix(here_link, 1, a, b)
            v_re, v_im = ahead[b], ahead[3 + b]
            front_re += u_re * v_re - u_im * v_im
            front_im += u_re * v_im + u_im * v_re
            w_re, w_im = matrix(back_link, 0, b, a), matrix(back_link, 1, b, a)
            v_re, v_im = behind[b], behind[3 + b]
            rear_re += w_re * v_re + w_im * v_im
            rear_im += w_re * v_im - w_im * v_re
        moved_re = front_re - rear_re
        moved_im = front_im - rear_im
        field[a] = cos_part * moved_re - sin_part * moved_im
        field[3 + a] = cos_part * moved_im + sin_part * moved_re

    for comp in range(6):
        for pair in range(6):
            both = [field[comp, pl.ds(2 * pair + k, 8, 12), :] for k in range(2)]
            out[comp, 16 * pair : 16 * pair + 16, :] = jnp.concatenate(both, 0).astype(
                jnp.bfloat16
            )


def crossed_kernel(one, two, three, four, out, vectors):
    half = pl.program_id(0)
    core = lax.axis_index("c")
    first = 24 * lax.axis_index("y") + 3 * jnp.where(half == 0, 1 - core, core)

    @pl.when(half == 0)
    def _():
        for plane, source in enumerate((one, two, three, four)):
            for comp in range(6):
                vectors[6 * plane + comp] = source[comp].astype(jnp.float32)

    def one_row(index, carry):
        high = index // 3
        low = index % 3
        j = first + 6 * high + low
        main = pl.multiple_of(256 * high + 96 * low, 32)
        tail = pl.multiple_of(jnp.where(low == 2, 1024 + 32 * high, main + 64), 32)
        for plane in range(4):
            mine = [vectors[6 * plane + comp, pl.ds(j, 1), :] for comp in range(6)]
            mine = [jnp.broadcast_to(m, (16, SITES)) for m in mine]
            for chunk in range(6):
                them = [
                    vectors[6 * plane + comp, 16 * chunk : 16 * chunk + 16, :]
                    for comp in range(6)
                ]
                if chunk < 4:
                    at = pl.multiple_of(main + 16 * chunk, 16)
                else:
                    at = pl.multiple_of(tail + 16 * (chunk - 4), 16)
                for a in range(3):
                    b = (a + 1) % 3
                    c = (a + 2) % 3
                    one_re = mine[b] * them[c] - mine[3 + b] * them[3 + c]
                    one_im = mine[b] * them[3 + c] + mine[3 + b] * them[c]
                    two_re = mine[c] * them[b] - mine[3 + c] * them[3 + b]
                    two_im = mine[c] * them[3 + b] + mine[3 + c] * them[b]
                    column = (6 * plane + a) * SITES
                    out[0, pl.ds(at, 16), column : column + SITES] = (
                        one_re - two_re
                    ).astype(jnp.bfloat16)
                    column += 3 * SITES
                    out[0, pl.ds(at, 16), column : column + SITES] = (
                        one_im - two_im
                    ).astype(jnp.bfloat16)
        return carry

    lax.fori_loop(0, 12, one_row, 0)


def product_kernel(one, two, three, four, crossed, out, left):
    for plane, source in enumerate((one, two, three, four)):
        for a in range(3):
            real = source[a]
            imag = source[3 + a]
            column = (6 * plane + a) * SITES
            left[:NEV, column : column + SITES] = real
            left[NEV:, column : column + SITES] = imag
            column += 3 * SITES
            left[:NEV, column : column + SITES] = -imag
            left[NEV:, column : column + SITES] = real
    for lanes in (slice(0, 256), slice(256, 512), slice(512, 768), slice(768, 1152)):
        out[:, lanes] = lax.dot_general(
            left[...],
            crossed[0, lanes, :],
            (((1,), (1,)), ((), ())),
            preferred_element_type=jnp.float32,
        )


def pack_kernel(mine, received, out, total):
    lane = lax.broadcasted_iota(jnp.int32, (8, SITES), 1)
    for tile in range(9):
        lanes = slice(SITES * tile, SITES * tile + SITES)
        total[tile] = mine[:, lanes] + received[:, lanes]
    for q in range(8):
        for zh in range(4):
            for half in range(2):
                out[4 * q + zh, 24 * half : 24 * half + 24, :] = total[
                    2 * zh + half, pl.ds(q, 24, 8), :
                ].astype(jnp.bfloat16)
        tail = total[8, pl.ds(q, 24, 8), :]
        for zh in range(4):
            joined = jnp.zeros((8, SITES), jnp.float32)
            for g in range(3):
                moved = pltpu.roll(tail[8 * g : 8 * g + 8], (32 * (g - zh)) % SITES, 1)
                joined = jnp.where(lane // 32 == g, moved, joined)
            out[4 * q + zh, 48:56, :] = joined.astype(jnp.bfloat16)


def final_kernel(parts, out, rows):
    scale = 1.0 / math.sqrt(LX * LY * LZ)
    for t in range(8):
        total = parts[4 * t].astype(jnp.float32)
        for zh in range(1, 4):
            total += parts[4 * t + zh].astype(jnp.float32)
        total *= scale
        rows[0, pl.ds(t, 24, 8), :] = total[:24]
        rows[1, pl.ds(t, 24, 8), :] = total[24:48]
        for g in range(3):
            tail = total[48:56]
            if g:
                tail = pltpu.roll(tail, SITES - 32 * g, 1)
            rows[2, pl.ds(64 * g + t, 8, 8), :] = tail
    for ri in range(2):
        pieces = [[], [], []]
        for i in range(12):
            at = 8 * (12 * ri + i)
            one, two, three = (rows[part, at : at + 8, :] for part in range(3))
            pieces[0].append(one[:, :96])
            pieces[1].append(one[:, 96:])
            pieces[1].append(two[:, :64])
            pieces[2].append(two[:, 64:])
            pieces[2].append(three[:, :32])
        for r in range(3):
            out[r, :, ri, :] = jnp.concatenate(pieces[r], axis=1)


def vmem():
    return pl.BlockSpec(memory_space=pltpu.VMEM)


def smem():
    return pl.BlockSpec(memory_space=pltpu.SMEM)


def params(mib):
    return pltpu.CompilerParams(vmem_limit_bytes=mib << 20)


def from_y(block):
    return [
        lax.ppermute(block, "y", [(i, (i + by) % 4) for i in range(4)]) for by in (1, 3, 2)
    ]


def on_device(vectors, gauge_links, momentum, direction):
    f32 = jnp.float32
    bf16 = jnp.bfloat16
    swap = [(0, 1), (1, 0)]
    own = jnp.transpose(vectors[0], (1, 2, 0, 3)).reshape(6, NEV, SITES)
    links = gauge_links[0].reshape(3, 18, SITES)
    outer = lax.ppermute(own, AXES, ring_pairs(outer_plane))
    back = lax.ppermute(links[2], AXES, ring_pairs(next_plane))
    other = lax.ppermute(own, "c", swap)
    near = from_y(own)
    phased = pl.pallas_call(
        phased_kernel,
        out_shape=jax.ShapeDtypeStruct((6, NEV, SITES), bf16),
        in_specs=[smem(), smem()] + [vmem()] * 5,
        out_specs=vmem(),
        scratch_shapes=[pltpu.VMEM((6, NEV, SITES), f32)] * 3,
        compiler_params=params(24),
    )(momentum, direction, own, other, outer, links, back)
    phased_near = from_y(phased)
    crossed = pl.pallas_call(
        crossed_kernel,
        grid=(2,),
        out_shape=jax.ShapeDtypeStruct((2, 1152, 4 * DEPTH), bf16),
        in_specs=[vmem()] * 4,
        out_specs=pl.BlockSpec((1, 1152, 4 * DEPTH), lambda half: (half, 0, 0)),
        scratch_shapes=[pltpu.VMEM((24, NEV, SITES), f32)],
        compiler_params=params(32),
    )(own, *near)

    def product(half):
        return pl.pallas_call(
            product_kernel,
            grid=(1,),
            out_shape=jax.ShapeDtypeStruct((192, 1152), f32),
            in_specs=[vmem()] * 4
            + [pl.BlockSpec((1, 1152, 4 * DEPTH), lambda step: (half, 0, 0))],
            out_specs=vmem(),
            scratch_shapes=[pltpu.VMEM((192, 4 * DEPTH), bf16)],
            compiler_params=params(32),
        )(phased, *phased_near, crossed)

    received = lax.ppermute(product(0), "c", swap)
    mine = product(1)
    packed = pl.pallas_call(
        pack_kernel,
        out_shape=jax.ShapeDtypeStruct((32, 56, SITES), bf16),
        in_specs=[vmem()] * 2,
        out_specs=vmem(),
        scratch_shapes=[pltpu.VMEM((9, 192, SITES), f32)],
        compiler_params=params(16),
    )(mine, received)
    packed = lax.all_to_all(packed, ("x", "zl", "zh"), 0, 0, tiled=True)
    return pl.pallas_call(
        final_kernel,
        out_shape=jax.ShapeDtypeStruct((3, 8, 2, 12 * NEV), f32),
        in_specs=[vmem()],
        out_specs=vmem(),
        scratch_shapes=[pltpu.VMEM((3, 192, SITES), f32)],
        compiler_params=params(16),
    )(packed)


def solution(mesh):
    cut = Mesh(mesh.devices.reshape(SIZES), AXES)
    return jax.shard_map(
        on_device,
        mesh=cut,
        in_specs=(
            P(("x", "zl"), None, None, None, ("y", "zh", "c")),
            P(("x", "zl"), None, None, None, None, ("y", "zh", "c")),
            P(),
            P(("x", "zl")),
        ),
        out_specs=P(("y", "zh", "c"), None, None, ("x", "zl")),
        check_vma=False,
    )
```

```python
import math

import jax
import jax.numpy as jnp
from jax import lax
from jax.experimental import pallas as pl
from jax.experimental.pallas import tpu as pltpu
from jax.sharding import Mesh
from jax.sharding import PartitionSpec as P

NEV = 96
LX = 16
LY = 8
LZ = 32
SITES = 128
AXES = ("x", "zl", "y", "zh", "c")
SIZES = (4, 2, 4, 4, 2)
DEPTH = 6 * SITES


def ring_pairs(target):
    pairs = []
    for x in range(4):
        for zl in range(2):
            for s in range(32):
                to = target(zl, s)
                if to is not None:
                    head = (x * 2 + zl) * 32
                    pairs.append((head + s, head + to))
    return pairs


def outer_plane(zl, s):
    if zl == 1:
        return None
    return (s + 1) % 32 if s % 2 == 1 else (s - 1) % 32


def phased_kernel(scalars, own, other, outer, out, field, ahead, behind):
    direction = scalars[3]
    core = lax.axis_index("c")
    plane = (lax.axis_index("y") * 4 + lax.axis_index("zh")) * 2 + core
    lane = lax.broadcasted_iota(jnp.int32, (1, SITES), 1)
    x_coord = lane % LX
    y_coord = lane // LX
    turns = (
        2 * jnp.bitwise_and(scalars[0] * x_coord, LX - 1)
        + 4 * jnp.bitwise_and(scalars[1] * y_coord, LY - 1)
        + jnp.bitwise_and(scalars[2] * plane, LZ - 1)
    )
    angle = (2.0 * math.pi / LZ) * jnp.bitwise_and(turns, LZ - 1).astype(jnp.float32)
    cos_part = jnp.cos(angle)
    sin_part = -jnp.sin(angle)

    @pl.when(direction == 2)
    def _():
        for comp in range(6):
            near = other[NEV * comp : NEV * comp + NEV, :].astype(jnp.float32)
            far = outer[NEV * comp : NEV * comp + NEV, :].astype(jnp.float32)
            ahead[comp] = jnp.where(core == 0, near, far)
            behind[comp] = jnp.where(core == 0, far, near)

    @pl.when(direction != 2)
    def _():
        step = jnp.where(direction == 0, 1, LX)
        last = jnp.logical_and(x_coord == LX - 1, direction == 0)
        first = jnp.logical_and(x_coord == 0, direction == 0)
        for comp in range(6):
            here = own[NEV * comp : NEV * comp + NEV, :].astype(jnp.float32)
            ahead[comp] = jnp.where(
                last, pltpu.roll(here, LX - 1, 1), pltpu.roll(here, SITES - step, 1)
            )
            behind[comp] = jnp.where(
                first, pltpu.roll(here, SITES - LX + 1, 1), pltpu.roll(here, step, 1)
            )

    links = own[6 * NEV :, :].astype(jnp.float32)
    z_back = jnp.where(
        core == 0,
        outer[6 * NEV :, :].astype(jnp.float32),
        other[6 * NEV :, :].astype(jnp.float32),
    )
    x_roll = jnp.where(
        x_coord == 0, pltpu.roll(links, SITES - LX + 1, 1), pltpu.roll(links, 1, 1)
    )
    y_roll = pltpu.roll(links, LX, 1)

    def matrix(table, part, row, column):
        return table[part * 9 + row * 3 + column]

    here_link = []
    back_link = []
    for at in range(18):
        x_at, y_at, z_at = (slice(at + 18 * d, at + 18 * d + 1) for d in range(3))
        here_link.append(
            jnp.where(
                direction == 0, links[x_at], jnp.where(direction == 1, links[y_at], links[z_at])
            )
        )
        back_link.append(
            jnp.where(
                direction == 0,
                x_roll[x_at],
                jnp.where(direction == 1, y_roll[y_at], z_back[z_at]),
            )
        )

    for a in range(3):
        front_re = front_im = rear_re = rear_im = 0.0
        for b in range(3):
            u_re, u_im = matrix(here_link, 0, a, b), matrix(here_link, 1, a, b)
            v_re, v_im = ahead[b], ahead[3 + b]
            front_re += u_re * v_re - u_im * v_im
            front_im += u_re * v_im + u_im * v_re
            w_re, w_im = matrix(back_link, 0, b, a), matrix(back_link, 1, b, a)
            v_re, v_im = behind[b], behind[3 + b]
            rear_re += w_re * v_re + w_im * v_im
            rear_im += w_re * v_im - w_im * v_re
        moved_re = front_re - rear_re
        moved_im = front_im - rear_im
        field[a] = cos_part * moved_re - sin_part * moved_im
        field[3 + a] = cos_part * moved_im + sin_part * moved_re

    for comp in range(6):
        for pair in range(6):
            both = [field[comp, pl.ds(2 * pair + k, 8, 12), :] for k in range(2)]
            out[comp, 16 * pair : 16 * pair + 16, :] = jnp.concatenate(both, 0).astype(
                jnp.bfloat16
            )


def cross_rows(vectors, j, at_main, at_tail, out):
    for plane in range(4):
        mine = [vectors[6 * plane + comp, pl.ds(j, 1), :] for comp in range(6)]
        mine = [jnp.broadcast_to(m, (16, SITES)) for m in mine]
        for chunk in range(6):
            them = [
                vectors[6 * plane + comp, 16 * chunk : 16 * chunk + 16, :]
                for comp in range(6)
            ]
            if chunk < 4:
                at = pl.multiple_of(at_main + 16 * chunk, 16)
            else:
                at = pl.multiple_of(at_tail + 16 * (chunk - 4), 16)
            for a in range(3):
                b = (a + 1) % 3
                c = (a + 2) % 3
                one_re = mine[b] * them[c] - mine[3 + b] * them[3 + c]
                one_im = mine[b] * them[3 + c] + mine[3 + b] * them[c]
                two_re = mine[c] * them[b] - mine[3 + c] * them[3 + b]
                two_im = mine[c] * them[3 + b] + mine[3 + c] * them[b]
                column = (6 * plane + a) * SITES
                out[pl.ds(at, 16), column : column + SITES] = (one_re - two_re).astype(
                    jnp.bfloat16
                )
                column += 3 * SITES
                out[pl.ds(at, 16), column : column + SITES] = (one_im - two_im).astype(
                    jnp.bfloat16
                )


def cross_place(high, low):
    main = 256 * high + 96 * low
    tail = 1024 + 32 * high if low == 2 else main + 64
    return main, tail


def crossed_kernel(one, two, three, four, out, vectors):
    first = 24 * lax.axis_index("y") + 3 * (1 - lax.axis_index("c"))
    for plane, source in enumerate((one, two, three, four)):
        for comp in range(6):
            vectors[6 * plane + comp] = source[NEV * comp : NEV * comp + NEV, :].astype(
                jnp.float32
            )

    def three_rows(high, carry):
        for low in range(3):
            cross_rows(vectors, first + 6 * high + low, *cross_place(high, low), out)
        return carry

    lax.fori_loop(0, 4, three_rows, 0)


def multiply(left, crossed, out, start, size):
    out[:, start : start + size] = lax.dot_general(
        left[...],
        crossed[start : start + size, :],
        (((1,), (1,)), ((), ())),
        preferred_element_type=jnp.float32,
    )


def half_kernel(
    one, two, three, four, p_one, p_two, p_three, p_four, theirs, product, mine, left, vectors
):
    first = 24 * lax.axis_index("y") + 3 * lax.axis_index("c")
    for plane, source in enumerate((one, two, three, four)):
        for comp in range(6):
            vectors[6 * plane + comp] = source[NEV * comp : NEV * comp + NEV, :].astype(
                jnp.float32
            )
    for plane, source in enumerate((p_one, p_two, p_three, p_four)):
        for a in range(3):
            real = source[a]
            imag = source[3 + a]
            column = (6 * plane + a) * SITES
            left[:NEV, column : column + SITES] = real
            left[NEV:, column : column + SITES] = imag
            column += 3 * SITES
            left[:NEV, column : column + SITES] = -imag
            left[NEV:, column : column + SITES] = real
    for high in range(4):
        multiply(left, theirs, product, 256 * high, 256)
        for low in range(3):
            cross_rows(vectors, first + 6 * high + low, *cross_place(high, low), mine)
    multiply(left, theirs, product, 1024, 128)


def product_kernel(left, crossed, out):
    for start, size in ((0, 256), (256, 256), (512, 256), (768, 256), (1024, 128)):
        multiply(left, crossed, out, start, size)


def pack_kernel(mine, received, out, total):
    lane = lax.broadcasted_iota(jnp.int32, (8, SITES), 1)
    for tile in range(9):
        lanes = slice(SITES * tile, SITES * tile + SITES)
        total[tile] = mine[:, lanes] + received[:, lanes]
    for q in range(8):
        for zh in range(4):
            for half in range(2):
                out[4 * q + zh, 24 * half : 24 * half + 24, :] = total[
                    2 * zh + half, pl.ds(q, 24, 8), :
                ].astype(jnp.bfloat16)
        tail = total[8, pl.ds(q, 24, 8), :]
        for zh in range(4):
            joined = jnp.zeros((8, SITES), jnp.float32)
            for g in range(3):
                moved = pltpu.roll(tail[8 * g : 8 * g + 8], (32 * (g - zh)) % SITES, 1)
                joined = jnp.where(lane // 32 == g, moved, joined)
            out[4 * q + zh, 48:56, :] = joined.astype(jnp.bfloat16)


def final_kernel(parts, out, rows):
    scale = 1.0 / math.sqrt(LX * LY * LZ)
    for t in range(8):
        total = parts[4 * t].astype(jnp.float32)
        for zh in range(1, 4):
            total += parts[4 * t + zh].astype(jnp.float32)
        total *= scale
        rows[0, pl.ds(t, 24, 8), :] = total[:24]
        rows[1, pl.ds(t, 24, 8), :] = total[24:48]
        for g in range(3):
            tail = total[48:56]
            if g:
                tail = pltpu.roll(tail, SITES - 32 * g, 1)
            rows[2, pl.ds(64 * g + t, 8, 8), :] = tail
    for ri in range(2):
        pieces = [[], [], []]
        for i in range(12):
            at = 8 * (12 * ri + i)
            one, two, three = (rows[part, at : at + 8, :] for part in range(3))
            pieces[0].append(one[:, :96])
            pieces[1].append(one[:, 96:])
            pieces[1].append(two[:, :64])
            pieces[2].append(two[:, 64:])
            pieces[2].append(three[:, :32])
        for r in range(3):
            out[r, :, ri, :] = jnp.concatenate(pieces[r], axis=1)


def vmem():
    return pl.BlockSpec(memory_space=pltpu.VMEM)


def smem():
    return pl.BlockSpec(memory_space=pltpu.SMEM)


def params(mib):
    return pltpu.CompilerParams(vmem_limit_bytes=mib << 20)


def from_y(block):
    return [
        lax.ppermute(block, "y", [(i, (i + by) % 4) for i in range(4)]) for by in (1, 3, 2)
    ]


def on_device(vectors, gauge_links, momentum, direction):
    f32 = jnp.float32
    bf16 = jnp.bfloat16
    swap = [(0, 1), (1, 0)]
    own = jnp.concatenate(
        [
            jnp.transpose(vectors[0], (1, 2, 0, 3)).reshape(6 * NEV, SITES),
            gauge_links[0].reshape(54, SITES),
            jnp.zeros((10, SITES), bf16),
        ]
    )
    scalars = jnp.concatenate([momentum, direction])
    outer = lax.ppermute(own, AXES, ring_pairs(outer_plane))
    other = lax.ppermute(own, "c", swap)
    near = from_y(own)
    phased = pl.pallas_call(
        phased_kernel,
        out_shape=jax.ShapeDtypeStruct((6, NEV, SITES), bf16),
        in_specs=[smem()] + [vmem()] * 3,
        out_specs=vmem(),
        scratch_shapes=[pltpu.VMEM((6, NEV, SITES), f32)] * 3,
        compiler_params=params(8),
    )(scalars, own, other, outer)
    phased_near = from_y(phased)
    theirs = pl.pallas_call(
        crossed_kernel,
        out_shape=jax.ShapeDtypeStruct((1152, 4 * DEPTH), bf16),
        in_specs=[vmem()] * 4,
        out_specs=vmem(),
        scratch_shapes=[pltpu.VMEM((24, NEV, SITES), f32)],
        compiler_params=params(8),
    )(own, *near)
    sent, crossed, left = pl.pallas_call(
        half_kernel,
        out_shape=(
            jax.ShapeDtypeStruct((192, 1152), f32),
            jax.ShapeDtypeStruct((1152, 4 * DEPTH), bf16),
            jax.ShapeDtypeStruct((192, 4 * DEPTH), bf16),
        ),
        in_specs=[vmem()] * 9,
        out_specs=(vmem(), vmem(), vmem()),
        scratch_shapes=[pltpu.VMEM((24, NEV, SITES), f32)],
        compiler_params=params(12),
    )(own, *near, phased, *phased_near, theirs)
    received = lax.ppermute(sent, "c", swap)
    mine = pl.pallas_call(
        product_kernel,
        out_shape=jax.ShapeDtypeStruct((192, 1152), f32),
        in_specs=[vmem()] * 2,
        out_specs=vmem(),
        compiler_params=params(8),
    )(left, crossed)
    packed = pl.pallas_call(
        pack_kernel,
        out_shape=jax.ShapeDtypeStruct((32, 56, SITES), bf16),
        in_specs=[vmem()] * 2,
        out_specs=vmem(),
        scratch_shapes=[pltpu.VMEM((9, 192, SITES), f32)],
        compiler_params=params(16),
    )(mine, received)
    packed = lax.all_to_all(packed, ("x", "zl", "zh"), 0, 0, tiled=True)
    return pl.pallas_call(
        final_kernel,
        out_shape=jax.ShapeDtypeStruct((3, 8, 2, 12 * NEV), f32),
        in_specs=[vmem()],
        out_specs=vmem(),
        scratch_shapes=[pltpu.VMEM((3, 192, SITES), f32)],
        compiler_params=params(16),
    )(packed)


def solution(mesh):
    cut = Mesh(mesh.devices.reshape(SIZES), AXES)
    return jax.shard_map(
        on_device,
        mesh=cut,
        in_specs=(
            P(("x", "zl"), None, None, None, ("y", "zh", "c")),
            P(("x", "zl"), None, None, None, None, ("y", "zh", "c")),
            P(),
            P(("x", "zl")),
        ),
        out_specs=P(("y", "zh", "c"), None, None, ("x", "zl")),
        check_vma=False,
    )
```

```python
import math

import jax
import jax.numpy as jnp
from jax import lax
from jax.experimental import pallas as pl
from jax.experimental.pallas import tpu as pltpu
from jax.sharding import Mesh
from jax.sharding import PartitionSpec as P

NEV = 96
LX = 16
LY = 8
LZ = 32
SITES = 128
AXES = ("x", "zl", "y", "zh", "c")
SIZES = (4, 2, 4, 4, 2)
DEPTH = 6 * SITES


def ring_pairs(target):
    pairs = []
    for x in range(4):
        for zl in range(2):
            for s in range(32):
                to = target(zl, s)
                if to is not None:
                    head = (x * 2 + zl) * 32
                    pairs.append((head + s, head + to))
    return pairs


def outer_plane(zl, s):
    if zl == 1:
        return None
    return (s + 1) % 32 if s % 2 == 1 else (s - 1) % 32


def phased_kernel(momentum, direction_ref, own, other, outer, out, field, ahead, behind):
    direction = direction_ref[0]
    core = lax.axis_index("c")
    plane = (lax.axis_index("y") * 4 + lax.axis_index("zh")) * 2 + core
    lane = lax.broadcasted_iota(jnp.int32, (1, SITES), 1)
    x_coord = lane % LX
    y_coord = lane // LX
    turns = (
        2 * jnp.bitwise_and(momentum[0] * x_coord, LX - 1)
        + 4 * jnp.bitwise_and(momentum[1] * y_coord, LY - 1)
        + jnp.bitwise_and(momentum[2] * plane, LZ - 1)
    )
    angle = (2.0 * math.pi / LZ) * jnp.bitwise_and(turns, LZ - 1).astype(jnp.float32)
    cos_part = jnp.cos(angle)
    sin_part = -jnp.sin(angle)

    @pl.when(direction == 2)
    def _():
        for comp in range(6):
            near = other[NEV * comp : NEV * comp + NEV, :].astype(jnp.float32)
            far = outer[NEV * comp : NEV * comp + NEV, :].astype(jnp.float32)
            ahead[comp] = jnp.where(core == 0, near, far)
            behind[comp] = jnp.where(core == 0, far, near)

    @pl.when(direction != 2)
    def _():
        step = jnp.where(direction == 0, 1, LX)
        last = jnp.logical_and(x_coord == LX - 1, direction == 0)
        first = jnp.logical_and(x_coord == 0, direction == 0)
        for comp in range(6):
            here = own[NEV * comp : NEV * comp + NEV, :].astype(jnp.float32)
            ahead[comp] = jnp.where(
                last, pltpu.roll(here, LX - 1, 1), pltpu.roll(here, SITES - step, 1)
            )
            behind[comp] = jnp.where(
                first, pltpu.roll(here, SITES - LX + 1, 1), pltpu.roll(here, step, 1)
            )

    links = own[6 * NEV :, :].astype(jnp.float32)
    z_back = jnp.where(
        core == 0,
        outer[6 * NEV :, :].astype(jnp.float32),
        other[6 * NEV :, :].astype(jnp.float32),
    )
    x_roll = jnp.where(
        x_coord == 0, pltpu.roll(links, SITES - LX + 1, 1), pltpu.roll(links, 1, 1)
    )
    y_roll = pltpu.roll(links, LX, 1)

    def matrix(table, part, row, column):
        return table[part * 9 + row * 3 + column]

    here_link = []
    back_link = []
    for at in range(18):
        x_at, y_at, z_at = (slice(at + 18 * d, at + 18 * d + 1) for d in range(3))
        here_link.append(
            jnp.where(
                direction == 0, links[x_at], jnp.where(direction == 1, links[y_at], links[z_at])
            )
        )
        back_link.append(
            jnp.where(
                direction == 0,
                x_roll[x_at],
                jnp.where(direction == 1, y_roll[y_at], z_back[z_at]),
            )
        )

    for a in range(3):
        front_re = front_im = rear_re = rear_im = 0.0
        for b in range(3):
            u_re, u_im = matrix(here_link, 0, a, b), matrix(here_link, 1, a, b)
            v_re, v_im = ahead[b], ahead[3 + b]
            front_re += u_re * v_re - u_im * v_im
            front_im += u_re * v_im + u_im * v_re
            w_re, w_im = matrix(back_link, 0, b, a), matrix(back_link, 1, b, a)
            v_re, v_im = behind[b], behind[3 + b]
            rear_re += w_re * v_re + w_im * v_im
            rear_im += w_re * v_im - w_im * v_re
        moved_re = front_re - rear_re
        moved_im = front_im - rear_im
        field[a] = cos_part * moved_re - sin_part * moved_im
        field[3 + a] = cos_part * moved_im + sin_part * moved_re

    for comp in range(6):
        for pair in range(6):
            both = [field[comp, pl.ds(2 * pair + k, 8, 12), :] for k in range(2)]
            out[comp, 16 * pair : 16 * pair + 16, :] = jnp.concatenate(both, 0).astype(
                jnp.bfloat16
            )


def crossed_kernel(source, out, vectors):
    core = lax.axis_index("c")
    first = 24 * lax.axis_index("y")
    for comp in range(6):
        vectors[comp] = source[NEV * comp : NEV * comp + NEV, :].astype(jnp.float32)

    def three_rows(step, carry):
        half = step // 4
        high = step % 4
        keeper = jnp.where(half == 0, 1 - core, core)
        for low in range(3):
            j = first + 6 * high + 3 * keeper + low
            main = 1152 * half + 256 * high + 96 * low
            tail = 1152 * half + 1024 + 32 * high if low == 2 else main + 64
            mine = [vectors[comp, pl.ds(j, 1), :] for comp in range(6)]
            mine = [jnp.broadcast_to(m, (16, SITES)) for m in mine]
            for chunk in range(6):
                them = [vectors[comp, 16 * chunk : 16 * chunk + 16, :] for comp in range(6)]
                if chunk < 4:
                    at = pl.multiple_of(main + 16 * chunk, 16)
                else:
                    at = pl.multiple_of(tail + 16 * (chunk - 4), 16)
                for a in range(3):
                    b = (a + 1) % 3
                    c = (a + 2) % 3
                    one_re = mine[b] * them[c] - mine[3 + b] * them[3 + c]
                    one_im = mine[b] * them[3 + c] + mine[3 + b] * them[c]
                    two_re = mine[c] * them[b] - mine[3 + c] * them[3 + b]
                    two_im = mine[c] * them[3 + b] + mine[3 + c] * them[b]
                    column = a * SITES
                    out[pl.ds(at, 16), column : column + SITES] = (one_re - two_re).astype(
                        jnp.bfloat16
                    )
                    column += 3 * SITES
                    out[pl.ds(at, 16), column : column + SITES] = (one_im - two_im).astype(
                        jnp.bfloat16
                    )
        return carry

    lax.fori_loop(0, 8, three_rows, 0)


def multiply(lefts, crossed, out, half):
    for at, size in ((0, 256), (256, 256), (512, 256), (768, 256), (1024, 128)):
        total = None
        for left, rows in zip(lefts, crossed):
            term = lax.dot_general(
                left,
                rows[1152 * half + at : 1152 * half + at + size, :],
                (((1,), (1,)), ((), ())),
                preferred_element_type=jnp.float32,
            )
            total = term if total is None else total + term
        out[:, at : at + size] = total


def half_kernel(p_one, p_two, p_three, p_four, one, two, three, four, out, left):
    for plane, source in enumerate((p_one, p_two, p_three, p_four)):
        for a in range(3):
            real = source[a]
            imag = source[3 + a]
            column = a * SITES
            left[plane, :NEV, column : column + SITES] = real
            left[plane, NEV:, column : column + SITES] = imag
            column += 3 * SITES
            left[plane, :NEV, column : column + SITES] = -imag
            left[plane, NEV:, column : column + SITES] = real
    multiply([left[plane] for plane in range(4)], (one, two, three, four), out, 0)


def product_kernel(left, one, two, three, four, out):
    multiply([left[plane] for plane in range(4)], (one, two, three, four), out, 1)


def pack_kernel(mine, received, out, total):
    lane = lax.broadcasted_iota(jnp.int32, (8, SITES), 1)
    for tile in range(9):
        lanes = slice(SITES * tile, SITES * tile + SITES)
        total[tile] = mine[:, lanes] + received[:, lanes]
    for q in range(8):
        for zh in range(4):
            for half in range(2):
                out[4 * q + zh, 24 * half : 24 * half + 24, :] = total[
                    2 * zh + half, pl.ds(q, 24, 8), :
                ].astype(jnp.bfloat16)
        tail = total[8, pl.ds(q, 24, 8), :]
        for zh in range(4):
            joined = jnp.zeros((8, SITES), jnp.float32)
            for g in range(3):
                moved = pltpu.roll(tail[8 * g : 8 * g + 8], (32 * (g - zh)) % SITES, 1)
                joined = jnp.where(lane // 32 == g, moved, joined)
            out[4 * q + zh, 48:56, :] = joined.astype(jnp.bfloat16)


def final_kernel(parts, out, rows):
    scale = 1.0 / math.sqrt(LX * LY * LZ)
    for t in range(8):
        total = parts[4 * t].astype(jnp.float32)
        for zh in range(1, 4):
            total += parts[4 * t + zh].astype(jnp.float32)
        total *= scale
        rows[0, pl.ds(t, 24, 8), :] = total[:24]
        rows[1, pl.ds(t, 24, 8), :] = total[24:48]
        for g in range(3):
            tail = total[48:56]
            if g:
                tail = pltpu.roll(tail, SITES - 32 * g, 1)
            rows[2, pl.ds(64 * g + t, 8, 8), :] = tail
    for ri in range(2):
        pieces = [[], [], []]
        for i in range(12):
            at = 8 * (12 * ri + i)
            one, two, three = (rows[part, at : at + 8, :] for part in range(3))
            pieces[0].append(one[:, :96])
            pieces[1].append(one[:, 96:])
            pieces[1].append(two[:, :64])
            pieces[2].append(two[:, 64:])
            pieces[2].append(three[:, :32])
        for r in range(3):
            out[r, :, ri, :] = jnp.concatenate(pieces[r], axis=1)


def vmem():
    return pl.BlockSpec(memory_space=pltpu.VMEM)


def smem():
    return pl.BlockSpec(memory_space=pltpu.SMEM)


def params(mib):
    return pltpu.CompilerParams(vmem_limit_bytes=mib << 20)


def from_y(block, by):
    return lax.ppermute(block, "y", [(i, (i + by) % 4) for i in range(4)])


def on_device(vectors, gauge_links, momentum, direction):
    f32 = jnp.float32
    bf16 = jnp.bfloat16
    swap = [(0, 1), (1, 0)]
    own = jnp.transpose(vectors[0], (1, 2, 0, 3)).reshape(6 * NEV, SITES)
    joined = jnp.concatenate(
        [own, gauge_links[0].reshape(54, SITES), jnp.zeros((10, SITES), bf16)]
    )
    outer = lax.ppermute(joined, AXES, ring_pairs(outer_plane))
    other = lax.ppermute(joined, "c", swap)
    before = from_y(own, 1)
    after = from_y(own, 3)
    opposite = from_y(after, 3)
    phased = pl.pallas_call(
        phased_kernel,
        out_shape=jax.ShapeDtypeStruct((6, NEV, SITES), bf16),
        in_specs=[vmem()] * 5,
        out_specs=vmem(),
        scratch_shapes=[pltpu.VMEM((6, NEV, SITES), f32)] * 3,
        compiler_params=params(8),
    )(momentum, direction, joined, other, outer)
    phased_before = from_y(phased, 1)
    phased_after = from_y(phased, 3)

    def crossed(source):
        return pl.pallas_call(
            crossed_kernel,
            out_shape=jax.ShapeDtypeStruct((2304, DEPTH), bf16),
            in_specs=[vmem()],
            out_specs=vmem(),
            scratch_shapes=[pltpu.VMEM((6, NEV, SITES), f32)],
            compiler_params=params(4),
        )(source)

    one = crossed(own)
    before, one = lax.optimization_barrier((before, one))
    two = crossed(before)
    phased_before, two = lax.optimization_barrier((phased_before, two))
    phased_opposite = from_y(phased_before, 1)
    after, two = lax.optimization_barrier((after, two))
    planes = [one, two] + [crossed(source) for source in (after, opposite)]
    sent, left = pl.pallas_call(
        half_kernel,
        out_shape=(
            jax.ShapeDtypeStruct((192, 1152), f32),
            jax.ShapeDtypeStruct((4, 192, DEPTH), bf16),
        ),
        in_specs=[vmem()] * 8,
        out_specs=(vmem(), vmem()),
        compiler_params=params(8),
    )(phased, phased_before, phased_after, phased_opposite, *planes)
    received = lax.ppermute(sent, "c", swap)
    mine = pl.pallas_call(
        product_kernel,
        out_shape=jax.ShapeDtypeStruct((192, 1152), f32),
        in_specs=[vmem()] * 5,
        out_specs=vmem(),
        compiler_params=params(8),
    )(left, *planes)
    packed = pl.pallas_call(
        pack_kernel,
        out_shape=jax.ShapeDtypeStruct((32, 56, SITES), bf16),
        in_specs=[vmem()] * 2,
        out_specs=vmem(),
        scratch_shapes=[pltpu.VMEM((9, 192, SITES), f32)],
        compiler_params=params(16),
    )(mine, received)
    packed = lax.all_to_all(packed, ("x", "zl", "zh"), 0, 0, tiled=True)
    return pl.pallas_call(
        final_kernel,
        out_shape=jax.ShapeDtypeStruct((3, 8, 2, 12 * NEV), f32),
        in_specs=[vmem()],
        out_specs=vmem(),
        scratch_shapes=[pltpu.VMEM((3, 192, SITES), f32)],
        compiler_params=params(16),
    )(packed)


def solution(mesh):
    cut = Mesh(mesh.devices.reshape(SIZES), AXES)
    return jax.shard_map(
        on_device,
        mesh=cut,
        in_specs=(
            P(("x", "zl"), None, None, None, ("y", "zh", "c")),
            P(("x", "zl"), None, None, None, None, ("y", "zh", "c")),
            P(),
            P(("x", "zl")),
        ),
        out_specs=P(("y", "zh", "c"), None, None, ("x", "zl")),
        check_vma=False,
    )
```

```python
import math

import jax
import jax.numpy as jnp
from jax import lax
from jax.experimental import pallas as pl
from jax.experimental.pallas import tpu as pltpu
from jax.sharding import Mesh
from jax.sharding import PartitionSpec as P

NEV = 96
LX = 16
LY = 8
LZ = 32
SITES = 128
AXES = ("x", "zl", "y", "zh", "c")
SIZES = (4, 2, 4, 4, 2)
DEPTH = 6 * SITES


def ring_pairs(target):
    pairs = []
    for x in range(4):
        for zl in range(2):
            for s in range(32):
                to = target(zl, s)
                if to is not None:
                    head = (x * 2 + zl) * 32
                    pairs.append((head + s, head + to))
    return pairs


def outer_plane(zl, s):
    if zl == 1:
        return None
    return (s + 1) % 32 if s % 2 == 1 else (s - 1) % 32


def phased_kernel(momentum, direction_ref, own, other, outer, out, field, ahead, behind):
    links = own[6 * NEV :, :].astype(jnp.float32)
    direction = direction_ref[0]
    core = lax.axis_index("c")
    plane = (lax.axis_index("y") * 4 + lax.axis_index("zh")) * 2 + core
    lane = lax.broadcasted_iota(jnp.int32, (1, SITES), 1)
    x_coord = lane % LX
    y_coord = lane // LX
    turns = (
        2 * jnp.bitwise_and(momentum[0] * x_coord, LX - 1)
        + 4 * jnp.bitwise_and(momentum[1] * y_coord, LY - 1)
        + jnp.bitwise_and(momentum[2] * plane, LZ - 1)
    )
    angle = (2.0 * math.pi / LZ) * jnp.bitwise_and(turns, LZ - 1).astype(jnp.float32)
    cos_part = jnp.cos(angle)
    sin_part = -jnp.sin(angle)

    @pl.when(direction == 2)
    def _():
        for comp in range(6):
            near = other[NEV * comp : NEV * comp + NEV, :].astype(jnp.float32)
            far = outer[NEV * comp : NEV * comp + NEV, :].astype(jnp.float32)
            ahead[comp] = jnp.where(core == 0, near, far)
            behind[comp] = jnp.where(core == 0, far, near)

    @pl.when(direction != 2)
    def _():
        step = jnp.where(direction == 0, 1, LX)
        last = jnp.logical_and(x_coord == LX - 1, direction == 0)
        first = jnp.logical_and(x_coord == 0, direction == 0)
        for comp in range(6):
            here = own[NEV * comp : NEV * comp + NEV, :].astype(jnp.float32)
            ahead[comp] = jnp.where(
                last, pltpu.roll(here, LX - 1, 1), pltpu.roll(here, SITES - step, 1)
            )
            behind[comp] = jnp.where(
                first, pltpu.roll(here, SITES - LX + 1, 1), pltpu.roll(here, step, 1)
            )

    z_back = jnp.where(
        core == 0,
        outer[6 * NEV :, :].astype(jnp.float32),
        other[6 * NEV :, :].astype(jnp.float32),
    )
    x_roll = jnp.where(
        x_coord == 0, pltpu.roll(links, SITES - LX + 1, 1), pltpu.roll(links, 1, 1)
    )
    y_roll = pltpu.roll(links, LX, 1)

    def matrix(table, part, row, column):
        return table[6 * row + 2 * column + part]

    here_link = []
    back_link = []
    for at in range(18):
        x_at, y_at, z_at = (slice(at + 18 * d, at + 18 * d + 1) for d in range(3))
        here_link.append(
            jnp.where(
                direction == 0, links[x_at], jnp.where(direction == 1, links[y_at], links[z_at])
            )
        )
        back_link.append(
            jnp.where(
                direction == 0,
                x_roll[x_at],
                jnp.where(direction == 1, y_roll[y_at], z_back[z_at]),
            )
        )

    for a in range(3):
        front_re = front_im = rear_re = rear_im = 0.0
        for b in range(3):
            u_re, u_im = matrix(here_link, 0, a, b), matrix(here_link, 1, a, b)
            v_re, v_im = ahead[b], ahead[3 + b]
            front_re += u_re * v_re - u_im * v_im
            front_im += u_re * v_im + u_im * v_re
            w_re, w_im = matrix(back_link, 0, b, a), matrix(back_link, 1, b, a)
            v_re, v_im = behind[b], behind[3 + b]
            rear_re += w_re * v_re + w_im * v_im
            rear_im += w_re * v_im - w_im * v_re
        moved_re = front_re - rear_re
        moved_im = front_im - rear_im
        field[a] = cos_part * moved_re - sin_part * moved_im
        field[3 + a] = cos_part * moved_im + sin_part * moved_re

    for comp in range(6):
        for pair in range(6):
            both = [field[comp, pl.ds(2 * pair + k, 8, 12), :] for k in range(2)]
            out[comp, 16 * pair : 16 * pair + 16, :] = jnp.concatenate(both, 0).astype(
                jnp.bfloat16
            )


def crossed_kernel(source, out, vectors):
    core = lax.axis_index("c")
    first = 24 * lax.axis_index("y")
    for colour in range(3):
        real = source[NEV * colour : NEV * colour + NEV, :].astype(jnp.float32)
        imag = source[NEV * (3 + colour) : NEV * (4 + colour), :].astype(jnp.float32)
        vectors[colour] = real
        vectors[3 + colour] = imag
        vectors[6 + colour] = real + imag
        vectors[9 + colour] = imag - real

    def three_rows(step, carry):
        half = step // 4
        high = step % 4
        keeper = jnp.where(half == 0, 1 - core, core)
        for low in range(3):
            j = first + 6 * high + 3 * keeper + low
            main = 1152 * half + 256 * high + 96 * low
            tail = 1152 * half + 1024 + 32 * high if low == 2 else main + 64
            mine = [vectors[comp, pl.ds(j, 1), :] for comp in range(9)]
            mine = [jnp.broadcast_to(m, (16, SITES)) for m in mine]
            my_re, my_im, my_sum = mine[:3], mine[3:6], mine[6:]
            for chunk in range(6):
                rows = slice(16 * chunk, 16 * chunk + 16)
                re, total, gap = (
                    [vectors[comp + colour, rows, :] for colour in range(3)]
                    for comp in (0, 6, 9)
                )
                if chunk < 4:
                    at = pl.multiple_of(main + 16 * chunk, 16)
                else:
                    at = pl.multiple_of(tail + 16 * (chunk - 4), 16)
                for a in range(3):
                    b = (a + 1) % 3
                    c = (a + 2) % 3
                    shared = my_sum[b] * re[c] - my_sum[c] * re[b]
                    real = shared - (my_im[b] * total[c] - my_im[c] * total[b])
                    imag = shared + (my_re[b] * gap[c] - my_re[c] * gap[b])
                    column = a * SITES
                    out[pl.ds(at, 16), column : column + SITES] = real.astype(jnp.bfloat16)
                    column += 3 * SITES
                    out[pl.ds(at, 16), column : column + SITES] = imag.astype(jnp.bfloat16)
        return carry

    lax.fori_loop(0, 8, three_rows, 0)


def multiply(lefts, crossed, out, half):
    for at, size in ((0, 256), (256, 256), (512, 256), (768, 256), (1024, 128)):
        total = None
        for left, rows in zip(lefts, crossed):
            term = lax.dot_general(
                left,
                rows[1152 * half + at : 1152 * half + at + size, :],
                (((1,), (1,)), ((), ())),
                preferred_element_type=jnp.float32,
            )
            total = term if total is None else total + term
        out[:, at : at + size] = total


def half_kernel(p_one, p_two, p_three, p_four, one, two, three, four, out, left):
    for plane, source in enumerate((p_one, p_two, p_three, p_four)):
        for a in range(3):
            real = source[a]
            imag = source[3 + a]
            column = a * SITES
            left[plane, :NEV, column : column + SITES] = real
            left[plane, NEV:, column : column + SITES] = imag
            column += 3 * SITES
            left[plane, :NEV, column : column + SITES] = -imag
            left[plane, NEV:, column : column + SITES] = real
    multiply([left[plane] for plane in range(4)], (one, two, three, four), out, 0)


def product_kernel(left, one, two, three, four, out):
    multiply([left[plane] for plane in range(4)], (one, two, three, four), out, 1)


def pack_kernel(mine, received, out, total):
    lane = lax.broadcasted_iota(jnp.int32, (8, SITES), 1)
    for tile in range(9):
        lanes = slice(SITES * tile, SITES * tile + SITES)
        total[tile] = mine[:, lanes] + received[:, lanes]
    for q in range(8):
        for zh in range(4):
            for half in range(2):
                out[4 * q + zh, 24 * half : 24 * half + 24, :] = total[
                    2 * zh + half, pl.ds(q, 24, 8), :
                ].astype(jnp.bfloat16)
        tail = total[8, pl.ds(q, 24, 8), :]
        for zh in range(4):
            joined = jnp.zeros((8, SITES), jnp.float32)
            for g in range(3):
                moved = pltpu.roll(tail[8 * g : 8 * g + 8], (32 * (g - zh)) % SITES, 1)
                joined = jnp.where(lane // 32 == g, moved, joined)
            out[4 * q + zh, 48:56, :] = joined.astype(jnp.bfloat16)


def final_kernel(parts, out, rows):
    scale = 1.0 / math.sqrt(LX * LY * LZ)
    for t in range(8):
        total = parts[4 * t].astype(jnp.float32)
        for zh in range(1, 4):
            total += parts[4 * t + zh].astype(jnp.float32)
        total *= scale
        rows[0, pl.ds(t, 24, 8), :] = total[:24]
        rows[1, pl.ds(t, 24, 8), :] = total[24:48]
        for g in range(3):
            tail = total[48:56]
            if g:
                tail = pltpu.roll(tail, SITES - 32 * g, 1)
            rows[2, pl.ds(64 * g + t, 8, 8), :] = tail
    for ri in range(2):
        pieces = [[], [], []]
        for i in range(12):
            at = 8 * (12 * ri + i)
            one, two, three = (rows[part, at : at + 8, :] for part in range(3))
            pieces[0].append(one[:, :96])
            pieces[1].append(one[:, 96:])
            pieces[1].append(two[:, :64])
            pieces[2].append(two[:, 64:])
            pieces[2].append(three[:, :32])
        for r in range(3):
            out[r, :, ri, :] = jnp.concatenate(pieces[r], axis=1)


def vmem():
    return pl.BlockSpec(memory_space=pltpu.VMEM)


def smem():
    return pl.BlockSpec(memory_space=pltpu.SMEM)


def params(mib):
    return pltpu.CompilerParams(vmem_limit_bytes=mib << 20)


def from_y(block, by):
    return lax.ppermute(block, "y", [(i, (i + by) % 4) for i in range(4)])


def on_device(vectors, gauge_links, momentum, direction):
    f32 = jnp.float32
    bf16 = jnp.bfloat16
    swap = [(0, 1), (1, 0)]
    own = jnp.transpose(vectors[0], (1, 2, 0, 3)).reshape(6 * NEV, SITES)
    joined = jnp.concatenate(
        [
            own,
            jnp.transpose(gauge_links[0], (0, 2, 3, 1, 4)).reshape(54, SITES),
            jnp.zeros((10, SITES), bf16),
        ]
    )
    outer = lax.ppermute(joined, AXES, ring_pairs(outer_plane))
    other = lax.ppermute(joined, "c", swap)
    before = from_y(own, 1)
    after = from_y(own, 3)
    opposite = from_y(own, 2)
    phased = pl.pallas_call(
        phased_kernel,
        out_shape=jax.ShapeDtypeStruct((6, NEV, SITES), bf16),
        in_specs=[vmem()] * 5,
        out_specs=vmem(),
        scratch_shapes=[pltpu.VMEM((6, NEV, SITES), f32)] * 3,
        compiler_params=params(8),
    )(momentum, direction, joined, other, outer)
    phased_before = from_y(phased, 1)
    phased_after = from_y(phased, 3)
    phased_opposite = from_y(phased, 2)

    def crossed(source):
        return pl.pallas_call(
            crossed_kernel,
            out_shape=jax.ShapeDtypeStruct((2304, DEPTH), bf16),
            in_specs=[vmem()],
            out_specs=vmem(),
            scratch_shapes=[pltpu.VMEM((12, NEV, SITES), f32)],
            compiler_params=params(4),
            cost_estimate=pl.CostEstimate(flops=0, bytes_accessed=0, transcendentals=0),
        )(source)

    planes = [crossed(own)]
    for source in (before, after, opposite):
        source, planes[-1] = lax.optimization_barrier((source, planes[-1]))
        planes.append(crossed(source))
    sent, left = pl.pallas_call(
        half_kernel,
        out_shape=(
            jax.ShapeDtypeStruct((192, 1152), f32),
            jax.ShapeDtypeStruct((4, 192, DEPTH), bf16),
        ),
        in_specs=[vmem()] * 8,
        out_specs=(vmem(), vmem()),
        compiler_params=params(8),
    )(phased, phased_before, phased_after, phased_opposite, *planes)
    received = lax.ppermute(sent, "c", swap)
    mine = pl.pallas_call(
        product_kernel,
        out_shape=jax.ShapeDtypeStruct((192, 1152), f32),
        in_specs=[vmem()] * 5,
        out_specs=vmem(),
        compiler_params=params(8),
    )(left, *planes)
    packed = pl.pallas_call(
        pack_kernel,
        out_shape=jax.ShapeDtypeStruct((32, 56, SITES), bf16),
        in_specs=[vmem()] * 2,
        out_specs=vmem(),
        scratch_shapes=[pltpu.VMEM((9, 192, SITES), f32)],
        compiler_params=params(16),
    )(mine, received)
    packed = lax.all_to_all(packed, ("x", "zl", "zh"), 0, 0, tiled=True)
    return pl.pallas_call(
        final_kernel,
        out_shape=jax.ShapeDtypeStruct((3, 8, 2, 12 * NEV), f32),
        in_specs=[vmem()],
        out_specs=vmem(),
        scratch_shapes=[pltpu.VMEM((3, 192, SITES), f32)],
        compiler_params=params(16),
    )(packed)


def solution(mesh):
    cut = Mesh(mesh.devices.reshape(SIZES), AXES)
    return jax.shard_map(
        on_device,
        mesh=cut,
        in_specs=(
            P(("x", "zl"), None, None, None, ("y", "zh", "c")),
            P(("x", "zl"), None, None, None, None, ("y", "zh", "c")),
            P(),
            P(("x", "zl")),
        ),
        out_specs=P(("y", "zh", "c"), None, None, ("x", "zl")),
        check_vma=False,
    )
```

```python
import math

import jax
import jax.numpy as jnp
from jax import lax
from jax.experimental import pallas as pl
from jax.experimental.pallas import tpu as pltpu
from jax.sharding import Mesh
from jax.sharding import PartitionSpec as P

NEV = 96
LX = 16
LY = 8
LZ = 32
SITES = 128
AXES = ("x", "zl", "y", "zh", "c")
SIZES = (4, 2, 4, 4, 2)
DEPTH = 6 * SITES


def ring_pairs(target):
    pairs = []
    for x in range(4):
        for zl in range(2):
            for s in range(32):
                to = target(zl, s)
                if to is not None:
                    head = (x * 2 + zl) * 32
                    pairs.append((head + s, head + to))
    return pairs


def outer_plane(zl, s):
    if zl == 1:
        return None
    return (s + 1) % 32 if s % 2 == 1 else (s - 1) % 32


def phased_kernel(momentum, direction_ref, own, other, outer, out, field, ahead, behind):
    links = own[6 * NEV :, :].astype(jnp.float32)
    direction = direction_ref[0]
    core = lax.axis_index("c")
    plane = (lax.axis_index("y") * 4 + lax.axis_index("zh")) * 2 + core
    lane = lax.broadcasted_iota(jnp.int32, (1, SITES), 1)
    x_coord = lane % LX
    y_coord = lane // LX
    turns = (
        2 * jnp.bitwise_and(momentum[0] * x_coord, LX - 1)
        + 4 * jnp.bitwise_and(momentum[1] * y_coord, LY - 1)
        + jnp.bitwise_and(momentum[2] * plane, LZ - 1)
    )
    angle = (2.0 * math.pi / LZ) * jnp.bitwise_and(turns, LZ - 1).astype(jnp.float32)
    cos_part = jnp.cos(angle)
    sin_part = -jnp.sin(angle)

    @pl.when(direction == 2)
    def _():
        for comp in range(6):
            near = other[NEV * comp : NEV * comp + NEV, :].astype(jnp.float32)
            far = outer[NEV * comp : NEV * comp + NEV, :].astype(jnp.float32)
            ahead[comp] = jnp.where(core == 0, near, far)
            behind[comp] = jnp.where(core == 0, far, near)

    @pl.when(direction != 2)
    def _():
        step = jnp.where(direction == 0, 1, LX)
        last = jnp.logical_and(x_coord == LX - 1, direction == 0)
        first = jnp.logical_and(x_coord == 0, direction == 0)
        for comp in range(6):
            here = own[NEV * comp : NEV * comp + NEV, :].astype(jnp.float32)
            ahead[comp] = jnp.where(
                last, pltpu.roll(here, LX - 1, 1), pltpu.roll(here, SITES - step, 1)
            )
            behind[comp] = jnp.where(
                first, pltpu.roll(here, SITES - LX + 1, 1), pltpu.roll(here, step, 1)
            )

    z_back = jnp.where(
        core == 0,
        outer[6 * NEV :, :].astype(jnp.float32),
        other[6 * NEV :, :].astype(jnp.float32),
    )
    x_roll = jnp.where(
        x_coord == 0, pltpu.roll(links, SITES - LX + 1, 1), pltpu.roll(links, 1, 1)
    )
    y_roll = pltpu.roll(links, LX, 1)

    def matrix(table, part, row, column):
        return table[6 * row + 2 * column + part]

    here_link = []
    back_link = []
    for at in range(18):
        x_at, y_at, z_at = (slice(at + 18 * d, at + 18 * d + 1) for d in range(3))
        here_link.append(
            jnp.where(
                direction == 0, links[x_at], jnp.where(direction == 1, links[y_at], links[z_at])
            )
        )
        back_link.append(
            jnp.where(
                direction == 0,
                x_roll[x_at],
                jnp.where(direction == 1, y_roll[y_at], z_back[z_at]),
            )
        )

    for a in range(3):
        front_re = front_im = rear_re = rear_im = 0.0
        for b in range(3):
            u_re, u_im = matrix(here_link, 0, a, b), matrix(here_link, 1, a, b)
            v_re, v_im = ahead[b], ahead[3 + b]
            front_re += u_re * v_re - u_im * v_im
            front_im += u_re * v_im + u_im * v_re
            w_re, w_im = matrix(back_link, 0, b, a), matrix(back_link, 1, b, a)
            v_re, v_im = behind[b], behind[3 + b]
            rear_re += w_re * v_re + w_im * v_im
            rear_im += w_re * v_im - w_im * v_re
        moved_re = front_re - rear_re
        moved_im = front_im - rear_im
        field[a] = cos_part * moved_re - sin_part * moved_im
        field[3 + a] = cos_part * moved_im + sin_part * moved_re

    for comp in range(6):
        for pair in range(6):
            both = [field[comp, pl.ds(2 * pair + k, 8, 12), :] for k in range(2)]
            out[comp, 16 * pair : 16 * pair + 16, :] = jnp.concatenate(both, 0).astype(
                jnp.bfloat16
            )


def crossed_kernel(source, main, tail, vectors):
    core = lax.axis_index("c")
    first = 24 * lax.axis_index("y")
    for colour in range(3):
        real = source[NEV * colour : NEV * colour + NEV, :].astype(jnp.float32)
        imag = source[NEV * (3 + colour) : NEV * (4 + colour), :].astype(jnp.float32)
        vectors[colour] = real
        vectors[3 + colour] = imag
        vectors[6 + colour] = real + imag
        vectors[9 + colour] = imag - real

    def three_rows(step, carry):
        keeper = jnp.where(step < 4, 1 - core, core)
        for low in range(3):
            j = first + 6 * (step % 4) + 3 * keeper + low
            mine = [vectors[comp, pl.ds(j, 1), :] for comp in range(9)]
            mine = [jnp.broadcast_to(m, (16, SITES)) for m in mine]
            my_re, my_im, my_sum = mine[:3], mine[3:6], mine[6:]
            for chunk in range(6):
                rows = slice(16 * chunk, 16 * chunk + 16)
                re, total, gap = (
                    [vectors[comp + colour, rows, :] for colour in range(3)]
                    for comp in (0, 6, 9)
                )
                at = 96 * low + 16 * chunk
                out = main if at < 256 else tail
                at %= 256
                for a in range(3):
                    b = (a + 1) % 3
                    c = (a + 2) % 3
                    shared = my_sum[b] * re[c] - my_sum[c] * re[b]
                    real = shared - (my_im[b] * total[c] - my_im[c] * total[b])
                    imag = shared + (my_re[b] * gap[c] - my_re[c] * gap[b])
                    column = a * SITES
                    out[step, at : at + 16, column : column + SITES] = real.astype(
                        jnp.bfloat16
                    )
                    column += 3 * SITES
                    out[step, at : at + 16, column : column + SITES] = imag.astype(
                        jnp.bfloat16
                    )
        return carry

    lax.fori_loop(0, 8, three_rows, 0)


def multiply(left, crossed, out, half):
    for tail in range(2):
        size = 128 if tail else 1024
        total = None
        for plane in range(4):
            term = lax.dot_general(
                crossed[2 * plane + tail][size * half : size * half + size, :],
                left[plane],
                (((1,), (1,)), ((), ())),
                preferred_element_type=jnp.float32,
            )
            total = term if total is None else total + term
        out[:, 1024 * tail : 1024 * tail + size] = total.T


def half_kernel(p_one, p_two, p_three, p_four, *rest):
    crossed, (out, left) = rest[:8], rest[8:]
    for plane, source in enumerate((p_one, p_two, p_three, p_four)):
        for a in range(3):
            real = source[a]
            imag = source[3 + a]
            column = a * SITES
            left[plane, :NEV, column : column + SITES] = real
            left[plane, NEV:, column : column + SITES] = imag
            column += 3 * SITES
            left[plane, :NEV, column : column + SITES] = -imag
            left[plane, NEV:, column : column + SITES] = real
    multiply(left, crossed, out, 0)


def product_kernel(left, *rest):
    multiply(left, rest[:8], rest[8], 1)


def pack_kernel(mine, received, out, total):
    lane = lax.broadcasted_iota(jnp.int32, (8, SITES), 1)
    for tile in range(9):
        lanes = slice(SITES * tile, SITES * tile + SITES)
        total[tile] = mine[:, lanes] + received[:, lanes]
    for q in range(8):
        for zh in range(4):
            for half in range(2):
                out[4 * q + zh, 24 * half : 24 * half + 24, :] = total[
                    2 * zh + half, pl.ds(q, 24, 8), :
                ].astype(jnp.bfloat16)
        tail = total[8, pl.ds(q, 24, 8), :]
        for zh in range(4):
            joined = jnp.zeros((8, SITES), jnp.float32)
            for g in range(3):
                moved = pltpu.roll(tail[8 * g : 8 * g + 8], (32 * (g - zh)) % SITES, 1)
                joined = jnp.where(lane // 32 == g, moved, joined)
            out[4 * q + zh, 48:56, :] = joined.astype(jnp.bfloat16)


def final_kernel(parts, out, rows):
    scale = 1.0 / math.sqrt(LX * LY * LZ)
    for t in range(8):
        total = parts[4 * t].astype(jnp.float32)
        for zh in range(1, 4):
            total += parts[4 * t + zh].astype(jnp.float32)
        total *= scale
        rows[0, pl.ds(t, 24, 8), :] = total[:24]
        rows[1, pl.ds(t, 24, 8), :] = total[24:48]
        for g in range(3):
            tail = total[48:56]
            if g:
                tail = pltpu.roll(tail, SITES - 32 * g, 1)
            rows[2, pl.ds(64 * g + t, 8, 8), :] = tail
    for ri in range(2):
        pieces = [[], [], []]
        for i in range(12):
            at = 8 * (12 * ri + i)
            one, two, three = (rows[part, at : at + 8, :] for part in range(3))
            pieces[0].append(one[:, :96])
            pieces[1].append(one[:, 96:])
            pieces[1].append(two[:, :64])
            pieces[2].append(two[:, 64:])
            pieces[2].append(three[:, :32])
        for r in range(3):
            out[r, :, ri, :] = jnp.concatenate(pieces[r], axis=1)


def vmem():
    return pl.BlockSpec(memory_space=pltpu.VMEM)


def smem():
    return pl.BlockSpec(memory_space=pltpu.SMEM)


def params(mib):
    return pltpu.CompilerParams(vmem_limit_bytes=mib << 20)


def from_y(block, by):
    return lax.ppermute(block, "y", [(i, (i + by) % 4) for i in range(4)])


def on_device(vectors, gauge_links, momentum, direction):
    f32 = jnp.float32
    bf16 = jnp.bfloat16
    swap = [(0, 1), (1, 0)]
    own = jnp.transpose(vectors[0], (1, 2, 0, 3)).reshape(6 * NEV, SITES)
    joined = jnp.concatenate(
        [
            own,
            jnp.transpose(gauge_links[0], (0, 2, 3, 1, 4)).reshape(54, SITES),
            jnp.zeros((10, SITES), bf16),
        ]
    )
    outer = lax.ppermute(joined, AXES, ring_pairs(outer_plane))
    other = lax.ppermute(joined, "c", swap)
    before = from_y(own, 1)
    after = from_y(own, 3)
    opposite = from_y(own, 2)
    phased = pl.pallas_call(
        phased_kernel,
        out_shape=jax.ShapeDtypeStruct((6, NEV, SITES), bf16),
        in_specs=[vmem()] * 5,
        out_specs=vmem(),
        scratch_shapes=[pltpu.VMEM((6, NEV, SITES), f32)] * 3,
        compiler_params=params(8),
    )(momentum, direction, joined, other, outer)
    phased_before = from_y(phased, 1)
    phased_after = from_y(phased, 3)
    phased_opposite = from_y(phased, 2)

    def crossed(source):
        main, tail = pl.pallas_call(
            crossed_kernel,
            out_shape=(
                jax.ShapeDtypeStruct((8, 256, DEPTH), bf16),
                jax.ShapeDtypeStruct((8, 32, DEPTH), bf16),
            ),
            in_specs=[vmem()],
            out_specs=(vmem(), vmem()),
            scratch_shapes=[pltpu.VMEM((12, NEV, SITES), f32)],
            compiler_params=params(4),
            cost_estimate=pl.CostEstimate(flops=0, bytes_accessed=0, transcendentals=0),
        )(source)
        return [main.reshape(2048, DEPTH), tail.reshape(256, DEPTH)]

    planes = crossed(own)
    for source in (before, after, opposite):
        source, planes[-1] = lax.optimization_barrier((source, planes[-1]))
        planes += crossed(source)
    sent, left = pl.pallas_call(
        half_kernel,
        out_shape=(
            jax.ShapeDtypeStruct((192, 1152), f32),
            jax.ShapeDtypeStruct((4, 192, DEPTH), bf16),
        ),
        in_specs=[vmem()] * 12,
        out_specs=(vmem(), vmem()),
        compiler_params=params(8),
    )(phased, phased_before, phased_after, phased_opposite, *planes)
    received = lax.ppermute(sent, "c", swap)
    mine = pl.pallas_call(
        product_kernel,
        out_shape=jax.ShapeDtypeStruct((192, 1152), f32),
        in_specs=[vmem()] * 9,
        out_specs=vmem(),
        compiler_params=params(8),
    )(left, *planes)
    packed = pl.pallas_call(
        pack_kernel,
        out_shape=jax.ShapeDtypeStruct((32, 56, SITES), bf16),
        in_specs=[vmem()] * 2,
        out_specs=vmem(),
        scratch_shapes=[pltpu.VMEM((9, 192, SITES), f32)],
        compiler_params=params(16),
    )(mine, received)
    packed = lax.all_to_all(packed, ("x", "zl", "zh"), 0, 0, tiled=True)
    return pl.pallas_call(
        final_kernel,
        out_shape=jax.ShapeDtypeStruct((3, 8, 2, 12 * NEV), f32),
        in_specs=[vmem()],
        out_specs=vmem(),
        scratch_shapes=[pltpu.VMEM((3, 192, SITES), f32)],
        compiler_params=params(16),
    )(packed)


def solution(mesh):
    cut = Mesh(mesh.devices.reshape(SIZES), AXES)
    return jax.shard_map(
        on_device,
        mesh=cut,
        in_specs=(
            P(("x", "zl"), None, None, None, ("y", "zh", "c")),
            P(("x", "zl"), None, None, None, None, ("y", "zh", "c")),
            P(),
            P(("x", "zl")),
        ),
        out_specs=P(("y", "zh", "c"), None, None, ("x", "zl")),
        check_vma=False,
    )
```

```python
import functools
import math

import jax
import jax.numpy as jnp
from jax import lax
from jax.experimental import pallas as pl
from jax.experimental.pallas import tpu as pltpu
from jax.sharding import Mesh
from jax.sharding import PartitionSpec as P

NEV = 96
LX = 16
LY = 8
LZ = 32
SITES = 128
AXES = ("x", "zl", "y", "zh", "c")
SIZES = (4, 2, 4, 4, 2)
DEPTH = 6 * SITES


def ring_pairs(target):
    pairs = []
    for x in range(4):
        for zl in range(2):
            for s in range(32):
                to = target(zl, s)
                if to is not None:
                    head = (x * 2 + zl) * 32
                    pairs.append((head + s, head + to))
    return pairs


def outer_plane(zl, s):
    if zl == 1:
        return None
    return (s + 1) % 32 if s % 2 == 1 else (s - 1) % 32


def phased_kernel(momentum, direction_ref, own, other, outer, out, field, ahead, behind):
    links = own[6 * NEV :, :].astype(jnp.float32)
    direction = direction_ref[0]
    core = lax.axis_index("c")
    plane = (lax.axis_index("y") * 4 + lax.axis_index("zh")) * 2 + core
    lane = lax.broadcasted_iota(jnp.int32, (1, SITES), 1)
    x_coord = lane % LX
    y_coord = lane // LX
    turns = (
        2 * jnp.bitwise_and(momentum[0] * x_coord, LX - 1)
        + 4 * jnp.bitwise_and(momentum[1] * y_coord, LY - 1)
        + jnp.bitwise_and(momentum[2] * plane, LZ - 1)
    )
    angle = (2.0 * math.pi / LZ) * jnp.bitwise_and(turns, LZ - 1).astype(jnp.float32)
    cos_part = jnp.cos(angle)
    sin_part = -jnp.sin(angle)

    @pl.when(direction == 2)
    def _():
        for comp in range(6):
            near = other[NEV * comp : NEV * comp + NEV, :].astype(jnp.float32)
            far = outer[NEV * comp : NEV * comp + NEV, :].astype(jnp.float32)
            ahead[comp] = jnp.where(core == 0, near, far)
            behind[comp] = jnp.where(core == 0, far, near)

    @pl.when(direction != 2)
    def _():
        step = jnp.where(direction == 0, 1, LX)
        last = jnp.logical_and(x_coord == LX - 1, direction == 0)
        first = jnp.logical_and(x_coord == 0, direction == 0)
        for comp in range(6):
            here = own[NEV * comp : NEV * comp + NEV, :].astype(jnp.float32)
            ahead[comp] = jnp.where(
                last, pltpu.roll(here, LX - 1, 1), pltpu.roll(here, SITES - step, 1)
            )
            behind[comp] = jnp.where(
                first, pltpu.roll(here, SITES - LX + 1, 1), pltpu.roll(here, step, 1)
            )

    z_back = jnp.where(
        core == 0,
        outer[6 * NEV :, :].astype(jnp.float32),
        other[6 * NEV :, :].astype(jnp.float32),
    )
    x_roll = jnp.where(
        x_coord == 0, pltpu.roll(links, SITES - LX + 1, 1), pltpu.roll(links, 1, 1)
    )
    y_roll = pltpu.roll(links, LX, 1)

    def matrix(table, part, row, column):
        return table[6 * row + 2 * column + part]

    here_link = []
    back_link = []
    for at in range(18):
        x_at, y_at, z_at = (slice(at + 18 * d, at + 18 * d + 1) for d in range(3))
        here_link.append(
            jnp.where(
                direction == 0, links[x_at], jnp.where(direction == 1, links[y_at], links[z_at])
            )
        )
        back_link.append(
            jnp.where(
                direction == 0,
                x_roll[x_at],
                jnp.where(direction == 1, y_roll[y_at], z_back[z_at]),
            )
        )

    for a in range(3):
        front_re = front_im = rear_re = rear_im = 0.0
        for b in range(3):
            u_re, u_im = matrix(here_link, 0, a, b), matrix(here_link, 1, a, b)
            v_re, v_im = ahead[b], ahead[3 + b]
            front_re += u_re * v_re - u_im * v_im
            front_im += u_re * v_im + u_im * v_re
            w_re, w_im = matrix(back_link, 0, b, a), matrix(back_link, 1, b, a)
            v_re, v_im = behind[b], behind[3 + b]
            rear_re += w_re * v_re + w_im * v_im
            rear_im += w_re * v_im - w_im * v_re
        moved_re = front_re - rear_re
        moved_im = front_im - rear_im
        field[a] = cos_part * moved_re - sin_part * moved_im
        field[3 + a] = cos_part * moved_im + sin_part * moved_re

    for comp in range(6):
        for pair in range(6):
            both = [field[comp, pl.ds(2 * pair + k, 8, 12), :] for k in range(2)]
            out[comp, 16 * pair : 16 * pair + 16, :] = jnp.concatenate(both, 0).astype(
                jnp.bfloat16
            )


def left_operand(phased, left):
    for a in range(3):
        real = phased[a]
        imag = phased[3 + a]
        column = a * SITES
        left[:NEV, column : column + SITES] = real
        left[NEV:, column : column + SITES] = imag
        column += 3 * SITES
        left[:NEV, column : column + SITES] = -imag
        left[NEV:, column : column + SITES] = real


def times(crossed, left):
    return lax.dot_general(
        crossed, left[...], (((1,), (1,)), ((), ())), preferred_element_type=jnp.float32
    )


def six_rows(step, vectors, out):
    core = lax.axis_index("c")
    keeper = jnp.where(step < 2, 1 - core, core)
    first = 24 * lax.axis_index("y") + 12 * (step % 2) + 3 * keeper
    for high in range(2):
        for low in range(3):
            mine = [vectors[comp, pl.ds(first + 6 * high + low, 1), :] for comp in range(9)]
            mine = [jnp.broadcast_to(m, (16, SITES)) for m in mine]
            my_re, my_im, my_sum = mine[:3], mine[3:6], mine[6:]
            for chunk in range(6):
                rows = slice(16 * chunk, 16 * chunk + 16)
                re, total, gap = (
                    [vectors[comp + colour, rows, :] for colour in range(3)]
                    for comp in (0, 6, 9)
                )
                at = 96 * low + 16 * chunk
                at = 256 * high + at if at < 256 else 256 + 32 * high + at
                for a in range(3):
                    b = (a + 1) % 3
                    c = (a + 2) % 3
                    shared = my_sum[b] * re[c] - my_sum[c] * re[b]
                    real = shared - (my_im[b] * total[c] - my_im[c] * total[b])
                    imag = shared + (my_re[b] * gap[c] - my_re[c] * gap[b])
                    column = a * SITES
                    out[step, at : at + 16, column : column + SITES] = real.astype(
                        jnp.bfloat16
                    )
                    column += 3 * SITES
                    out[step, at : at + 16, column : column + SITES] = imag.astype(
                        jnp.bfloat16
                    )


def spread(source, vectors):
    for colour in range(3):
        real = source[NEV * colour : NEV * colour + NEV, :].astype(jnp.float32)
        imag = source[NEV * (3 + colour) : NEV * (4 + colour), :].astype(jnp.float32)
        vectors[colour] = real
        vectors[3 + colour] = imag
        vectors[6 + colour] = real + imag
        vectors[9 + colour] = imag - real


def crossed_kernel(source, out, vectors):
    spread(source, vectors)

    def one_step(step, carry):
        six_rows(step, vectors, out)
        return carry

    lax.fori_loop(0, 4, one_step, 0)


def both_kernel(source, phased, previous, *rest):
    sums = rest[0] if len(rest) == 5 else None
    out, total, vectors, left = rest[-4:]
    spread(source, vectors)
    left_operand(phased, left)

    def one_step(step, carry):
        term = times(previous[step], left)
        total[step] = term if sums is None else sums[step] + term
        six_rows(step, vectors, out)
        return carry

    lax.fori_loop(0, 4, one_step, 0)


def last_kernel(half, phased, crossed, sums, out, left):
    left_operand(phased, left)
    tails = []
    for part in range(2):
        step = 2 * half + part
        total = sums[step] + times(crossed[step], left)
        out[:, 512 * part : 512 * part + 512] = total[:512].T.astype(out.dtype)
        tails.append(total[512:])
    out[:, 1024:] = jnp.concatenate(tails, 0).T.astype(out.dtype)


def pack_kernel(mine, received, out, total):
    lane = lax.broadcasted_iota(jnp.int32, (8, SITES), 1)
    for tile in range(9):
        lanes = slice(SITES * tile, SITES * tile + SITES)
        total[tile] = mine[:, lanes] + received[:, lanes].astype(jnp.float32)
    for q in range(8):
        for zh in range(4):
            for half in range(2):
                out[4 * q + zh, 24 * half : 24 * half + 24, :] = total[
                    2 * zh + half, pl.ds(q, 24, 8), :
                ].astype(jnp.bfloat16)
        tail = total[8, pl.ds(q, 24, 8), :]
        for zh in range(4):
            joined = jnp.zeros((8, SITES), jnp.float32)
            for g in range(3):
                moved = pltpu.roll(tail[8 * g : 8 * g + 8], (32 * (g - zh)) % SITES, 1)
                joined = jnp.where(lane // 32 == g, moved, joined)
            out[4 * q + zh, 48:56, :] = joined.astype(jnp.bfloat16)


def final_kernel(parts, out, rows):
    scale = 1.0 / math.sqrt(LX * LY * LZ)
    for t in range(8):
        total = parts[4 * t].astype(jnp.float32)
        for zh in range(1, 4):
            total += parts[4 * t + zh].astype(jnp.float32)
        total *= scale
        rows[0, pl.ds(t, 24, 8), :] = total[:24]
        rows[1, pl.ds(t, 24, 8), :] = total[24:48]
        for g in range(3):
            tail = total[48:56]
            if g:
                tail = pltpu.roll(tail, SITES - 32 * g, 1)
            rows[2, pl.ds(64 * g + t, 8, 8), :] = tail
    for ri in range(2):
        pieces = [[], [], []]
        for i in range(12):
            at = 8 * (12 * ri + i)
            one, two, three = (rows[part, at : at + 8, :] for part in range(3))
            pieces[0].append(one[:, :96])
            pieces[1].append(one[:, 96:])
            pieces[1].append(two[:, :64])
            pieces[2].append(two[:, 64:])
            pieces[2].append(three[:, :32])
        for r in range(3):
            out[r, :, ri, :] = jnp.concatenate(pieces[r], axis=1)


def vmem():
    return pl.BlockSpec(memory_space=pltpu.VMEM)


def smem():
    return pl.BlockSpec(memory_space=pltpu.SMEM)


def params(mib):
    return pltpu.CompilerParams(vmem_limit_bytes=mib << 20)


def from_y(block, by):
    return lax.ppermute(block, "y", [(i, (i + by) % 4) for i in range(4)])


def on_device(vectors, gauge_links, momentum, direction):
    f32 = jnp.float32
    bf16 = jnp.bfloat16
    swap = [(0, 1), (1, 0)]
    own = jnp.transpose(vectors[0], (1, 2, 0, 3)).reshape(6 * NEV, SITES)
    joined = jnp.concatenate(
        [
            own,
            jnp.transpose(gauge_links[0], (0, 2, 3, 1, 4)).reshape(54, SITES),
            jnp.zeros((10, SITES), bf16),
        ]
    )
    outer = lax.ppermute(joined, AXES, ring_pairs(outer_plane))
    other = lax.ppermute(joined, "c", swap)
    before = from_y(own, 1)
    after = from_y(own, 3)
    opposite = from_y(own, 2)
    phased = pl.pallas_call(
        phased_kernel,
        out_shape=jax.ShapeDtypeStruct((6, NEV, SITES), bf16),
        in_specs=[vmem()] * 5,
        out_specs=vmem(),
        scratch_shapes=[pltpu.VMEM((6, NEV, SITES), f32)] * 3,
        compiler_params=params(8),
    )(momentum, direction, joined, other, outer)
    phased_before = from_y(phased, 1)
    phased_after = from_y(phased, 3)
    phased_opposite = from_y(phased, 2)

    crossed_shape = jax.ShapeDtypeStruct((4, 576, DEPTH), bf16)
    sums_shape = jax.ShapeDtypeStruct((4, 576, 192), f32)
    spread_scratch = pltpu.VMEM((12, NEV, SITES), f32)
    left_scratch = pltpu.VMEM((192, DEPTH), bf16)
    short = pl.CostEstimate(flops=0, bytes_accessed=0, transcendentals=0)

    def both(source, phased_plane, previous, *sums):
        return pl.pallas_call(
            both_kernel,
            out_shape=(crossed_shape, sums_shape),
            in_specs=[vmem()] * (3 + len(sums)),
            out_specs=(vmem(), vmem()),
            scratch_shapes=[spread_scratch, left_scratch],
            compiler_params=params(6),
            cost_estimate=short,
        )(source, phased_plane, previous, *sums)

    def last(half, kind):
        return pl.pallas_call(
            functools.partial(last_kernel, half),
            out_shape=jax.ShapeDtypeStruct((192, 1152), kind),
            in_specs=[vmem()] * 3,
            out_specs=vmem(),
            scratch_shapes=[left_scratch],
            compiler_params=params(6),
        )(phased_opposite, crossed, sums)

    crossed = pl.pallas_call(
        crossed_kernel,
        out_shape=crossed_shape,
        in_specs=[vmem()],
        out_specs=vmem(),
        scratch_shapes=[spread_scratch],
        compiler_params=params(4),
        cost_estimate=short,
    )(own)
    crossed, sums = both(before, phased, crossed)
    crossed, sums = both(after, phased_before, crossed, sums)
    crossed, sums = both(opposite, phased_after, crossed, sums)
    received = lax.ppermute(last(0, bf16), "c", swap)
    mine = last(1, f32)
    packed = pl.pallas_call(
        pack_kernel,
        out_shape=jax.ShapeDtypeStruct((32, 56, SITES), bf16),
        in_specs=[vmem()] * 2,
        out_specs=vmem(),
        scratch_shapes=[pltpu.VMEM((9, 192, SITES), f32)],
        compiler_params=params(16),
    )(mine, received)
    packed = lax.all_to_all(packed, ("x", "zl", "zh"), 0, 0, tiled=True)
    return pl.pallas_call(
        final_kernel,
        out_shape=jax.ShapeDtypeStruct((3, 8, 2, 12 * NEV), f32),
        in_specs=[vmem()],
        out_specs=vmem(),
        scratch_shapes=[pltpu.VMEM((3, 192, SITES), f32)],
        compiler_params=params(16),
    )(packed)


def solution(mesh):
    cut = Mesh(mesh.devices.reshape(SIZES), AXES)
    return jax.shard_map(
        on_device,
        mesh=cut,
        in_specs=(
            P(("x", "zl"), None, None, None, ("y", "zh", "c")),
            P(("x", "zl"), None, None, None, None, ("y", "zh", "c")),
            P(),
            P(("x", "zl")),
        ),
        out_specs=P(("y", "zh", "c"), None, None, ("x", "zl")),
        check_vma=False,
    )
```

```python
import math

import jax
import jax.numpy as jnp
from jax import lax
from jax.experimental import pallas as pl
from jax.experimental.pallas import tpu as pltpu
from jax.sharding import Mesh
from jax.sharding import PartitionSpec as P

NEV = 96
LX = 16
LY = 8
LZ = 32
SITES = 128
AXES = ("x", "zl", "y", "zh", "c")
SIZES = (4, 2, 4, 4, 2)
DEPTH = 6 * SITES


def ring_pairs(target):
    pairs = []
    for x in range(4):
        for zl in range(2):
            for s in range(32):
                to = target(zl, s)
                if to is not None:
                    head = (x * 2 + zl) * 32
                    pairs.append((head + s, head + to))
    return pairs


def outer_plane(zl, s):
    if zl == 1:
        return None
    return (s + 1) % 32 if s % 2 == 1 else (s - 1) % 32


def phased_kernel(numbers, own, other, outer, out, field, ahead, behind):
    links = own[6 * NEV :, :].astype(jnp.float32)
    direction = numbers[3]
    core = lax.axis_index("c")
    plane = (lax.axis_index("y") * 4 + lax.axis_index("zh")) * 2 + core
    lane = lax.broadcasted_iota(jnp.int32, (1, SITES), 1)
    x_coord = lane % LX
    y_coord = lane // LX
    turns = (
        2 * jnp.bitwise_and(numbers[0] * x_coord, LX - 1)
        + 4 * jnp.bitwise_and(numbers[1] * y_coord, LY - 1)
        + jnp.bitwise_and(numbers[2] * plane, LZ - 1)
    )
    angle = (2.0 * math.pi / LZ) * jnp.bitwise_and(turns, LZ - 1).astype(jnp.float32)
    cos_part = jnp.cos(angle)
    sin_part = -jnp.sin(angle)

    @pl.when(direction == 2)
    def _():
        for comp in range(6):
            near = other[NEV * comp : NEV * comp + NEV, :].astype(jnp.float32)
            far = outer[NEV * comp : NEV * comp + NEV, :].astype(jnp.float32)
            ahead[comp] = jnp.where(core == 0, near, far)
            behind[comp] = jnp.where(core == 0, far, near)

    @pl.when(direction != 2)
    def _():
        step = jnp.where(direction == 0, 1, LX)
        last = jnp.logical_and(x_coord == LX - 1, direction == 0)
        first = jnp.logical_and(x_coord == 0, direction == 0)
        for comp in range(6):
            here = own[NEV * comp : NEV * comp + NEV, :].astype(jnp.float32)
            ahead[comp] = jnp.where(
                last, pltpu.roll(here, LX - 1, 1), pltpu.roll(here, SITES - step, 1)
            )
            behind[comp] = jnp.where(
                first, pltpu.roll(here, SITES - LX + 1, 1), pltpu.roll(here, step, 1)
            )

    z_back = jnp.where(
        core == 0,
        outer[6 * NEV :, :].astype(jnp.float32),
        other[6 * NEV :, :].astype(jnp.float32),
    )
    x_roll = jnp.where(
        x_coord == 0, pltpu.roll(links, SITES - LX + 1, 1), pltpu.roll(links, 1, 1)
    )
    y_roll = pltpu.roll(links, LX, 1)

    def matrix(table, part, row, column):
        return table[6 * row + 2 * column + part]

    here_link = []
    back_link = []
    for at in range(18):
        x_at, y_at, z_at = (slice(at + 18 * d, at + 18 * d + 1) for d in range(3))
        here_link.append(
            jnp.where(
                direction == 0, links[x_at], jnp.where(direction == 1, links[y_at], links[z_at])
            )
        )
        back_link.append(
            jnp.where(
                direction == 0,
                x_roll[x_at],
                jnp.where(direction == 1, y_roll[y_at], z_back[z_at]),
            )
        )

    for a in range(3):
        front_re = front_im = rear_re = rear_im = 0.0
        for b in range(3):
            u_re, u_im = matrix(here_link, 0, a, b), matrix(here_link, 1, a, b)
            v_re, v_im = ahead[b], ahead[3 + b]
            front_re += u_re * v_re - u_im * v_im
            front_im += u_re * v_im + u_im * v_re
            w_re, w_im = matrix(back_link, 0, b, a), matrix(back_link, 1, b, a)
            v_re, v_im = behind[b], behind[3 + b]
            rear_re += w_re * v_re + w_im * v_im
            rear_im += w_re * v_im - w_im * v_re
        moved_re = front_re - rear_re
        moved_im = front_im - rear_im
        field[a] = cos_part * moved_re - sin_part * moved_im
        field[3 + a] = cos_part * moved_im + sin_part * moved_re

    for comp in range(6):
        for rows in range(6):
            both = [field[comp, pl.ds(2 * rows + k, 8, 12), :] for k in range(2)]
            out[comp, 16 * rows : 16 * rows + 16, :] = jnp.concatenate(both, 0).astype(
                jnp.bfloat16
            )


def left_operand(phased, left):
    for a in range(3):
        real = phased[a]
        imag = phased[3 + a]
        column = a * SITES
        left[:NEV, column : column + SITES] = real
        left[NEV:, column : column + SITES] = imag
        column += 3 * SITES
        left[:NEV, column : column + SITES] = -imag
        left[NEV:, column : column + SITES] = real


def times(crossed, left):
    return lax.dot_general(
        crossed, left[...], (((1,), (1,)), ((), ())), preferred_element_type=jnp.float32
    )


def six_rows(step, vectors, out):
    core = lax.axis_index("c")
    keeper = jnp.where(step < 2, 1 - core, core)
    first = 24 * lax.axis_index("y") + 12 * (step % 2) + 3 * keeper
    for high in range(2):
        for low in range(3):
            mine = [vectors[comp, pl.ds(first + 6 * high + low, 1), :] for comp in range(9)]
            mine = [jnp.broadcast_to(m, (16, SITES)) for m in mine]
            my_re, my_im, my_sum = mine[:3], mine[3:6], mine[6:]
            for chunk in range(6):
                rows = slice(16 * chunk, 16 * chunk + 16)
                re, total, gap = (
                    [vectors[comp + colour, rows, :] for colour in range(3)]
                    for comp in (0, 6, 9)
                )
                at = 96 * low + 16 * chunk
                at = 256 * high + at if at < 256 else 256 + 32 * high + at
                for a in range(3):
                    b = (a + 1) % 3
                    c = (a + 2) % 3
                    shared = my_sum[b] * re[c] - my_sum[c] * re[b]
                    real = shared - (my_im[b] * total[c] - my_im[c] * total[b])
                    imag = shared + (my_re[b] * gap[c] - my_re[c] * gap[b])
                    column = a * SITES
                    out[step, at : at + 16, column : column + SITES] = real.astype(
                        jnp.bfloat16
                    )
                    column += 3 * SITES
                    out[step, at : at + 16, column : column + SITES] = imag.astype(
                        jnp.bfloat16
                    )


def spread(source, vectors):
    for colour in range(3):
        real = source[colour].astype(jnp.float32)
        imag = source[3 + colour].astype(jnp.float32)
        vectors[colour] = real
        vectors[3 + colour] = imag
        vectors[6 + colour] = real + imag
        vectors[9 + colour] = imag - real


def crossed_kernel(source, out, vectors):
    spread(source, vectors)

    def one_step(step, carry):
        six_rows(step, vectors, out)
        return carry

    lax.fori_loop(0, 4, one_step, 0)


def both_kernel(source, phased, previous, *rest):
    sums = rest[0] if len(rest) == 5 else None
    out, total, vectors, left = rest[-4:]
    spread(source, vectors)
    left_operand(phased, left)

    def one_step(step, carry):
        term = times(previous[step], left)
        total[step] = term if sums is None else sums[step] + term
        six_rows(step, vectors, out)
        return carry

    lax.fori_loop(0, 4, one_step, 0)


def last_kernel(phased, crossed, sums, theirs, mine, left):
    left_operand(phased, left)
    for out, half in ((theirs, 0), (mine, 1)):
        tails = []
        for part in range(2):
            step = 2 * half + part
            total = sums[step] + times(crossed[step], left)
            out[:, 512 * part : 512 * part + 512] = total[:512].T.astype(out.dtype)
            tails.append(total[512:])
        out[:, 1024:] = jnp.concatenate(tails, 0).T.astype(out.dtype)


def pack_kernel(mine, received, out, total):
    lane = lax.broadcasted_iota(jnp.int32, (8, SITES), 1)
    for tile in range(9):
        lanes = slice(SITES * tile, SITES * tile + SITES)
        total[tile] = mine[:, lanes] + received[:, lanes].astype(jnp.float32)
    for q in range(8):
        for zh in range(4):
            for half in range(2):
                out[4 * q + zh, 24 * half : 24 * half + 24, :] = total[
                    2 * zh + half, pl.ds(q, 24, 8), :
                ].astype(jnp.bfloat16)
        tail = total[8, pl.ds(q, 24, 8), :]
        for zh in range(4):
            joined = jnp.zeros((8, SITES), jnp.float32)
            for g in range(3):
                moved = pltpu.roll(tail[8 * g : 8 * g + 8], (32 * (g - zh)) % SITES, 1)
                joined = jnp.where(lane // 32 == g, moved, joined)
            out[4 * q + zh, 48:56, :] = joined.astype(jnp.bfloat16)


def final_kernel(parts, out, rows):
    scale = 1.0 / math.sqrt(LX * LY * LZ)
    for t in range(8):
        total = parts[4 * t].astype(jnp.float32)
        for zh in range(1, 4):
            total += parts[4 * t + zh].astype(jnp.float32)
        total *= scale
        rows[0, pl.ds(t, 24, 8), :] = total[:24]
        rows[1, pl.ds(t, 24, 8), :] = total[24:48]
        for g in range(3):
            tail = total[48:56]
            if g:
                tail = pltpu.roll(tail, SITES - 32 * g, 1)
            rows[2, pl.ds(64 * g + t, 8, 8), :] = tail
    for ri in range(2):
        pieces = [[], [], []]
        for i in range(12):
            at = 8 * (12 * ri + i)
            one, two, three = (rows[part, at : at + 8, :] for part in range(3))
            pieces[0].append(one[:, :96])
            pieces[1].append(one[:, 96:])
            pieces[1].append(two[:, :64])
            pieces[2].append(two[:, 64:])
            pieces[2].append(three[:, :32])
        for r in range(3):
            out[r, :, ri, :] = jnp.concatenate(pieces[r], axis=1)


def vmem():
    return pl.BlockSpec(memory_space=pltpu.VMEM)


def smem():
    return pl.BlockSpec(memory_space=pltpu.SMEM)


def params(mib):
    return pltpu.CompilerParams(vmem_limit_bytes=mib << 20)


def from_y(block, by):
    return lax.ppermute(block, "y", [(i, (i + by) % 4) for i in range(4)])


def on_device(vectors, gauge_links, momentum, direction):
    f32 = jnp.float32
    bf16 = jnp.bfloat16
    swap = [(0, 1), (1, 0)]
    own = jnp.transpose(vectors[0], (1, 2, 0, 3)).reshape(6, NEV, SITES)
    joined = jnp.concatenate(
        [
            own.reshape(6 * NEV, SITES),
            jnp.transpose(gauge_links[0], (0, 2, 3, 1, 4)).reshape(54, SITES),
            jnp.zeros((10, SITES), bf16),
        ]
    )
    outer = lax.ppermute(joined, AXES, ring_pairs(outer_plane))
    other = lax.ppermute(joined, "c", swap)
    before = from_y(own, 1)
    after = from_y(own, 3)
    opposite = from_y(own, 2)
    phased = pl.pallas_call(
        phased_kernel,
        out_shape=jax.ShapeDtypeStruct((6, NEV, SITES), bf16),
        in_specs=[vmem()] * 4,
        out_specs=vmem(),
        scratch_shapes=[pltpu.VMEM((6, NEV, SITES), f32)] * 3,
        compiler_params=params(8),
    )(jnp.concatenate([momentum, direction]), joined, other, outer)
    phased_before = from_y(phased, 1)
    phased_after = from_y(phased, 3)
    phased_opposite = from_y(phased, 2)
    before, after, opposite = lax.optimization_barrier((before, after, opposite))

    crossed_shape = jax.ShapeDtypeStruct((4, 576, DEPTH), bf16)
    sums_shape = jax.ShapeDtypeStruct((4, 576, 192), f32)
    spread_scratch = pltpu.VMEM((12, NEV, SITES), f32)
    left_scratch = pltpu.VMEM((192, DEPTH), bf16)
    short = pl.CostEstimate(flops=0, bytes_accessed=0, transcendentals=0)

    def both(source, phased_plane, previous, *sums):
        return pl.pallas_call(
            both_kernel,
            out_shape=(crossed_shape, sums_shape),
            in_specs=[vmem()] * (3 + len(sums)),
            out_specs=(vmem(), vmem()),
            scratch_shapes=[spread_scratch, left_scratch],
            compiler_params=params(6),
            cost_estimate=short,
        )(source, phased_plane, previous, *sums)

    crossed = pl.pallas_call(
        crossed_kernel,
        out_shape=crossed_shape,
        in_specs=[vmem()],
        out_specs=vmem(),
        scratch_shapes=[spread_scratch],
        compiler_params=params(4),
        cost_estimate=short,
    )(own)
    crossed, sums = both(before, phased, crossed)
    crossed, sums = both(after, phased_before, crossed, sums)
    crossed, sums = both(opposite, phased_after, crossed, sums)
    sent, mine = pl.pallas_call(
        last_kernel,
        out_shape=(
            jax.ShapeDtypeStruct((192, 1152), bf16),
            jax.ShapeDtypeStruct((192, 1152), f32),
        ),
        in_specs=[vmem()] * 3,
        out_specs=(vmem(), vmem()),
        scratch_shapes=[left_scratch],
        compiler_params=params(6),
    )(phased_opposite, crossed, sums)
    received = lax.ppermute(sent, "c", swap)
    packed = pl.pallas_call(
        pack_kernel,
        out_shape=jax.ShapeDtypeStruct((32, 56, SITES), bf16),
        in_specs=[vmem()] * 2,
        out_specs=vmem(),
        scratch_shapes=[pltpu.VMEM((9, 192, SITES), f32)],
        compiler_params=params(16),
    )(mine, received)
    packed = lax.all_to_all(packed, ("x", "zl", "zh"), 0, 0, tiled=True)
    return pl.pallas_call(
        final_kernel,
        out_shape=jax.ShapeDtypeStruct((3, 8, 2, 12 * NEV), f32),
        in_specs=[vmem()],
        out_specs=vmem(),
        scratch_shapes=[pltpu.VMEM((3, 192, SITES), f32)],
        compiler_params=params(16),
    )(packed)


def solution(mesh):
    cut = Mesh(mesh.devices.reshape(SIZES), AXES)
    return jax.shard_map(
        on_device,
        mesh=cut,
        in_specs=(
            P(("x", "zl"), None, None, None, ("y", "zh", "c")),
            P(("x", "zl"), None, None, None, None, ("y", "zh", "c")),
            P(),
            P(("x", "zl")),
        ),
        out_specs=P(("y", "zh", "c"), None, None, ("x", "zl")),
        check_vma=False,
    )
```

```python
import math

import jax
import jax.numpy as jnp
from jax import lax
from jax.experimental import pallas as pl
from jax.experimental.pallas import tpu as pltpu
from jax.sharding import Mesh
from jax.sharding import PartitionSpec as P

NEV = 96
LX = 16
LY = 8
LZ = 32
SITES = 128
AXES = ("x", "zl", "y", "zh", "c")
SIZES = (4, 2, 4, 4, 2)
DEPTH = 6 * SITES


def ring_pairs(target):
    pairs = []
    for x in range(4):
        for zl in range(2):
            for s in range(32):
                to = target(zl, s)
                if to is not None:
                    head = (x * 2 + zl) * 32
                    pairs.append((head + s, head + to))
    return pairs


def outer_plane(zl, s):
    if zl == 1:
        return None
    return (s + 1) % 32 if s % 2 == 1 else (s - 1) % 32


def phased_kernel(numbers, own, other, outer, out, field, ahead, behind):
    links = own[6 * NEV :, :].astype(jnp.float32)
    direction = numbers[3]
    core = lax.axis_index("c")
    plane = (lax.axis_index("y") * 4 + lax.axis_index("zh")) * 2 + core
    lane = lax.broadcasted_iota(jnp.int32, (1, SITES), 1)
    x_coord = lane % LX
    y_coord = lane // LX
    turns = (
        2 * jnp.bitwise_and(numbers[0] * x_coord, LX - 1)
        + 4 * jnp.bitwise_and(numbers[1] * y_coord, LY - 1)
        + jnp.bitwise_and(numbers[2] * plane, LZ - 1)
    )
    angle = (2.0 * math.pi / LZ) * jnp.bitwise_and(turns, LZ - 1).astype(jnp.float32)
    cos_part = jnp.cos(angle)
    sin_part = -jnp.sin(angle)

    @pl.when(direction == 2)
    def _():
        for comp in range(6):
            near = other[NEV * comp : NEV * comp + NEV, :].astype(jnp.float32)
            far = outer[NEV * comp : NEV * comp + NEV, :].astype(jnp.float32)
            ahead[comp] = jnp.where(core == 0, near, far)
            behind[comp] = jnp.where(core == 0, far, near)

    @pl.when(direction != 2)
    def _():
        step = jnp.where(direction == 0, 1, LX)
        last = jnp.logical_and(x_coord == LX - 1, direction == 0)
        first = jnp.logical_and(x_coord == 0, direction == 0)
        for comp in range(6):
            here = own[NEV * comp : NEV * comp + NEV, :].astype(jnp.float32)
            ahead[comp] = jnp.where(
                last, pltpu.roll(here, LX - 1, 1), pltpu.roll(here, SITES - step, 1)
            )
            behind[comp] = jnp.where(
                first, pltpu.roll(here, SITES - LX + 1, 1), pltpu.roll(here, step, 1)
            )

    z_back = jnp.where(
        core == 0,
        outer[6 * NEV :, :].astype(jnp.float32),
        other[6 * NEV :, :].astype(jnp.float32),
    )
    x_roll = jnp.where(
        x_coord == 0, pltpu.roll(links, SITES - LX + 1, 1), pltpu.roll(links, 1, 1)
    )
    y_roll = pltpu.roll(links, LX, 1)

    def matrix(table, part, row, column):
        return table[6 * row + 2 * column + part]

    here_link = []
    back_link = []
    for at in range(18):
        x_at, y_at, z_at = (slice(at + 18 * d, at + 18 * d + 1) for d in range(3))
        here_link.append(
            jnp.where(
                direction == 0, links[x_at], jnp.where(direction == 1, links[y_at], links[z_at])
            )
        )
        back_link.append(
            jnp.where(
                direction == 0,
                x_roll[x_at],
                jnp.where(direction == 1, y_roll[y_at], z_back[z_at]),
            )
        )

    for a in range(3):
        front_re = front_im = rear_re = rear_im = 0.0
        for b in range(3):
            u_re, u_im = matrix(here_link, 0, a, b), matrix(here_link, 1, a, b)
            v_re, v_im = ahead[b], ahead[3 + b]
            front_re += u_re * v_re - u_im * v_im
            front_im += u_re * v_im + u_im * v_re
            w_re, w_im = matrix(back_link, 0, b, a), matrix(back_link, 1, b, a)
            v_re, v_im = behind[b], behind[3 + b]
            rear_re += w_re * v_re + w_im * v_im
            rear_im += w_re * v_im - w_im * v_re
        moved_re = front_re - rear_re
        moved_im = front_im - rear_im
        field[a] = cos_part * moved_re - sin_part * moved_im
        field[3 + a] = cos_part * moved_im + sin_part * moved_re

    for comp in range(6):
        for rows in range(6):
            both = [field[comp, pl.ds(2 * rows + k, 8, 12), :] for k in range(2)]
            out[comp, 16 * rows : 16 * rows + 16, :] = jnp.concatenate(both, 0).astype(
                jnp.bfloat16
            )


def left_operand(phased, left):
    for a in range(3):
        real = phased[a]
        imag = phased[3 + a]
        column = a * SITES
        left[:NEV, column : column + SITES] = real
        left[NEV:, column : column + SITES] = imag
        column += 3 * SITES
        left[:NEV, column : column + SITES] = -imag
        left[NEV:, column : column + SITES] = real


def times(crossed, left):
    return lax.dot_general(
        crossed, left[...], (((1,), (1,)), ((), ())), preferred_element_type=jnp.float32
    )


def six_rows(step, vectors, out):
    core = lax.axis_index("c")
    keeper = jnp.where(step < 2, 1 - core, core)
    first = 24 * lax.axis_index("y") + 12 * (step % 2) + 3 * keeper
    for high in range(2):
        for low in range(3):
            mine = [vectors[comp, pl.ds(first + 6 * high + low, 1), :] for comp in range(9)]
            mine = [jnp.broadcast_to(m, (16, SITES)) for m in mine]
            my_re, my_im, my_sum = mine[:3], mine[3:6], mine[6:]
            for chunk in range(6):
                rows = slice(16 * chunk, 16 * chunk + 16)
                re, total, gap = (
                    [vectors[comp + colour, rows, :] for colour in range(3)]
                    for comp in (0, 6, 9)
                )
                at = 96 * low + 16 * chunk
                at = 256 * high + at if at < 256 else 256 + 32 * high + at
                for a in range(3):
                    b = (a + 1) % 3
                    c = (a + 2) % 3
                    shared = my_sum[b] * re[c] - my_sum[c] * re[b]
                    real = shared - (my_im[b] * total[c] - my_im[c] * total[b])
                    imag = shared + (my_re[b] * gap[c] - my_re[c] * gap[b])
                    column = a * SITES
                    out[step, at : at + 16, column : column + SITES] = real.astype(
                        jnp.bfloat16
                    )
                    column += 3 * SITES
                    out[step, at : at + 16, column : column + SITES] = imag.astype(
                        jnp.bfloat16
                    )


def spread(source, vectors):
    for colour in range(3):
        real = source[colour].astype(jnp.float32)
        imag = source[3 + colour].astype(jnp.float32)
        vectors[colour] = real
        vectors[3 + colour] = imag
        vectors[6 + colour] = real + imag
        vectors[9 + colour] = imag - real


def crossed_kernel(source, out, vectors):
    spread(source, vectors)

    def one_step(step, carry):
        six_rows(step, vectors, out)
        return carry

    lax.fori_loop(0, 4, one_step, 0)


def both_kernel(source, phased, previous, *rest):
    sums = rest[0] if len(rest) == 5 else None
    out, total, vectors, left = rest[-4:]
    spread(source, vectors)
    left_operand(phased, left)

    def one_step(step, carry):
        term = times(previous[step], left)
        total[step] = term if sums is None else sums[step] + term
        six_rows(step, vectors, out)
        return carry

    lax.fori_loop(0, 4, one_step, 0)


def last_kernel(phased, crossed, sums, theirs, mine, left):
    left_operand(phased, left)
    for out, half in ((theirs, 0), (mine, 1)):
        tails = []
        for part in range(2):
            step = 2 * half + part
            total = sums[step] + times(crossed[step], left)
            out[:, 512 * part : 512 * part + 512] = total[:512].T.astype(out.dtype)
            tails.append(total[512:])
        out[:, 1024:] = jnp.concatenate(tails, 0).T.astype(out.dtype)


def pack_kernel(mine, received, out, total):
    lane = lax.broadcasted_iota(jnp.int32, (8, SITES), 1)
    for tile in range(9):
        lanes = slice(SITES * tile, SITES * tile + SITES)
        total[tile] = mine[:, lanes] + received[:, lanes].astype(jnp.float32)
    for q in range(8):
        for zh in range(4):
            for half in range(2):
                out[4 * q + zh, 24 * half : 24 * half + 24, :] = total[
                    2 * zh + half, pl.ds(q, 24, 8), :
                ].astype(jnp.bfloat16)
        tail = total[8, pl.ds(q, 24, 8), :]
        for zh in range(4):
            joined = jnp.zeros((8, SITES), jnp.float32)
            for g in range(3):
                moved = pltpu.roll(tail[8 * g : 8 * g + 8], (32 * (g - zh)) % SITES, 1)
                joined = jnp.where(lane // 32 == g, moved, joined)
            out[4 * q + zh, 48:56, :] = joined.astype(jnp.bfloat16)


def final_kernel(parts, out, rows):
    scale = 1.0 / math.sqrt(LX * LY * LZ)
    for t in range(8):
        total = parts[4 * t].astype(jnp.float32)
        for zh in range(1, 4):
            total += parts[4 * t + zh].astype(jnp.float32)
        total *= scale
        rows[0, pl.ds(t, 24, 8), :] = total[:24]
        rows[1, pl.ds(t, 24, 8), :] = total[24:48]
        for g in range(3):
            tail = total[48:56]
            if g:
                tail = pltpu.roll(tail, SITES - 32 * g, 1)
            rows[2, pl.ds(64 * g + t, 8, 8), :] = tail
    for ri in range(2):
        pieces = [[], [], []]
        for i in range(12):
            at = 8 * (12 * ri + i)
            one, two, three = (rows[part, at : at + 8, :] for part in range(3))
            pieces[0].append(one[:, :96])
            pieces[1].append(one[:, 96:])
            pieces[1].append(two[:, :64])
            pieces[2].append(two[:, 64:])
            pieces[2].append(three[:, :32])
        for r in range(3):
            out[r, :, ri, :] = jnp.concatenate(pieces[r], axis=1)


def vmem():
    return pl.BlockSpec(memory_space=pltpu.VMEM)


def smem():
    return pl.BlockSpec(memory_space=pltpu.SMEM)


def params(mib):
    return pltpu.CompilerParams(vmem_limit_bytes=mib << 20)


def from_y(block, by):
    return lax.ppermute(block, "y", [(i, (i + by) % 4) for i in range(4)])


def on_device(vectors, gauge_links, momentum, direction):
    f32 = jnp.float32
    bf16 = jnp.bfloat16
    swap = [(0, 1), (1, 0)]
    own = jnp.transpose(vectors[0], (1, 2, 0, 3)).reshape(6, NEV, SITES)
    joined = jnp.concatenate(
        [
            own.reshape(6 * NEV, SITES),
            jnp.transpose(gauge_links[0], (0, 2, 3, 1, 4)).reshape(54, SITES),
            jnp.zeros((10, SITES), bf16),
        ]
    )
    before = from_y(own, 1)
    after = from_y(own, 3)
    crossed_shape = jax.ShapeDtypeStruct((4, 576, DEPTH), bf16)
    sums_shape = jax.ShapeDtypeStruct((4, 576, 192), f32)
    spread_scratch = pltpu.VMEM((12, NEV, SITES), f32)
    left_scratch = pltpu.VMEM((192, DEPTH), bf16)
    short = pl.CostEstimate(flops=0, bytes_accessed=0, transcendentals=0)

    crossed = pl.pallas_call(
        crossed_kernel,
        out_shape=crossed_shape,
        in_specs=[vmem()],
        out_specs=vmem(),
        scratch_shapes=[spread_scratch],
        compiler_params=params(4),
        cost_estimate=short,
    )(own)
    joined, here, before, after, crossed = lax.optimization_barrier(
        (joined, own, before, after, crossed)
    )
    outer = lax.ppermute(joined, AXES, ring_pairs(outer_plane))
    other = lax.ppermute(joined, "c", swap)
    opposite = from_y(here, 2)
    phased = pl.pallas_call(
        phased_kernel,
        out_shape=jax.ShapeDtypeStruct((6, NEV, SITES), bf16),
        in_specs=[vmem()] * 4,
        out_specs=vmem(),
        scratch_shapes=[pltpu.VMEM((6, NEV, SITES), f32)] * 3,
        compiler_params=params(8),
    )(jnp.concatenate([momentum, direction]), joined, other, outer)
    phased_before = from_y(phased, 1)
    phased_after = from_y(phased, 3)
    phased_opposite = from_y(phased, 2)

    def both(source, phased_plane, previous, *sums):
        return pl.pallas_call(
            both_kernel,
            out_shape=(crossed_shape, sums_shape),
            in_specs=[vmem()] * (3 + len(sums)),
            out_specs=(vmem(), vmem()),
            scratch_shapes=[spread_scratch, left_scratch],
            compiler_params=params(6),
            cost_estimate=short,
        )(source, phased_plane, previous, *sums)

    crossed, sums = both(before, phased, crossed)
    crossed, sums = both(opposite, phased_before, crossed, sums)
    crossed, sums = both(after, phased_opposite, crossed, sums)
    sent, mine = pl.pallas_call(
        last_kernel,
        out_shape=(
            jax.ShapeDtypeStruct((192, 1152), bf16),
            jax.ShapeDtypeStruct((192, 1152), f32),
        ),
        in_specs=[vmem()] * 3,
        out_specs=(vmem(), vmem()),
        scratch_shapes=[left_scratch],
        compiler_params=params(6),
    )(phased_after, crossed, sums)
    received = lax.ppermute(sent, "c", swap)
    packed = pl.pallas_call(
        pack_kernel,
        out_shape=jax.ShapeDtypeStruct((32, 56, SITES), bf16),
        in_specs=[vmem()] * 2,
        out_specs=vmem(),
        scratch_shapes=[pltpu.VMEM((9, 192, SITES), f32)],
        compiler_params=params(16),
    )(mine, received)
    packed = lax.all_to_all(packed, ("x", "zl", "zh"), 0, 0, tiled=True)
    return pl.pallas_call(
        final_kernel,
        out_shape=jax.ShapeDtypeStruct((3, 8, 2, 12 * NEV), f32),
        in_specs=[vmem()],
        out_specs=vmem(),
        scratch_shapes=[pltpu.VMEM((3, 192, SITES), f32)],
        compiler_params=params(16),
    )(packed)


def solution(mesh):
    cut = Mesh(mesh.devices.reshape(SIZES), AXES)
    return jax.shard_map(
        on_device,
        mesh=cut,
        in_specs=(
            P(("x", "zl"), None, None, None, ("y", "zh", "c")),
            P(("x", "zl"), None, None, None, None, ("y", "zh", "c")),
            P(),
            P(("x", "zl")),
        ),
        out_specs=P(("y", "zh", "c"), None, None, ("x", "zl")),
        check_vma=False,
    )
```

```python
import math

import jax
import jax.numpy as jnp
from jax import lax
from jax.experimental import pallas as pl
from jax.experimental.pallas import tpu as pltpu
from jax.sharding import Mesh
from jax.sharding import PartitionSpec as P

NEV = 96
LX = 16
LY = 8
LZ = 32
SITES = 128
AXES = ("x", "zl", "y", "zh", "c")
SIZES = (4, 2, 4, 4, 2)
DEPTH = 6 * SITES


def ring_pairs(target):
    pairs = []
    for x in range(4):
        for zl in range(2):
            for s in range(32):
                to = target(zl, s)
                if to is not None:
                    head = (x * 2 + zl) * 32
                    pairs.append((head + s, head + to))
    return pairs


def outer_plane(zl, s):
    if zl == 1:
        return None
    return (s + 1) % 32 if s % 2 == 1 else (s - 1) % 32


def phased_kernel(numbers, own, other, outer, out, field, ahead, behind):
    links = own[6 * NEV :, :].astype(jnp.float32)
    direction = numbers[3]
    core = lax.axis_index("c")
    plane = (lax.axis_index("y") * 4 + lax.axis_index("zh")) * 2 + core
    lane = lax.broadcasted_iota(jnp.int32, (1, SITES), 1)
    x_coord = lane % LX
    y_coord = lane // LX
    turns = (
        2 * jnp.bitwise_and(numbers[0] * x_coord, LX - 1)
        + 4 * jnp.bitwise_and(numbers[1] * y_coord, LY - 1)
        + jnp.bitwise_and(numbers[2] * plane, LZ - 1)
    )
    angle = (2.0 * math.pi / LZ) * jnp.bitwise_and(turns, LZ - 1).astype(jnp.float32)
    cos_part = jnp.cos(angle)
    sin_part = -jnp.sin(angle)

    @pl.when(direction == 2)
    def _():
        for comp in range(6):
            near = other[NEV * comp : NEV * comp + NEV, :].astype(jnp.float32)
            far = outer[NEV * comp : NEV * comp + NEV, :].astype(jnp.float32)
            ahead[comp] = jnp.where(core == 0, near, far)
            behind[comp] = jnp.where(core == 0, far, near)

    @pl.when(direction != 2)
    def _():
        step = jnp.where(direction == 0, 1, LX)
        last = jnp.logical_and(x_coord == LX - 1, direction == 0)
        first = jnp.logical_and(x_coord == 0, direction == 0)
        for comp in range(6):
            here = own[NEV * comp : NEV * comp + NEV, :].astype(jnp.float32)
            ahead[comp] = jnp.where(
                last, pltpu.roll(here, LX - 1, 1), pltpu.roll(here, SITES - step, 1)
            )
            behind[comp] = jnp.where(
                first, pltpu.roll(here, SITES - LX + 1, 1), pltpu.roll(here, step, 1)
            )

    z_back = jnp.where(
        core == 0,
        outer[6 * NEV :, :].astype(jnp.float32),
        other[6 * NEV :, :].astype(jnp.float32),
    )
    x_roll = jnp.where(
        x_coord == 0, pltpu.roll(links, SITES - LX + 1, 1), pltpu.roll(links, 1, 1)
    )
    y_roll = pltpu.roll(links, LX, 1)

    def matrix(table, part, row, column):
        return table[6 * row + 2 * column + part]

    here_link = []
    back_link = []
    for at in range(18):
        x_at, y_at, z_at = (slice(at + 18 * d, at + 18 * d + 1) for d in range(3))
        here_link.append(
            jnp.where(
                direction == 0, links[x_at], jnp.where(direction == 1, links[y_at], links[z_at])
            )
        )
        back_link.append(
            jnp.where(
                direction == 0,
                x_roll[x_at],
                jnp.where(direction == 1, y_roll[y_at], z_back[z_at]),
            )
        )

    for a in range(3):
        front_re = front_im = rear_re = rear_im = 0.0
        for b in range(3):
            u_re, u_im = matrix(here_link, 0, a, b), matrix(here_link, 1, a, b)
            v_re, v_im = ahead[b], ahead[3 + b]
            front_re += u_re * v_re - u_im * v_im
            front_im += u_re * v_im + u_im * v_re
            w_re, w_im = matrix(back_link, 0, b, a), matrix(back_link, 1, b, a)
            v_re, v_im = behind[b], behind[3 + b]
            rear_re += w_re * v_re + w_im * v_im
            rear_im += w_re * v_im - w_im * v_re
        moved_re = front_re - rear_re
        moved_im = front_im - rear_im
        field[a] = cos_part * moved_re - sin_part * moved_im
        field[3 + a] = cos_part * moved_im + sin_part * moved_re

    for comp in range(6):
        for rows in range(6):
            both = [field[comp, pl.ds(2 * rows + k, 8, 12), :] for k in range(2)]
            out[comp, 16 * rows : 16 * rows + 16, :] = jnp.concatenate(both, 0).astype(
                jnp.bfloat16
            )


def left_operand(phased, left):
    for a in range(3):
        real = phased[a]
        imag = phased[3 + a]
        column = a * SITES
        left[:NEV, column : column + SITES] = real
        left[NEV:, column : column + SITES] = imag
        column += 3 * SITES
        left[:NEV, column : column + SITES] = -imag
        left[NEV:, column : column + SITES] = real


def times(crossed, left):
    return lax.dot_general(
        crossed, left[...], (((1,), (1,)), ((), ())), preferred_element_type=jnp.float32
    )


def six_rows(step, vectors, out):
    core = lax.axis_index("c")
    keeper = jnp.where(step < 2, 1 - core, core)
    first = 24 * lax.axis_index("y") + 12 * (step % 2) + 3 * keeper
    for high in range(2):
        for low in range(3):
            mine = [vectors[comp, pl.ds(first + 6 * high + low, 1), :] for comp in range(9)]
            mine = [jnp.broadcast_to(m, (16, SITES)) for m in mine]
            my_re, my_im, my_sum = mine[:3], mine[3:6], mine[6:]
            for chunk in range(6):
                rows = slice(16 * chunk, 16 * chunk + 16)
                re, total, gap = (
                    [vectors[comp + colour, rows, :] for colour in range(3)]
                    for comp in (0, 6, 9)
                )
                at = 96 * low + 16 * chunk
                at = 256 * high + at if at < 256 else 256 + 32 * high + at
                for a in range(3):
                    b = (a + 1) % 3
                    c = (a + 2) % 3
                    shared = my_sum[b] * re[c] - my_sum[c] * re[b]
                    real = shared - (my_im[b] * total[c] - my_im[c] * total[b])
                    imag = shared + (my_re[b] * gap[c] - my_re[c] * gap[b])
                    column = a * SITES
                    out[step, at : at + 16, column : column + SITES] = real.astype(
                        jnp.bfloat16
                    )
                    column += 3 * SITES
                    out[step, at : at + 16, column : column + SITES] = imag.astype(
                        jnp.bfloat16
                    )


def spread(source, vectors):
    for colour in range(3):
        real = source[colour].astype(jnp.float32)
        imag = source[3 + colour].astype(jnp.float32)
        vectors[colour] = real
        vectors[3 + colour] = imag
        vectors[6 + colour] = real + imag
        vectors[9 + colour] = imag - real


def crossed_kernel(source, out, vectors):
    spread(source, vectors)

    def one_step(step, carry):
        six_rows(step, vectors, out)
        return carry

    lax.fori_loop(0, 4, one_step, 0)


def both_kernel(source, phased, previous, *rest):
    sums = rest[0] if len(rest) == 5 else None
    out, total, vectors, left = rest[-4:]
    spread(source, vectors)
    left_operand(phased, left)

    def one_step(step, carry):
        term = times(previous[step], left)
        total[step] = term if sums is None else sums[step] + term
        six_rows(step, vectors, out)
        return carry

    lax.fori_loop(0, 4, one_step, 0)


def last_kernel(phased, crossed, sums, theirs, mine, left):
    left_operand(phased, left)
    for out, half in ((theirs, 0), (mine, 1)):
        tails = []
        for part in range(2):
            step = 2 * half + part
            total = sums[step] + times(crossed[step], left)
            out[:, 512 * part : 512 * part + 512] = total[:512].T.astype(out.dtype)
            tails.append(total[512:])
        out[:, 1024:] = jnp.concatenate(tails, 0).T.astype(out.dtype)


def pack_kernel(mine, received, out, total):
    lane = lax.broadcasted_iota(jnp.int32, (8, SITES), 1)
    for tile in range(9):
        lanes = slice(SITES * tile, SITES * tile + SITES)
        total[tile] = mine[:, lanes] + received[:, lanes].astype(jnp.float32)
    for q in range(8):
        for zh in range(4):
            for half in range(2):
                out[4 * q + zh, 24 * half : 24 * half + 24, :] = total[
                    2 * zh + half, pl.ds(q, 24, 8), :
                ].astype(jnp.bfloat16)
        tail = total[8, pl.ds(q, 24, 8), :]
        for zh in range(4):
            joined = jnp.zeros((8, SITES), jnp.float32)
            for g in range(3):
                moved = pltpu.roll(tail[8 * g : 8 * g + 8], (32 * (g - zh)) % SITES, 1)
                joined = jnp.where(lane // 32 == g, moved, joined)
            out[4 * q + zh, 48:56, :] = joined.astype(jnp.bfloat16)


def final_kernel(parts, out, rows):
    scale = 1.0 / math.sqrt(LX * LY * LZ)
    for t in range(8):
        total = parts[4 * t].astype(jnp.float32)
        for zh in range(1, 4):
            total += parts[4 * t + zh].astype(jnp.float32)
        total *= scale
        rows[0, pl.ds(t, 24, 8), :] = total[:24]
        rows[1, pl.ds(t, 24, 8), :] = total[24:48]
        for g in range(3):
            tail = total[48:56]
            if g:
                tail = pltpu.roll(tail, SITES - 32 * g, 1)
            rows[2, pl.ds(64 * g + t, 8, 8), :] = tail
    for ri in range(2):
        pieces = [[], [], []]
        for i in range(12):
            at = 8 * (12 * ri + i)
            one, two, three = (rows[part, at : at + 8, :] for part in range(3))
            pieces[0].append(one[:, :96])
            pieces[1].append(one[:, 96:])
            pieces[1].append(two[:, :64])
            pieces[2].append(two[:, 64:])
            pieces[2].append(three[:, :32])
        for r in range(3):
            out[r, :, ri, :] = jnp.concatenate(pieces[r], axis=1)


def vmem():
    return pl.BlockSpec(memory_space=pltpu.VMEM)


def smem():
    return pl.BlockSpec(memory_space=pltpu.SMEM)


def params(mib):
    return pltpu.CompilerParams(vmem_limit_bytes=mib << 20)


def from_y(block, by):
    return lax.ppermute(block, "y", [(i, (i + by) % 4) for i in range(4)])


def on_device(vectors, gauge_links, momentum, direction):
    f32 = jnp.float32
    bf16 = jnp.bfloat16
    swap = [(0, 1), (1, 0)]
    own = jnp.transpose(vectors[0], (1, 2, 0, 3)).reshape(6, NEV, SITES)
    joined = jnp.concatenate(
        [
            own.reshape(6 * NEV, SITES),
            jnp.transpose(gauge_links[0], (0, 2, 3, 1, 4)).reshape(54, SITES),
            jnp.zeros((10, SITES), bf16),
        ]
    )
    before = from_y(own, 1)
    after = from_y(own, 3)
    crossed_shape = jax.ShapeDtypeStruct((4, 576, DEPTH), bf16)
    sums_shape = jax.ShapeDtypeStruct((4, 576, 192), f32)
    spread_scratch = pltpu.VMEM((12, NEV, SITES), f32)
    left_scratch = pltpu.VMEM((192, DEPTH), bf16)
    short = pl.CostEstimate(flops=0, bytes_accessed=0, transcendentals=0)

    numbers = jnp.concatenate([momentum, direction])
    joined, numbers, here, before, after = lax.optimization_barrier(
        (joined, numbers, own, before, after)
    )
    outer = lax.ppermute(joined, AXES, ring_pairs(outer_plane))
    other = lax.ppermute(joined, "c", swap)
    opposite = from_y(here, 2)
    crossed = pl.pallas_call(
        crossed_kernel,
        out_shape=crossed_shape,
        in_specs=[vmem()],
        out_specs=vmem(),
        scratch_shapes=[spread_scratch],
        compiler_params=params(4),
        cost_estimate=short,
    )(here)
    joined, crossed = lax.optimization_barrier((joined, crossed))
    phased = pl.pallas_call(
        phased_kernel,
        out_shape=jax.ShapeDtypeStruct((6, NEV, SITES), bf16),
        in_specs=[vmem()] * 4,
        out_specs=vmem(),
        scratch_shapes=[pltpu.VMEM((6, NEV, SITES), f32)] * 3,
        compiler_params=params(8),
    )(numbers, joined, other, outer)
    phased_before = from_y(phased, 1)
    phased_after = from_y(phased, 3)
    phased_opposite = from_y(phased, 2)

    def both(source, phased_plane, previous, *sums):
        return pl.pallas_call(
            both_kernel,
            out_shape=(crossed_shape, sums_shape),
            in_specs=[vmem()] * (3 + len(sums)),
            out_specs=(vmem(), vmem()),
            scratch_shapes=[spread_scratch, left_scratch],
            compiler_params=params(6),
            cost_estimate=short,
        )(source, phased_plane, previous, *sums)

    crossed, sums = both(before, phased, crossed)
    crossed, sums = both(opposite, phased_before, crossed, sums)
    crossed, sums = both(after, phased_opposite, crossed, sums)
    sent, mine = pl.pallas_call(
        last_kernel,
        out_shape=(
            jax.ShapeDtypeStruct((192, 1152), bf16),
            jax.ShapeDtypeStruct((192, 1152), f32),
        ),
        in_specs=[vmem()] * 3,
        out_specs=(vmem(), vmem()),
        scratch_shapes=[left_scratch],
        compiler_params=params(6),
    )(phased_after, crossed, sums)
    received = lax.ppermute(sent, "c", swap)
    packed = pl.pallas_call(
        pack_kernel,
        out_shape=jax.ShapeDtypeStruct((32, 56, SITES), bf16),
        in_specs=[vmem()] * 2,
        out_specs=vmem(),
        scratch_shapes=[pltpu.VMEM((9, 192, SITES), f32)],
        compiler_params=params(16),
    )(mine, received)
    packed = lax.all_to_all(packed, ("x", "zl", "zh"), 0, 0, tiled=True)
    return pl.pallas_call(
        final_kernel,
        out_shape=jax.ShapeDtypeStruct((3, 8, 2, 12 * NEV), f32),
        in_specs=[vmem()],
        out_specs=vmem(),
        scratch_shapes=[pltpu.VMEM((3, 192, SITES), f32)],
        compiler_params=params(16),
    )(packed)


def solution(mesh):
    cut = Mesh(mesh.devices.reshape(SIZES), AXES)
    return jax.shard_map(
        on_device,
        mesh=cut,
        in_specs=(
            P(("x", "zl"), None, None, None, ("y", "zh", "c")),
            P(("x", "zl"), None, None, None, None, ("y", "zh", "c")),
            P(),
            P(("x", "zl")),
        ),
        out_specs=P(("y", "zh", "c"), None, None, ("x", "zl")),
        check_vma=False,
    )
```

```python
import math

import jax
import jax.numpy as jnp
from jax import lax
from jax.experimental import pallas as pl
from jax.experimental.pallas import tpu as pltpu
from jax.sharding import Mesh
from jax.sharding import PartitionSpec as P

NEV = 96
LX = 16
LY = 8
LZ = 32
SITES = 128
AXES = ("x", "zl", "y", "zh", "c")
SIZES = (4, 2, 4, 4, 2)
DEPTH = 6 * SITES


def ring_pairs(target):
    pairs = []
    for x in range(4):
        for zl in range(2):
            for s in range(32):
                to = target(zl, s)
                if to is not None:
                    head = (x * 2 + zl) * 32
                    pairs.append((head + s, head + to))
    return pairs


def outer_plane(zl, s):
    if zl == 1:
        return None
    return (s + 1) % 32 if s % 2 == 1 else (s - 1) % 32


def phased_kernel(numbers, own, outer, other, out, field, ahead, behind):
    links = own[6 * NEV :, :].astype(jnp.float32)
    direction = numbers[3]
    core = lax.axis_index("c")
    plane = (lax.axis_index("y") * 4 + lax.axis_index("zh")) * 2 + core
    lane = lax.broadcasted_iota(jnp.int32, (1, SITES), 1)
    x_coord = lane % LX
    y_coord = lane // LX
    turns = (
        2 * jnp.bitwise_and(numbers[0] * x_coord, LX - 1)
        + 4 * jnp.bitwise_and(numbers[1] * y_coord, LY - 1)
        + jnp.bitwise_and(numbers[2] * plane, LZ - 1)
    )
    angle = (2.0 * math.pi / LZ) * jnp.bitwise_and(turns, LZ - 1).astype(jnp.float32)
    cos_part = jnp.cos(angle)
    sin_part = -jnp.sin(angle)

    @pl.when(direction == 2)
    def _():
        for comp in range(6):
            near = other[NEV * comp : NEV * comp + NEV, :].astype(jnp.float32)
            far = outer[NEV * comp : NEV * comp + NEV, :].astype(jnp.float32)
            ahead[comp] = jnp.where(core == 0, near, far)
            behind[comp] = jnp.where(core == 0, far, near)

    @pl.when(direction != 2)
    def _():
        step = jnp.where(direction == 0, 1, LX)
        last = jnp.logical_and(x_coord == LX - 1, direction == 0)
        first = jnp.logical_and(x_coord == 0, direction == 0)
        for comp in range(6):
            here = own[NEV * comp : NEV * comp + NEV, :].astype(jnp.float32)
            ahead[comp] = jnp.where(
                last, pltpu.roll(here, LX - 1, 1), pltpu.roll(here, SITES - step, 1)
            )
            behind[comp] = jnp.where(
                first, pltpu.roll(here, SITES - LX + 1, 1), pltpu.roll(here, step, 1)
            )

    z_back = jnp.where(
        core == 0,
        outer[6 * NEV :, :].astype(jnp.float32),
        other[6 * NEV :, :].astype(jnp.float32),
    )
    x_roll = jnp.where(
        x_coord == 0, pltpu.roll(links, SITES - LX + 1, 1), pltpu.roll(links, 1, 1)
    )
    y_roll = pltpu.roll(links, LX, 1)

    def matrix(table, part, row, column):
        return table[6 * row + 2 * column + part]

    here_link = []
    back_link = []
    for at in range(18):
        x_at, y_at, z_at = (slice(at + 18 * d, at + 18 * d + 1) for d in range(3))
        here_link.append(
            jnp.where(
                direction == 0, links[x_at], jnp.where(direction == 1, links[y_at], links[z_at])
            )
        )
        back_link.append(
            jnp.where(
                direction == 0,
                x_roll[x_at],
                jnp.where(direction == 1, y_roll[y_at], z_back[z_at]),
            )
        )

    for a in range(3):
        front_re = front_im = rear_re = rear_im = 0.0
        for b in range(3):
            u_re, u_im = matrix(here_link, 0, a, b), matrix(here_link, 1, a, b)
            v_re, v_im = ahead[b], ahead[3 + b]
            front_re += u_re * v_re - u_im * v_im
            front_im += u_re * v_im + u_im * v_re
            w_re, w_im = matrix(back_link, 0, b, a), matrix(back_link, 1, b, a)
            v_re, v_im = behind[b], behind[3 + b]
            rear_re += w_re * v_re + w_im * v_im
            rear_im += w_re * v_im - w_im * v_re
        moved_re = front_re - rear_re
        moved_im = front_im - rear_im
        field[a] = cos_part * moved_re - sin_part * moved_im
        field[3 + a] = cos_part * moved_im + sin_part * moved_re

    for comp in range(6):
        for rows in range(6):
            both = [field[comp, pl.ds(2 * rows + k, 8, 12), :] for k in range(2)]
            out[comp, 16 * rows : 16 * rows + 16, :] = jnp.concatenate(both, 0).astype(
                jnp.bfloat16
            )


def left_operand(phased, left):
    for a in range(3):
        real = phased[a]
        imag = phased[3 + a]
        column = a * SITES
        left[:NEV, column : column + SITES] = real
        left[NEV:, column : column + SITES] = imag
        column += 3 * SITES
        left[:NEV, column : column + SITES] = -imag
        left[NEV:, column : column + SITES] = real


def times(crossed, left):
    return lax.dot_general(
        crossed, left[...], (((1,), (1,)), ((), ())), preferred_element_type=jnp.float32
    )


def six_rows(step, vectors, out):
    core = lax.axis_index("c")
    keeper = jnp.where(step < 2, 1 - core, core)
    first = 24 * lax.axis_index("y") + 12 * (step % 2) + 3 * keeper
    for high in range(2):
        for low in range(3):
            mine = [vectors[comp, pl.ds(first + 6 * high + low, 1), :] for comp in range(9)]
            mine = [jnp.broadcast_to(m, (16, SITES)) for m in mine]
            my_re, my_im, my_sum = mine[:3], mine[3:6], mine[6:]
            for chunk in range(6):
                rows = slice(16 * chunk, 16 * chunk + 16)
                re, total, gap = (
                    [vectors[comp + colour, rows, :] for colour in range(3)]
                    for comp in (0, 6, 9)
                )
                at = 96 * low + 16 * chunk
                at = 256 * high + at if at < 256 else 256 + 32 * high + at
                for a in range(3):
                    b = (a + 1) % 3
                    c = (a + 2) % 3
                    shared = my_sum[b] * re[c] - my_sum[c] * re[b]
                    real = shared - (my_im[b] * total[c] - my_im[c] * total[b])
                    imag = shared + (my_re[b] * gap[c] - my_re[c] * gap[b])
                    column = a * SITES
                    out[step, at : at + 16, column : column + SITES] = real.astype(
                        jnp.bfloat16
                    )
                    column += 3 * SITES
                    out[step, at : at + 16, column : column + SITES] = imag.astype(
                        jnp.bfloat16
                    )


def spread(source, vectors):
    for colour in range(3):
        real = source[colour].astype(jnp.float32)
        imag = source[3 + colour].astype(jnp.float32)
        vectors[colour] = real
        vectors[3 + colour] = imag
        vectors[6 + colour] = real + imag
        vectors[9 + colour] = imag - real


def crossed_kernel(source, out, vectors):
    spread(source, vectors)

    def one_step(step, carry):
        six_rows(step, vectors, out)
        return carry

    lax.fori_loop(0, 4, one_step, 0)


def both_kernel(source, phased, previous, *rest):
    sums = rest[0] if len(rest) == 5 else None
    out, total, vectors, left = rest[-4:]
    spread(source, vectors)
    left_operand(phased, left)

    def one_step(step, carry):
        term = times(previous[step], left)
        total[step] = term if sums is None else sums[step] + term
        six_rows(step, vectors, out)
        return carry

    lax.fori_loop(0, 4, one_step, 0)


def last_kernel(phased, crossed, sums, theirs, mine, left):
    left_operand(phased, left)
    for out, half in ((theirs, 0), (mine, 1)):
        tails = []
        for part in range(2):
            step = 2 * half + part
            total = sums[step] + times(crossed[step], left)
            out[:, 512 * part : 512 * part + 512] = total[:512].T.astype(out.dtype)
            tails.append(total[512:])
        out[:, 1024:] = jnp.concatenate(tails, 0).T.astype(out.dtype)


def pack_kernel(mine, received, out, total):
    lane = lax.broadcasted_iota(jnp.int32, (8, SITES), 1)
    for tile in range(9):
        lanes = slice(SITES * tile, SITES * tile + SITES)
        total[tile] = mine[:, lanes] + received[:, lanes].astype(jnp.float32)
    for q in range(8):
        for zh in range(4):
            for half in range(2):
                out[4 * q + zh, 24 * half : 24 * half + 24, :] = total[
                    2 * zh + half, pl.ds(q, 24, 8), :
                ].astype(jnp.bfloat16)
        tail = total[8, pl.ds(q, 24, 8), :]
        for zh in range(4):
            joined = jnp.zeros((8, SITES), jnp.float32)
            for g in range(3):
                moved = pltpu.roll(tail[8 * g : 8 * g + 8], (32 * (g - zh)) % SITES, 1)
                joined = jnp.where(lane // 32 == g, moved, joined)
            out[4 * q + zh, 48:56, :] = joined.astype(jnp.bfloat16)


def final_kernel(parts, out, rows):
    scale = 1.0 / math.sqrt(LX * LY * LZ)
    for t in range(8):
        total = parts[4 * t].astype(jnp.float32)
        for zh in range(1, 4):
            total += parts[4 * t + zh].astype(jnp.float32)
        total *= scale
        rows[0, pl.ds(t, 24, 8), :] = total[:24]
        rows[1, pl.ds(t, 24, 8), :] = total[24:48]
        for g in range(3):
            tail = total[48:56]
            if g:
                tail = pltpu.roll(tail, SITES - 32 * g, 1)
            rows[2, pl.ds(64 * g + t, 8, 8), :] = tail
    for ri in range(2):
        pieces = [[], [], []]
        for i in range(12):
            at = 8 * (12 * ri + i)
            one, two, three = (rows[part, at : at + 8, :] for part in range(3))
            pieces[0].append(one[:, :96])
            pieces[1].append(one[:, 96:])
            pieces[1].append(two[:, :64])
            pieces[2].append(two[:, 64:])
            pieces[2].append(three[:, :32])
        for r in range(3):
            out[r, :, ri, :] = jnp.concatenate(pieces[r], axis=1)


def vmem():
    return pl.BlockSpec(memory_space=pltpu.VMEM)


def smem():
    return pl.BlockSpec(memory_space=pltpu.SMEM)


def params(mib):
    return pltpu.CompilerParams(vmem_limit_bytes=mib << 20)


def from_y(block, by):
    return lax.ppermute(block, "y", [(i, (i + by) % 4) for i in range(4)])


def on_device(vectors, gauge_links, momentum, direction):
    f32 = jnp.float32
    bf16 = jnp.bfloat16
    swap = [(0, 1), (1, 0)]
    own = jnp.transpose(vectors[0], (1, 2, 0, 3)).reshape(6, NEV, SITES)
    joined = jnp.concatenate(
        [
            own.reshape(6 * NEV, SITES),
            jnp.transpose(gauge_links[0], (0, 2, 3, 1, 4)).reshape(54, SITES),
            jnp.zeros((10, SITES), bf16),
        ]
    )
    other = lax.ppermute(joined, "c", swap)
    outer = lax.ppermute(joined, AXES, ring_pairs(outer_plane))
    before = from_y(own, 1)
    after = from_y(own, 3)
    opposite = from_y(own, 2)
    phased = pl.pallas_call(
        phased_kernel,
        out_shape=jax.ShapeDtypeStruct((6, NEV, SITES), bf16),
        in_specs=[vmem()] * 4,
        out_specs=vmem(),
        scratch_shapes=[pltpu.VMEM((6, NEV, SITES), f32)] * 3,
        compiler_params=params(8),
    )(jnp.concatenate([momentum, direction]), joined, outer, other)
    phased_before = from_y(phased, 1)
    phased_after = from_y(phased, 3)
    phased_opposite = from_y(phased, 2)
    before, after, opposite = lax.optimization_barrier((before, after, opposite))

    crossed_shape = jax.ShapeDtypeStruct((4, 576, DEPTH), bf16)
    sums_shape = jax.ShapeDtypeStruct((4, 576, 192), f32)
    spread_scratch = pltpu.VMEM((12, NEV, SITES), f32)
    left_scratch = pltpu.VMEM((192, DEPTH), bf16)
    short = pl.CostEstimate(flops=0, bytes_accessed=0, transcendentals=0)

    def both(source, phased_plane, previous, *sums):
        return pl.pallas_call(
            both_kernel,
            out_shape=(crossed_shape, sums_shape),
            in_specs=[vmem()] * (3 + len(sums)),
            out_specs=(vmem(), vmem()),
            scratch_shapes=[spread_scratch, left_scratch],
            compiler_params=params(6),
            cost_estimate=short,
        )(source, phased_plane, previous, *sums)

    crossed = pl.pallas_call(
        crossed_kernel,
        out_shape=crossed_shape,
        in_specs=[vmem()],
        out_specs=vmem(),
        scratch_shapes=[spread_scratch],
        compiler_params=params(4),
        cost_estimate=short,
    )(own)
    crossed, sums = both(before, phased, crossed)
    crossed, sums = both(after, phased_before, crossed, sums)
    crossed, sums = both(opposite, phased_after, crossed, sums)
    sent, mine = pl.pallas_call(
        last_kernel,
        out_shape=(
            jax.ShapeDtypeStruct((192, 1152), bf16),
            jax.ShapeDtypeStruct((192, 1152), f32),
        ),
        in_specs=[vmem()] * 3,
        out_specs=(vmem(), vmem()),
        scratch_shapes=[left_scratch],
        compiler_params=params(6),
    )(phased_opposite, crossed, sums)
    received = lax.ppermute(sent, "c", swap)
    packed = pl.pallas_call(
        pack_kernel,
        out_shape=jax.ShapeDtypeStruct((32, 56, SITES), bf16),
        in_specs=[vmem()] * 2,
        out_specs=vmem(),
        scratch_shapes=[pltpu.VMEM((9, 192, SITES), f32)],
        compiler_params=params(16),
    )(mine, received)
    packed = lax.all_to_all(packed, ("x", "zl", "zh"), 0, 0, tiled=True)
    return pl.pallas_call(
        final_kernel,
        out_shape=jax.ShapeDtypeStruct((3, 8, 2, 12 * NEV), f32),
        in_specs=[vmem()],
        out_specs=vmem(),
        scratch_shapes=[pltpu.VMEM((3, 192, SITES), f32)],
        compiler_params=params(16),
    )(packed)


def solution(mesh):
    cut = Mesh(mesh.devices.reshape(SIZES), AXES)
    return jax.shard_map(
        on_device,
        mesh=cut,
        in_specs=(
            P(("x", "zl"), None, None, None, ("y", "zh", "c")),
            P(("x", "zl"), None, None, None, None, ("y", "zh", "c")),
            P(),
            P(("x", "zl")),
        ),
        out_specs=P(("y", "zh", "c"), None, None, ("x", "zl")),
        check_vma=False,
    )
```

```python
import math

import jax
import jax.numpy as jnp
from jax import lax
from jax.experimental import pallas as pl
from jax.experimental.pallas import tpu as pltpu
from jax.sharding import Mesh
from jax.sharding import PartitionSpec as P

NEV = 96
LX = 16
LY = 8
LZ = 32
SITES = 128
AXES = ("x", "zl", "y", "zh", "c")
SIZES = (4, 2, 4, 4, 2)
DEPTH = 6 * SITES


def ring_pairs(target):
    pairs = []
    for x in range(4):
        for zl in range(2):
            for s in range(32):
                to = target(zl, s)
                if to is not None:
                    head = (x * 2 + zl) * 32
                    pairs.append((head + s, head + to))
    return pairs


def outer_plane(zl, s):
    if zl == 1:
        return None
    return (s + 1) % 32 if s % 2 == 1 else (s - 1) % 32


def phased_kernel(numbers, own, outer, other, out, pair, field, ahead, behind):
    links = own[6 * NEV :, :].astype(jnp.float32)
    direction = numbers[3]
    core = lax.axis_index("c")
    plane = (lax.axis_index("y") * 4 + lax.axis_index("zh")) * 2 + core
    lane = lax.broadcasted_iota(jnp.int32, (1, SITES), 1)
    x_coord = lane % LX
    y_coord = lane // LX
    turns = (
        2 * jnp.bitwise_and(numbers[0] * x_coord, LX - 1)
        + 4 * jnp.bitwise_and(numbers[1] * y_coord, LY - 1)
        + jnp.bitwise_and(numbers[2] * plane, LZ - 1)
    )
    angle = (2.0 * math.pi / LZ) * jnp.bitwise_and(turns, LZ - 1).astype(jnp.float32)
    cos_part = jnp.cos(angle)
    sin_part = -jnp.sin(angle)

    @pl.when(direction == 2)
    def _():
        for comp in range(6):
            near = other[NEV * comp : NEV * comp + NEV, :].astype(jnp.float32)
            far = outer[NEV * comp : NEV * comp + NEV, :].astype(jnp.float32)
            ahead[comp] = jnp.where(core == 0, near, far)
            behind[comp] = jnp.where(core == 0, far, near)

    @pl.when(direction != 2)
    def _():
        step = jnp.where(direction == 0, 1, LX)
        last = jnp.logical_and(x_coord == LX - 1, direction == 0)
        first = jnp.logical_and(x_coord == 0, direction == 0)
        for comp in range(6):
            here = own[NEV * comp : NEV * comp + NEV, :].astype(jnp.float32)
            ahead[comp] = jnp.where(
                last, pltpu.roll(here, LX - 1, 1), pltpu.roll(here, SITES - step, 1)
            )
            behind[comp] = jnp.where(
                first, pltpu.roll(here, SITES - LX + 1, 1), pltpu.roll(here, step, 1)
            )

    z_back = jnp.where(
        core == 0,
        outer[6 * NEV :, :].astype(jnp.float32),
        other[6 * NEV :, :].astype(jnp.float32),
    )
    x_roll = jnp.where(
        x_coord == 0, pltpu.roll(links, SITES - LX + 1, 1), pltpu.roll(links, 1, 1)
    )
    y_roll = pltpu.roll(links, LX, 1)

    def matrix(table, part, row, column):
        return table[6 * row + 2 * column + part]

    here_link = []
    back_link = []
    for at in range(18):
        x_at, y_at, z_at = (slice(at + 18 * d, at + 18 * d + 1) for d in range(3))
        here_link.append(
            jnp.where(
                direction == 0, links[x_at], jnp.where(direction == 1, links[y_at], links[z_at])
            )
        )
        back_link.append(
            jnp.where(
                direction == 0,
                x_roll[x_at],
                jnp.where(direction == 1, y_roll[y_at], z_back[z_at]),
            )
        )

    for a in range(3):
        front_re = front_im = rear_re = rear_im = 0.0
        for b in range(3):
            u_re, u_im = matrix(here_link, 0, a, b), matrix(here_link, 1, a, b)
            v_re, v_im = ahead[b], ahead[3 + b]
            front_re += u_re * v_re - u_im * v_im
            front_im += u_re * v_im + u_im * v_re
            w_re, w_im = matrix(back_link, 0, b, a), matrix(back_link, 1, b, a)
            v_re, v_im = behind[b], behind[3 + b]
            rear_re += w_re * v_re + w_im * v_im
            rear_im += w_re * v_im - w_im * v_re
        moved_re = front_re - rear_re
        moved_im = front_im - rear_im
        field[a] = cos_part * moved_re - sin_part * moved_im
        field[3 + a] = cos_part * moved_im + sin_part * moved_re

    for comp in range(6):
        for rows in range(6):
            both = [field[comp, pl.ds(2 * rows + k, 8, 12), :] for k in range(2)]
            block = jnp.concatenate(both, 0).astype(jnp.bfloat16)
            out[comp, 16 * rows : 16 * rows + 16, :] = block
            pair[1, comp, 16 * rows : 16 * rows + 16, :] = block
        pair[0, comp] = own[NEV * comp : NEV * comp + NEV, :]


def left_operand(phased, left):
    for a in range(3):
        real = phased[a]
        imag = phased[3 + a]
        column = a * SITES
        left[:NEV, column : column + SITES] = real
        left[NEV:, column : column + SITES] = imag
        column += 3 * SITES
        left[:NEV, column : column + SITES] = -imag
        left[NEV:, column : column + SITES] = real


def times(crossed, left):
    return lax.dot_general(
        crossed, left[...], (((1,), (1,)), ((), ())), preferred_element_type=jnp.float32
    )


def six_rows(step, vectors, out):
    core = lax.axis_index("c")
    keeper = jnp.where(step < 2, 1 - core, core)
    first = 24 * lax.axis_index("y") + 12 * (step % 2) + 3 * keeper
    for high in range(2):
        for low in range(3):
            mine = [vectors[comp, pl.ds(first + 6 * high + low, 1), :] for comp in range(9)]
            mine = [jnp.broadcast_to(m, (16, SITES)) for m in mine]
            my_re, my_im, my_sum = mine[:3], mine[3:6], mine[6:]
            for chunk in range(6):
                rows = slice(16 * chunk, 16 * chunk + 16)
                re, total, gap = (
                    [vectors[comp + colour, rows, :] for colour in range(3)]
                    for comp in (0, 6, 9)
                )
                at = 96 * low + 16 * chunk
                at = 256 * high + at if at < 256 else 256 + 32 * high + at
                for a in range(3):
                    b = (a + 1) % 3
                    c = (a + 2) % 3
                    shared = my_sum[b] * re[c] - my_sum[c] * re[b]
                    real = shared - (my_im[b] * total[c] - my_im[c] * total[b])
                    imag = shared + (my_re[b] * gap[c] - my_re[c] * gap[b])
                    column = a * SITES
                    out[step, at : at + 16, column : column + SITES] = real.astype(
                        jnp.bfloat16
                    )
                    column += 3 * SITES
                    out[step, at : at + 16, column : column + SITES] = imag.astype(
                        jnp.bfloat16
                    )


def spread(source, vectors):
    for colour in range(3):
        real = source[colour].astype(jnp.float32)
        imag = source[3 + colour].astype(jnp.float32)
        vectors[colour] = real
        vectors[3 + colour] = imag
        vectors[6 + colour] = real + imag
        vectors[9 + colour] = imag - real


def crossed_kernel(source, out, vectors):
    spread(source, vectors)

    def one_step(step, carry):
        six_rows(step, vectors, out)
        return carry

    lax.fori_loop(0, 4, one_step, 0)


def both_kernel(source, phased, previous, *rest):
    if len(source.shape) == 4:
        source = source.at[0]
    sums = rest[0] if len(rest) == 5 else None
    out, total, vectors, left = rest[-4:]
    spread(source, vectors)
    left_operand(phased, left)

    def one_step(step, carry):
        term = times(previous[step], left)
        total[step] = term if sums is None else sums[step] + term
        six_rows(step, vectors, out)
        return carry

    lax.fori_loop(0, 4, one_step, 0)


def last_kernel(pair, crossed, sums, theirs, mine, left):
    left_operand(pair.at[1], left)
    for out, half in ((theirs, 0), (mine, 1)):
        tails = []
        for part in range(2):
            step = 2 * half + part
            total = sums[step] + times(crossed[step], left)
            out[:, 512 * part : 512 * part + 512] = total[:512].T.astype(out.dtype)
            tails.append(total[512:])
        out[:, 1024:] = jnp.concatenate(tails, 0).T.astype(out.dtype)


def pack_kernel(mine, received, out, total):
    lane = lax.broadcasted_iota(jnp.int32, (8, SITES), 1)
    for tile in range(9):
        lanes = slice(SITES * tile, SITES * tile + SITES)
        total[tile] = mine[:, lanes] + received[:, lanes].astype(jnp.float32)
    for q in range(8):
        for zh in range(4):
            for half in range(2):
                out[4 * q + zh, 24 * half : 24 * half + 24, :] = total[
                    2 * zh + half, pl.ds(q, 24, 8), :
                ].astype(jnp.bfloat16)
        tail = total[8, pl.ds(q, 24, 8), :]
        for zh in range(4):
            joined = jnp.zeros((8, SITES), jnp.float32)
            for g in range(3):
                moved = pltpu.roll(tail[8 * g : 8 * g + 8], (32 * (g - zh)) % SITES, 1)
                joined = jnp.where(lane // 32 == g, moved, joined)
            out[4 * q + zh, 48:56, :] = joined.astype(jnp.bfloat16)


def final_kernel(parts, out, rows):
    scale = 1.0 / math.sqrt(LX * LY * LZ)
    for t in range(8):
        total = parts[4 * t].astype(jnp.float32)
        for zh in range(1, 4):
            total += parts[4 * t + zh].astype(jnp.float32)
        total *= scale
        rows[0, pl.ds(t, 24, 8), :] = total[:24]
        rows[1, pl.ds(t, 24, 8), :] = total[24:48]
        for g in range(3):
            tail = total[48:56]
            if g:
                tail = pltpu.roll(tail, SITES - 32 * g, 1)
            rows[2, pl.ds(64 * g + t, 8, 8), :] = tail
    for ri in range(2):
        pieces = [[], [], []]
        for i in range(12):
            at = 8 * (12 * ri + i)
            one, two, three = (rows[part, at : at + 8, :] for part in range(3))
            pieces[0].append(one[:, :96])
            pieces[1].append(one[:, 96:])
            pieces[1].append(two[:, :64])
            pieces[2].append(two[:, 64:])
            pieces[2].append(three[:, :32])
        for r in range(3):
            out[r, :, ri, :] = jnp.concatenate(pieces[r], axis=1)


def vmem():
    return pl.BlockSpec(memory_space=pltpu.VMEM)


def smem():
    return pl.BlockSpec(memory_space=pltpu.SMEM)


def params(mib):
    return pltpu.CompilerParams(vmem_limit_bytes=mib << 20)


def from_y(block, by):
    return lax.ppermute(block, "y", [(i, (i + by) % 4) for i in range(4)])


def on_device(vectors, gauge_links, momentum, direction):
    f32 = jnp.float32
    bf16 = jnp.bfloat16
    swap = [(0, 1), (1, 0)]
    own = jnp.transpose(vectors[0], (1, 2, 0, 3)).reshape(6, NEV, SITES)
    joined = jnp.concatenate(
        [
            own.reshape(6 * NEV, SITES),
            jnp.transpose(gauge_links[0], (0, 2, 3, 1, 4)).reshape(54, SITES),
            jnp.zeros((10, SITES), bf16),
        ]
    )
    other = lax.ppermute(joined, "c", swap)
    outer = lax.ppermute(joined, AXES, ring_pairs(outer_plane))
    before = from_y(own, 1)
    after = from_y(own, 3)
    phased, pair = pl.pallas_call(
        phased_kernel,
        out_shape=(
            jax.ShapeDtypeStruct((6, NEV, SITES), bf16),
            jax.ShapeDtypeStruct((2, 6, NEV, SITES), bf16),
        ),
        in_specs=[vmem()] * 4,
        out_specs=(vmem(), vmem()),
        scratch_shapes=[pltpu.VMEM((6, NEV, SITES), f32)] * 3,
        compiler_params=params(8),
    )(jnp.concatenate([momentum, direction]), joined, outer, other)
    phased_before = from_y(phased, 1)
    phased_after = from_y(phased, 3)
    pair, before, after = lax.optimization_barrier((pair, before, after))
    opposite = from_y(pair, 2)

    crossed_shape = jax.ShapeDtypeStruct((4, 576, DEPTH), bf16)
    sums_shape = jax.ShapeDtypeStruct((4, 576, 192), f32)
    spread_scratch = pltpu.VMEM((12, NEV, SITES), f32)
    left_scratch = pltpu.VMEM((192, DEPTH), bf16)
    short = pl.CostEstimate(flops=0, bytes_accessed=0, transcendentals=0)

    def both(source, phased_plane, previous, *sums):
        return pl.pallas_call(
            both_kernel,
            out_shape=(crossed_shape, sums_shape),
            in_specs=[vmem()] * (3 + len(sums)),
            out_specs=(vmem(), vmem()),
            scratch_shapes=[spread_scratch, left_scratch],
            compiler_params=params(6),
            cost_estimate=short,
        )(source, phased_plane, previous, *sums)

    crossed = pl.pallas_call(
        crossed_kernel,
        out_shape=crossed_shape,
        in_specs=[vmem()],
        out_specs=vmem(),
        scratch_shapes=[spread_scratch],
        compiler_params=params(4),
        cost_estimate=short,
    )(own)
    crossed, sums = both(before, phased, crossed)
    crossed, sums = both(after, phased_before, crossed, sums)
    crossed, sums = both(opposite, phased_after, crossed, sums)
    sent, mine = pl.pallas_call(
        last_kernel,
        out_shape=(
            jax.ShapeDtypeStruct((192, 1152), bf16),
            jax.ShapeDtypeStruct((192, 1152), f32),
        ),
        in_specs=[vmem()] * 3,
        out_specs=(vmem(), vmem()),
        scratch_shapes=[left_scratch],
        compiler_params=params(6),
    )(opposite, crossed, sums)
    received = lax.ppermute(sent, "c", swap)
    packed = pl.pallas_call(
        pack_kernel,
        out_shape=jax.ShapeDtypeStruct((32, 56, SITES), bf16),
        in_specs=[vmem()] * 2,
        out_specs=vmem(),
        scratch_shapes=[pltpu.VMEM((9, 192, SITES), f32)],
        compiler_params=params(16),
    )(mine, received)
    packed = lax.all_to_all(packed, ("x", "zl", "zh"), 0, 0, tiled=True)
    return pl.pallas_call(
        final_kernel,
        out_shape=jax.ShapeDtypeStruct((3, 8, 2, 12 * NEV), f32),
        in_specs=[vmem()],
        out_specs=vmem(),
        scratch_shapes=[pltpu.VMEM((3, 192, SITES), f32)],
        compiler_params=params(16),
    )(packed)


def solution(mesh):
    cut = Mesh(mesh.devices.reshape(SIZES), AXES)
    return jax.shard_map(
        on_device,
        mesh=cut,
        in_specs=(
            P(("x", "zl"), None, None, None, ("y", "zh", "c")),
            P(("x", "zl"), None, None, None, None, ("y", "zh", "c")),
            P(),
            P(("x", "zl")),
        ),
        out_specs=P(("y", "zh", "c"), None, None, ("x", "zl")),
        check_vma=False,
    )
```

```python
import math

import jax
import jax.numpy as jnp
from jax import lax
from jax.experimental import pallas as pl
from jax.experimental.pallas import tpu as pltpu
from jax.sharding import Mesh
from jax.sharding import PartitionSpec as P

NEV = 96
LX = 16
LY = 8
LZ = 32
SITES = 128
AXES = ("x", "zl", "y", "zh", "c")
SIZES = (4, 2, 4, 4, 2)
DEPTH = 6 * SITES


def ring_pairs(target):
    pairs = []
    for x in range(4):
        for zl in range(2):
            for s in range(32):
                to = target(zl, s)
                if to is not None:
                    head = (x * 2 + zl) * 32
                    pairs.append((head + s, head + to))
    return pairs


def outer_plane(zl, s):
    if zl == 1:
        return None
    return (s + 1) % 32 if s % 2 == 1 else (s - 1) % 32


def phased_kernel(numbers, own, outer, other, out, field, ahead, behind):
    links = own[6 * NEV :, :].astype(jnp.float32)
    direction = numbers[3]
    core = lax.axis_index("c")
    plane = (lax.axis_index("y") * 4 + lax.axis_index("zh")) * 2 + core
    lane = lax.broadcasted_iota(jnp.int32, (1, SITES), 1)
    x_coord = lane % LX
    y_coord = lane // LX
    turns = (
        2 * jnp.bitwise_and(numbers[0] * x_coord, LX - 1)
        + 4 * jnp.bitwise_and(numbers[1] * y_coord, LY - 1)
        + jnp.bitwise_and(numbers[2] * plane, LZ - 1)
    )
    angle = (2.0 * math.pi / LZ) * jnp.bitwise_and(turns, LZ - 1).astype(jnp.float32)
    cos_part = jnp.cos(angle)
    sin_part = -jnp.sin(angle)

    @pl.when(direction == 2)
    def _():
        for comp in range(6):
            near = other[NEV * comp : NEV * comp + NEV, :].astype(jnp.float32)
            far = outer[NEV * comp : NEV * comp + NEV, :].astype(jnp.float32)
            ahead[comp] = jnp.where(core == 0, near, far)
            behind[comp] = jnp.where(core == 0, far, near)

    @pl.when(direction != 2)
    def _():
        step = jnp.where(direction == 0, 1, LX)
        last = jnp.logical_and(x_coord == LX - 1, direction == 0)
        first = jnp.logical_and(x_coord == 0, direction == 0)
        for comp in range(6):
            here = own[NEV * comp : NEV * comp + NEV, :].astype(jnp.float32)
            ahead[comp] = jnp.where(
                last, pltpu.roll(here, LX - 1, 1), pltpu.roll(here, SITES - step, 1)
            )
            behind[comp] = jnp.where(
                first, pltpu.roll(here, SITES - LX + 1, 1), pltpu.roll(here, step, 1)
            )

    z_back = jnp.where(
        core == 0,
        outer[6 * NEV :, :].astype(jnp.float32),
        other[6 * NEV :, :].astype(jnp.float32),
    )
    x_roll = jnp.where(
        x_coord == 0, pltpu.roll(links, SITES - LX + 1, 1), pltpu.roll(links, 1, 1)
    )
    y_roll = pltpu.roll(links, LX, 1)

    def matrix(table, part, row, column):
        return table[6 * row + 2 * column + part]

    here_link = []
    back_link = []
    for at in range(18):
        x_at, y_at, z_at = (slice(at + 18 * d, at + 18 * d + 1) for d in range(3))
        here_link.append(
            jnp.where(
                direction == 0, links[x_at], jnp.where(direction == 1, links[y_at], links[z_at])
            )
        )
        back_link.append(
            jnp.where(
                direction == 0,
                x_roll[x_at],
                jnp.where(direction == 1, y_roll[y_at], z_back[z_at]),
            )
        )

    for a in range(3):
        front_re = front_im = rear_re = rear_im = 0.0
        for b in range(3):
            u_re, u_im = matrix(here_link, 0, a, b), matrix(here_link, 1, a, b)
            v_re, v_im = ahead[b], ahead[3 + b]
            front_re += u_re * v_re - u_im * v_im
            front_im += u_re * v_im + u_im * v_re
            w_re, w_im = matrix(back_link, 0, b, a), matrix(back_link, 1, b, a)
            v_re, v_im = behind[b], behind[3 + b]
            rear_re += w_re * v_re + w_im * v_im
            rear_im += w_re * v_im - w_im * v_re
        moved_re = front_re - rear_re
        moved_im = front_im - rear_im
        field[a] = cos_part * moved_re - sin_part * moved_im
        field[3 + a] = cos_part * moved_im + sin_part * moved_re

    for comp in range(6):
        for rows in range(6):
            both = [field[comp, pl.ds(2 * rows + k, 8, 12), :] for k in range(2)]
            out[comp, 16 * rows : 16 * rows + 16, :] = jnp.concatenate(both, 0).astype(
                jnp.bfloat16
            )


def left_operand(phased, left):
    for a in range(3):
        real = phased[a]
        imag = phased[3 + a]
        column = a * SITES
        left[:NEV, column : column + SITES] = real
        left[NEV:, column : column + SITES] = imag
        column += 3 * SITES
        left[:NEV, column : column + SITES] = -imag
        left[NEV:, column : column + SITES] = real


def times(crossed, left):
    return lax.dot_general(
        crossed, left[...], (((1,), (1,)), ((), ())), preferred_element_type=jnp.float32
    )


def six_rows(step, vectors, out):
    core = lax.axis_index("c")
    keeper = jnp.where(step < 2, 1 - core, core)
    first = 24 * lax.axis_index("y") + 12 * (step % 2) + 3 * keeper
    for high in range(2):
        for low in range(3):
            mine = [vectors[comp, pl.ds(first + 6 * high + low, 1), :] for comp in range(9)]
            mine = [jnp.broadcast_to(m, (16, SITES)) for m in mine]
            my_re, my_im, my_sum = mine[:3], mine[3:6], mine[6:]
            for chunk in range(6):
                rows = slice(16 * chunk, 16 * chunk + 16)
                re, total, gap = (
                    [vectors[comp + colour, rows, :] for colour in range(3)]
                    for comp in (0, 6, 9)
                )
                at = 96 * low + 16 * chunk
                at = 256 * high + at if at < 256 else 256 + 32 * high + at
                for a in range(3):
                    b = (a + 1) % 3
                    c = (a + 2) % 3
                    shared = my_sum[b] * re[c] - my_sum[c] * re[b]
                    real = shared - (my_im[b] * total[c] - my_im[c] * total[b])
                    imag = shared + (my_re[b] * gap[c] - my_re[c] * gap[b])
                    column = a * SITES
                    out[step, at : at + 16, column : column + SITES] = real.astype(
                        jnp.bfloat16
                    )
                    column += 3 * SITES
                    out[step, at : at + 16, column : column + SITES] = imag.astype(
                        jnp.bfloat16
                    )


def spread(source, vectors):
    for colour in range(3):
        real = source[colour].astype(jnp.float32)
        imag = source[3 + colour].astype(jnp.float32)
        vectors[colour] = real
        vectors[3 + colour] = imag
        vectors[6 + colour] = real + imag
        vectors[9 + colour] = imag - real


def crossed_kernel(source, out, vectors):
    spread(source, vectors)

    def one_step(step, carry):
        six_rows(step, vectors, out)
        return carry

    lax.fori_loop(0, 4, one_step, 0)


def both_kernel(source, phased, previous, *rest):
    sums = rest[0] if len(rest) == 5 else None
    out, total, vectors, left = rest[-4:]
    spread(source, vectors)
    left_operand(phased, left)

    def one_step(step, carry):
        term = times(previous[step], left)
        total[step] = term if sums is None else sums[step] + term
        six_rows(step, vectors, out)
        return carry

    lax.fori_loop(0, 4, one_step, 0)


def last_kernel(phased, crossed, sums, theirs, mine, left):
    left_operand(phased, left)
    for out, half in ((theirs, 0), (mine, 1)):
        tails = []
        for part in range(2):
            step = 2 * half + part
            total = sums[step] + times(crossed[step], left)
            out[:, 512 * part : 512 * part + 512] = total[:512].T.astype(out.dtype)
            tails.append(total[512:])
        out[:, 1024:] = jnp.concatenate(tails, 0).T.astype(out.dtype)


def pack_kernel(mine, received, out, total):
    lane = lax.broadcasted_iota(jnp.int32, (8, SITES), 1)
    for tile in range(9):
        lanes = slice(SITES * tile, SITES * tile + SITES)
        total[tile] = mine[:, lanes] + received[:, lanes].astype(jnp.float32)
    for q in range(8):
        for zh in range(4):
            for half in range(2):
                out[4 * q + zh, 24 * half : 24 * half + 24, :] = total[
                    2 * zh + half, pl.ds(q, 24, 8), :
                ].astype(jnp.bfloat16)
        tail = total[8, pl.ds(q, 24, 8), :]
        for zh in range(4):
            joined = jnp.zeros((8, SITES), jnp.float32)
            for g in range(3):
                moved = pltpu.roll(tail[8 * g : 8 * g + 8], (32 * (g - zh)) % SITES, 1)
                joined = jnp.where(lane // 32 == g, moved, joined)
            out[4 * q + zh, 48:56, :] = joined.astype(jnp.bfloat16)


def final_kernel(parts, out, rows):
    scale = 1.0 / math.sqrt(LX * LY * LZ)
    for t in range(8):
        total = parts[4 * t].astype(jnp.float32)
        for zh in range(1, 4):
            total += parts[4 * t + zh].astype(jnp.float32)
        total *= scale
        rows[0, pl.ds(t, 24, 8), :] = total[:24]
        rows[1, pl.ds(t, 24, 8), :] = total[24:48]
        for g in range(3):
            tail = total[48:56]
            if g:
                tail = pltpu.roll(tail, SITES - 32 * g, 1)
            rows[2, pl.ds(64 * g + t, 8, 8), :] = tail
    for ri in range(2):
        pieces = [[], [], []]
        for i in range(12):
            at = 8 * (12 * ri + i)
            one, two, three = (rows[part, at : at + 8, :] for part in range(3))
            pieces[0].append(one[:, :96])
            pieces[1].append(one[:, 96:])
            pieces[1].append(two[:, :64])
            pieces[2].append(two[:, 64:])
            pieces[2].append(three[:, :32])
        for r in range(3):
            out[r, :, ri, :] = jnp.concatenate(pieces[r], axis=1)


def vmem():
    return pl.BlockSpec(memory_space=pltpu.VMEM)


def smem():
    return pl.BlockSpec(memory_space=pltpu.SMEM)


def params(mib):
    return pltpu.CompilerParams(vmem_limit_bytes=mib << 20)


def from_y(block, by):
    return lax.ppermute(block, "y", [(i, (i + by) % 4) for i in range(4)])


def on_device(vectors, gauge_links, momentum, direction):
    f32 = jnp.float32
    bf16 = jnp.bfloat16
    swap = [(0, 1), (1, 0)]
    own = jnp.transpose(vectors[0], (1, 2, 0, 3)).reshape(6, NEV, SITES)
    joined = jnp.concatenate(
        [
            own.reshape(6 * NEV, SITES),
            jnp.transpose(gauge_links[0], (0, 2, 3, 1, 4)).reshape(54, SITES),
            jnp.zeros((10, SITES), bf16),
        ]
    )
    other = lax.ppermute(joined, "c", swap)
    outer = lax.ppermute(joined, AXES, ring_pairs(outer_plane))
    before = from_y(own, 1)
    after = from_y(own, 3)
    phased = pl.pallas_call(
        phased_kernel,
        out_shape=jax.ShapeDtypeStruct((6, NEV, SITES), bf16),
        in_specs=[vmem()] * 4,
        out_specs=vmem(),
        scratch_shapes=[pltpu.VMEM((6, NEV, SITES), f32)] * 3,
        compiler_params=params(8),
    )(jnp.concatenate([momentum, direction]), joined, outer, other)
    phased_before = from_y(phased, 1)
    phased_after = from_y(phased, 3)
    phased_opposite = from_y(phased, 2)
    opposite = from_y(after, 3)
    before, after = lax.optimization_barrier((before, after))

    crossed_shape = jax.ShapeDtypeStruct((4, 576, DEPTH), bf16)
    sums_shape = jax.ShapeDtypeStruct((4, 576, 192), f32)
    spread_scratch = pltpu.VMEM((12, NEV, SITES), f32)
    left_scratch = pltpu.VMEM((192, DEPTH), bf16)
    short = pl.CostEstimate(flops=0, bytes_accessed=0, transcendentals=0)

    def both(source, phased_plane, previous, *sums):
        return pl.pallas_call(
            both_kernel,
            out_shape=(crossed_shape, sums_shape),
            in_specs=[vmem()] * (3 + len(sums)),
            out_specs=(vmem(), vmem()),
            scratch_shapes=[spread_scratch, left_scratch],
            compiler_params=params(6),
            cost_estimate=short,
        )(source, phased_plane, previous, *sums)

    crossed = pl.pallas_call(
        crossed_kernel,
        out_shape=crossed_shape,
        in_specs=[vmem()],
        out_specs=vmem(),
        scratch_shapes=[spread_scratch],
        compiler_params=params(4),
        cost_estimate=short,
    )(own)
    crossed, sums = both(before, phased, crossed)
    crossed, sums = both(after, phased_before, crossed, sums)
    crossed, sums = both(opposite, phased_after, crossed, sums)
    sent, mine = pl.pallas_call(
        last_kernel,
        out_shape=(
            jax.ShapeDtypeStruct((192, 1152), bf16),
            jax.ShapeDtypeStruct((192, 1152), f32),
        ),
        in_specs=[vmem()] * 3,
        out_specs=(vmem(), vmem()),
        scratch_shapes=[left_scratch],
        compiler_params=params(6),
    )(phased_opposite, crossed, sums)
    received = lax.ppermute(sent, "c", swap)
    packed = pl.pallas_call(
        pack_kernel,
        out_shape=jax.ShapeDtypeStruct((32, 56, SITES), bf16),
        in_specs=[vmem()] * 2,
        out_specs=vmem(),
        scratch_shapes=[pltpu.VMEM((9, 192, SITES), f32)],
        compiler_params=params(16),
    )(mine, received)
    packed = lax.all_to_all(packed, ("x", "zl", "zh"), 0, 0, tiled=True)
    return pl.pallas_call(
        final_kernel,
        out_shape=jax.ShapeDtypeStruct((3, 8, 2, 12 * NEV), f32),
        in_specs=[vmem()],
        out_specs=vmem(),
        scratch_shapes=[pltpu.VMEM((3, 192, SITES), f32)],
        compiler_params=params(16),
    )(packed)


def solution(mesh):
    cut = Mesh(mesh.devices.reshape(SIZES), AXES)
    return jax.shard_map(
        on_device,
        mesh=cut,
        in_specs=(
            P(("x", "zl"), None, None, None, ("y", "zh", "c")),
            P(("x", "zl"), None, None, None, None, ("y", "zh", "c")),
            P(),
            P(("x", "zl")),
        ),
        out_specs=P(("y", "zh", "c"), None, None, ("x", "zl")),
        check_vma=False,
    )
```

```python
import math

import jax
import jax.numpy as jnp
from jax import lax
from jax.experimental import pallas as pl
from jax.experimental.pallas import tpu as pltpu
from jax.sharding import Mesh
from jax.sharding import PartitionSpec as P

NEV = 96
LX = 16
LY = 8
LZ = 32
SITES = 128
AXES = ("x", "zl", "y", "zh", "c")
SIZES = (4, 2, 4, 4, 2)
DEPTH = 6 * SITES


def ring_pairs(target):
    pairs = []
    for x in range(4):
        for zl in range(2):
            for s in range(32):
                to = target(zl, s)
                if to is not None:
                    head = (x * 2 + zl) * 32
                    pairs.append((head + s, head + to))
    return pairs


def outer_plane(zl, s):
    if zl == 1:
        return None
    return (s + 1) % 32 if s % 2 == 1 else (s - 1) % 32


def phased_kernel(numbers, own, other, outer, out, field, ahead, behind):
    links = own[6 * NEV :, :].astype(jnp.float32)
    direction = jnp.bitwise_and(numbers[0], 3)
    momentum = [lax.shift_right_arithmetic(numbers[d], 2) for d in range(3)]
    core = lax.axis_index("c")
    plane = (lax.axis_index("y") * 4 + lax.axis_index("zh")) * 2 + core
    lane = lax.broadcasted_iota(jnp.int32, (1, SITES), 1)
    x_coord = lane % LX
    y_coord = lane // LX
    turns = (
        2 * jnp.bitwise_and(momentum[0] * x_coord, LX - 1)
        + 4 * jnp.bitwise_and(momentum[1] * y_coord, LY - 1)
        + jnp.bitwise_and(momentum[2] * plane, LZ - 1)
    )
    angle = (2.0 * math.pi / LZ) * jnp.bitwise_and(turns, LZ - 1).astype(jnp.float32)
    cos_part = jnp.cos(angle)
    sin_part = -jnp.sin(angle)

    @pl.when(direction == 2)
    def _():
        for comp in range(6):
            near = other[NEV * comp : NEV * comp + NEV, :].astype(jnp.float32)
            far = outer[NEV * comp : NEV * comp + NEV, :].astype(jnp.float32)
            ahead[comp] = jnp.where(core == 0, near, far)
            behind[comp] = jnp.where(core == 0, far, near)

    @pl.when(direction != 2)
    def _():
        step = jnp.where(direction == 0, 1, LX)
        last = jnp.logical_and(x_coord == LX - 1, direction == 0)
        first = jnp.logical_and(x_coord == 0, direction == 0)
        for comp in range(6):
            here = own[NEV * comp : NEV * comp + NEV, :].astype(jnp.float32)
            ahead[comp] = jnp.where(
                last, pltpu.roll(here, LX - 1, 1), pltpu.roll(here, SITES - step, 1)
            )
            behind[comp] = jnp.where(
                first, pltpu.roll(here, SITES - LX + 1, 1), pltpu.roll(here, step, 1)
            )

    z_back = jnp.where(
        core == 0,
        outer[6 * NEV :, :].astype(jnp.float32),
        other[6 * NEV :, :].astype(jnp.float32),
    )
    x_roll = jnp.where(
        x_coord == 0, pltpu.roll(links, SITES - LX + 1, 1), pltpu.roll(links, 1, 1)
    )
    y_roll = pltpu.roll(links, LX, 1)

    def matrix(table, part, row, column):
        return table[6 * row + 2 * column + part]

    here_link = []
    back_link = []
    for at in range(18):
        x_at, y_at, z_at = (slice(at + 18 * d, at + 18 * d + 1) for d in range(3))
        here_link.append(
            jnp.where(
                direction == 0, links[x_at], jnp.where(direction == 1, links[y_at], links[z_at])
            )
        )
        back_link.append(
            jnp.where(
                direction == 0,
                x_roll[x_at],
                jnp.where(direction == 1, y_roll[y_at], z_back[z_at]),
            )
        )

    for a in range(3):
        front_re = front_im = rear_re = rear_im = 0.0
        for b in range(3):
            u_re, u_im = matrix(here_link, 0, a, b), matrix(here_link, 1, a, b)
            v_re, v_im = ahead[b], ahead[3 + b]
            front_re += u_re * v_re - u_im * v_im
            front_im += u_re * v_im + u_im * v_re
            w_re, w_im = matrix(back_link, 0, b, a), matrix(back_link, 1, b, a)
            v_re, v_im = behind[b], behind[3 + b]
            rear_re += w_re * v_re + w_im * v_im
            rear_im += w_re * v_im - w_im * v_re
        moved_re = front_re - rear_re
        moved_im = front_im - rear_im
        field[a] = cos_part * moved_re - sin_part * moved_im
        field[3 + a] = cos_part * moved_im + sin_part * moved_re

    for comp in range(6):
        for rows in range(6):
            both = [field[comp, pl.ds(2 * rows + k, 8, 12), :] for k in range(2)]
            out[comp, 16 * rows : 16 * rows + 16, :] = jnp.concatenate(both, 0).astype(
                jnp.bfloat16
            )


def left_operand(phased, left):
    for a in range(3):
        real = phased[a]
        imag = phased[3 + a]
        column = a * SITES
        left[:NEV, column : column + SITES] = real
        left[NEV:, column : column + SITES] = imag
        column += 3 * SITES
        left[:NEV, column : column + SITES] = -imag
        left[NEV:, column : column + SITES] = real


def times(crossed, left):
    return lax.dot_general(
        crossed, left[...], (((1,), (1,)), ((), ())), preferred_element_type=jnp.float32
    )


def six_rows(step, vectors, out):
    core = lax.axis_index("c")
    keeper = jnp.where(step < 2, 1 - core, core)
    first = 24 * lax.axis_index("y") + 12 * (step % 2) + 3 * keeper
    for high in range(2):
        for low in range(3):
            mine = [vectors[comp, pl.ds(first + 6 * high + low, 1), :] for comp in range(9)]
            mine = [jnp.broadcast_to(m, (16, SITES)) for m in mine]
            my_re, my_im, my_sum = mine[:3], mine[3:6], mine[6:]
            for chunk in range(6):
                rows = slice(16 * chunk, 16 * chunk + 16)
                re, total, gap = (
                    [vectors[comp + colour, rows, :] for colour in range(3)]
                    for comp in (0, 6, 9)
                )
                at = 96 * low + 16 * chunk
                at = 256 * high + at if at < 256 else 256 + 32 * high + at
                for a in range(3):
                    b = (a + 1) % 3
                    c = (a + 2) % 3
                    shared = my_sum[b] * re[c] - my_sum[c] * re[b]
                    real = shared - (my_im[b] * total[c] - my_im[c] * total[b])
                    imag = shared + (my_re[b] * gap[c] - my_re[c] * gap[b])
                    column = a * SITES
                    out[step, at : at + 16, column : column + SITES] = real.astype(
                        jnp.bfloat16
                    )
                    column += 3 * SITES
                    out[step, at : at + 16, column : column + SITES] = imag.astype(
                        jnp.bfloat16
                    )


def spread(source, vectors):
    for colour in range(3):
        real = source[colour].astype(jnp.float32)
        imag = source[3 + colour].astype(jnp.float32)
        vectors[colour] = real
        vectors[3 + colour] = imag
        vectors[6 + colour] = real + imag
        vectors[9 + colour] = imag - real


def crossed_kernel(source, out, vectors):
    spread(source, vectors)

    def one_step(step, carry):
        six_rows(step, vectors, out)
        return carry

    lax.fori_loop(0, 4, one_step, 0)


def both_kernel(source, phased, previous, *rest):
    sums = rest[0] if len(rest) == 5 else None
    out, total, vectors, left = rest[-4:]
    spread(source, vectors)
    left_operand(phased, left)

    def one_step(step, carry):
        term = times(previous[step], left)
        total[step] = term if sums is None else sums[step] + term
        six_rows(step, vectors, out)
        return carry

    lax.fori_loop(0, 4, one_step, 0)


def last_kernel(phased, crossed, sums, theirs, mine, left):
    left_operand(phased, left)
    for out, half in ((theirs, 0), (mine, 1)):
        tails = []
        for part in range(2):
            step = 2 * half + part
            total = sums[step] + times(crossed[step], left)
            out[:, 512 * part : 512 * part + 512] = total[:512].T.astype(out.dtype)
            tails.append(total[512:])
        out[:, 1024:] = jnp.concatenate(tails, 0).T.astype(out.dtype)


def pack_kernel(mine, received, out, total):
    lane = lax.broadcasted_iota(jnp.int32, (8, SITES), 1)
    for tile in range(9):
        lanes = slice(SITES * tile, SITES * tile + SITES)
        total[tile] = mine[:, lanes] + received[:, lanes].astype(jnp.float32)
    for q in range(8):
        for zh in range(4):
            for half in range(2):
                out[4 * q + zh, 24 * half : 24 * half + 24, :] = total[
                    2 * zh + half, pl.ds(q, 24, 8), :
                ].astype(jnp.bfloat16)
        tail = total[8, pl.ds(q, 24, 8), :]
        for zh in range(4):
            joined = jnp.zeros((8, SITES), jnp.float32)
            for g in range(3):
                moved = pltpu.roll(tail[8 * g : 8 * g + 8], (32 * (g - zh)) % SITES, 1)
                joined = jnp.where(lane // 32 == g, moved, joined)
            out[4 * q + zh, 48:56, :] = joined.astype(jnp.bfloat16)


def final_kernel(parts, out, rows):
    scale = 1.0 / math.sqrt(LX * LY * LZ)
    for t in range(8):
        total = parts[4 * t].astype(jnp.float32)
        for zh in range(1, 4):
            total += parts[4 * t + zh].astype(jnp.float32)
        total *= scale
        rows[0, pl.ds(t, 24, 8), :] = total[:24]
        rows[1, pl.ds(t, 24, 8), :] = total[24:48]
        for g in range(3):
            tail = total[48:56]
            if g:
                tail = pltpu.roll(tail, SITES - 32 * g, 1)
            rows[2, pl.ds(64 * g + t, 8, 8), :] = tail
    for ri in range(2):
        pieces = [[], [], []]
        for i in range(12):
            at = 8 * (12 * ri + i)
            one, two, three = (rows[part, at : at + 8, :] for part in range(3))
            pieces[0].append(one[:, :96])
            pieces[1].append(one[:, 96:])
            pieces[1].append(two[:, :64])
            pieces[2].append(two[:, 64:])
            pieces[2].append(three[:, :32])
        for r in range(3):
            out[r, :, ri, :] = jnp.concatenate(pieces[r], axis=1)


def vmem():
    return pl.BlockSpec(memory_space=pltpu.VMEM)


def smem():
    return pl.BlockSpec(memory_space=pltpu.SMEM)


def params(mib):
    return pltpu.CompilerParams(vmem_limit_bytes=mib << 20)


def from_y(block, by):
    return lax.ppermute(block, "y", [(i, (i + by) % 4) for i in range(4)])


def on_device(vectors, gauge_links, momentum, direction):
    f32 = jnp.float32
    bf16 = jnp.bfloat16
    swap = [(0, 1), (1, 0)]
    own = jnp.transpose(vectors[0], (1, 2, 0, 3)).reshape(6, NEV, SITES)
    joined = jnp.concatenate(
        [
            own.reshape(6 * NEV, SITES),
            jnp.transpose(gauge_links[0], (0, 2, 3, 1, 4)).reshape(54, SITES),
            jnp.zeros((10, SITES), bf16),
        ]
    )
    outer = lax.ppermute(joined, AXES, ring_pairs(outer_plane))
    other = lax.ppermute(joined, "c", swap)
    before = from_y(own, 1)
    after = from_y(own, 3)
    opposite = from_y(own, 2)
    phased = pl.pallas_call(
        phased_kernel,
        out_shape=jax.ShapeDtypeStruct((6, NEV, SITES), bf16),
        in_specs=[vmem()] * 4,
        out_specs=vmem(),
        scratch_shapes=[pltpu.VMEM((6, NEV, SITES), f32)] * 3,
        compiler_params=params(8),
    )(4 * momentum + direction, joined, other, outer)
    phased_before = from_y(phased, 1)
    phased_after = from_y(phased, 3)
    phased_opposite = from_y(phased, 2)
    before, after, opposite = lax.optimization_barrier((before, after, opposite))

    crossed_shape = jax.ShapeDtypeStruct((4, 576, DEPTH), bf16)
    sums_shape = jax.ShapeDtypeStruct((4, 576, 192), f32)
    spread_scratch = pltpu.VMEM((12, NEV, SITES), f32)
    left_scratch = pltpu.VMEM((192, DEPTH), bf16)
    short = pl.CostEstimate(flops=0, bytes_accessed=0, transcendentals=0)

    def both(source, phased_plane, previous, *sums):
        return pl.pallas_call(
            both_kernel,
            out_shape=(crossed_shape, sums_shape),
            in_specs=[vmem()] * (3 + len(sums)),
            out_specs=(vmem(), vmem()),
            scratch_shapes=[spread_scratch, left_scratch],
            compiler_params=params(6),
            cost_estimate=short,
        )(source, phased_plane, previous, *sums)

    crossed = pl.pallas_call(
        crossed_kernel,
        out_shape=crossed_shape,
        in_specs=[vmem()],
        out_specs=vmem(),
        scratch_shapes=[spread_scratch],
        compiler_params=params(4),
        cost_estimate=short,
    )(own)
    crossed, sums = both(before, phased, crossed)
    crossed, sums = both(after, phased_before, crossed, sums)
    crossed, sums = both(opposite, phased_after, crossed, sums)
    sent, mine = pl.pallas_call(
        last_kernel,
        out_shape=(
            jax.ShapeDtypeStruct((192, 1152), bf16),
            jax.ShapeDtypeStruct((192, 1152), f32),
        ),
        in_specs=[vmem()] * 3,
        out_specs=(vmem(), vmem()),
        scratch_shapes=[left_scratch],
        compiler_params=params(6),
    )(phased_opposite, crossed, sums)
    received = lax.ppermute(sent, "c", swap)
    packed = pl.pallas_call(
        pack_kernel,
        out_shape=jax.ShapeDtypeStruct((32, 56, SITES), bf16),
        in_specs=[vmem()] * 2,
        out_specs=vmem(),
        scratch_shapes=[pltpu.VMEM((9, 192, SITES), f32)],
        compiler_params=params(16),
    )(mine, received)
    packed = lax.all_to_all(packed, ("x", "zl", "zh"), 0, 0, tiled=True)
    return pl.pallas_call(
        final_kernel,
        out_shape=jax.ShapeDtypeStruct((3, 8, 2, 12 * NEV), f32),
        in_specs=[vmem()],
        out_specs=vmem(),
        scratch_shapes=[pltpu.VMEM((3, 192, SITES), f32)],
        compiler_params=params(16),
    )(packed)


def solution(mesh):
    cut = Mesh(mesh.devices.reshape(SIZES), AXES)
    return jax.shard_map(
        on_device,
        mesh=cut,
        in_specs=(
            P(("x", "zl"), None, None, None, ("y", "zh", "c")),
            P(("x", "zl"), None, None, None, None, ("y", "zh", "c")),
            P(),
            P(("x", "zl")),
        ),
        out_specs=P(("y", "zh", "c"), None, None, ("x", "zl")),
        check_vma=False,
    )
```

```python
import math

import jax
import jax.numpy as jnp
from jax import lax
from jax.experimental import pallas as pl
from jax.experimental.pallas import tpu as pltpu
from jax.sharding import Mesh
from jax.sharding import PartitionSpec as P

NEV = 96
LX = 16
LY = 8
LZ = 32
SITES = 128
AXES = ("x", "zl", "y", "zh", "c")
SIZES = (4, 2, 4, 4, 2)
DEPTH = 6 * SITES


def ring_pairs(target):
    pairs = []
    for x in range(4):
        for zl in range(2):
            for s in range(32):
                to = target(zl, s)
                if to is not None:
                    head = (x * 2 + zl) * 32
                    pairs.append((head + s, head + to))
    return pairs


def outer_plane(zl, s):
    if zl == 1:
        return None
    return (s + 1) % 32 if s % 2 == 1 else (s - 1) % 32


def phased_kernel(numbers, own, other, outer, out, field, ahead, behind):
    links = own[6 * NEV :, :].astype(jnp.float32)
    direction = numbers[3]
    core = lax.axis_index("c")
    plane = (lax.axis_index("y") * 4 + lax.axis_index("zh")) * 2 + core
    lane = lax.broadcasted_iota(jnp.int32, (1, SITES), 1)
    x_coord = lane % LX
    y_coord = lane // LX
    turns = (
        2 * jnp.bitwise_and(numbers[0] * x_coord, LX - 1)
        + 4 * jnp.bitwise_and(numbers[1] * y_coord, LY - 1)
        + jnp.bitwise_and(numbers[2] * plane, LZ - 1)
    )
    angle = (2.0 * math.pi / LZ) * jnp.bitwise_and(turns, LZ - 1).astype(jnp.float32)
    cos_part = jnp.cos(angle)
    sin_part = -jnp.sin(angle)

    @pl.when(direction == 2)
    def _():
        for comp in range(6):
            near = other[NEV * comp : NEV * comp + NEV, :].astype(jnp.float32)
            far = outer[NEV * comp : NEV * comp + NEV, :].astype(jnp.float32)
            ahead[comp] = jnp.where(core == 0, near, far)
            behind[comp] = jnp.where(core == 0, far, near)

    @pl.when(direction != 2)
    def _():
        step = jnp.where(direction == 0, 1, LX)
        last = jnp.logical_and(x_coord == LX - 1, direction == 0)
        first = jnp.logical_and(x_coord == 0, direction == 0)
        for comp in range(6):
            here = own[NEV * comp : NEV * comp + NEV, :].astype(jnp.float32)
            ahead[comp] = jnp.where(
                last, pltpu.roll(here, LX - 1, 1), pltpu.roll(here, SITES - step, 1)
            )
            behind[comp] = jnp.where(
                first, pltpu.roll(here, SITES - LX + 1, 1), pltpu.roll(here, step, 1)
            )

    z_back = jnp.where(
        core == 0,
        outer[6 * NEV :, :].astype(jnp.float32),
        other[6 * NEV :, :].astype(jnp.float32),
    )
    x_roll = jnp.where(
        x_coord == 0, pltpu.roll(links, SITES - LX + 1, 1), pltpu.roll(links, 1, 1)
    )
    y_roll = pltpu.roll(links, LX, 1)

    def matrix(table, part, row, column):
        return table[6 * row + 2 * column + part]

    here_link = []
    back_link = []
    for at in range(18):
        x_at, y_at, z_at = (slice(at + 18 * d, at + 18 * d + 1) for d in range(3))
        here_link.append(
            jnp.where(
                direction == 0, links[x_at], jnp.where(direction == 1, links[y_at], links[z_at])
            )
        )
        back_link.append(
            jnp.where(
                direction == 0,
                x_roll[x_at],
                jnp.where(direction == 1, y_roll[y_at], z_back[z_at]),
            )
        )

    for a in range(3):
        front_re = front_im = rear_re = rear_im = 0.0
        for b in range(3):
            u_re, u_im = matrix(here_link, 0, a, b), matrix(here_link, 1, a, b)
            v_re, v_im = ahead[b], ahead[3 + b]
            front_re += u_re * v_re - u_im * v_im
            front_im += u_re * v_im + u_im * v_re
            w_re, w_im = matrix(back_link, 0, b, a), matrix(back_link, 1, b, a)
            v_re, v_im = behind[b], behind[3 + b]
            rear_re += w_re * v_re + w_im * v_im
            rear_im += w_re * v_im - w_im * v_re
        moved_re = front_re - rear_re
        moved_im = front_im - rear_im
        field[a] = cos_part * moved_re - sin_part * moved_im
        field[3 + a] = cos_part * moved_im + sin_part * moved_re

    for comp in range(6):
        for rows in range(6):
            both = [field[comp, pl.ds(2 * rows + k, 8, 12), :] for k in range(2)]
            out[comp, 16 * rows : 16 * rows + 16, :] = jnp.concatenate(both, 0).astype(
                jnp.bfloat16
            )


def left_operand(phased, left):
    for a in range(3):
        real = phased[a]
        imag = phased[3 + a]
        column = a * SITES
        left[:NEV, column : column + SITES] = real
        left[NEV:, column : column + SITES] = imag
        column += 3 * SITES
        left[:NEV, column : column + SITES] = -imag
        left[NEV:, column : column + SITES] = real


def times(crossed, left):
    return lax.dot_general(
        crossed, left[...], (((1,), (1,)), ((), ())), preferred_element_type=jnp.float32
    )


def six_rows(step, vectors, out):
    core = lax.axis_index("c")
    keeper = jnp.where(step < 2, 1 - core, core)
    first = 24 * lax.axis_index("y") + 12 * (step % 2) + 3 * keeper
    for high in range(2):
        for low in range(3):
            mine = [vectors[comp, pl.ds(first + 6 * high + low, 1), :] for comp in range(9)]
            mine = [jnp.broadcast_to(m, (16, SITES)) for m in mine]
            my_re, my_im, my_sum = mine[:3], mine[3:6], mine[6:]
            for chunk in range(6):
                rows = slice(16 * chunk, 16 * chunk + 16)
                re, total, gap = (
                    [vectors[comp + colour, rows, :] for colour in range(3)]
                    for comp in (0, 6, 9)
                )
                at = 96 * low + 16 * chunk
                at = 256 * high + at if at < 256 else 256 + 32 * high + at
                for a in range(3):
                    b = (a + 1) % 3
                    c = (a + 2) % 3
                    shared = my_sum[b] * re[c] - my_sum[c] * re[b]
                    real = shared - (my_im[b] * total[c] - my_im[c] * total[b])
                    imag = shared + (my_re[b] * gap[c] - my_re[c] * gap[b])
                    column = a * SITES
                    out[step, at : at + 16, column : column + SITES] = real.astype(
                        jnp.bfloat16
                    )
                    column += 3 * SITES
                    out[step, at : at + 16, column : column + SITES] = imag.astype(
                        jnp.bfloat16
                    )


def spread(source, vectors):
    for colour in range(3):
        real = source[colour].astype(jnp.float32)
        imag = source[3 + colour].astype(jnp.float32)
        vectors[colour] = real
        vectors[3 + colour] = imag
        vectors[6 + colour] = real + imag
        vectors[9 + colour] = imag - real


def crossed_kernel(source, out, vectors):
    spread(source, vectors)

    def one_step(step, carry):
        six_rows(step, vectors, out)
        return carry

    lax.fori_loop(0, 4, one_step, 0)


def both_kernel(source, phased, previous, *rest):
    sums = rest[0] if len(rest) == 5 else None
    out, total, vectors, left = rest[-4:]
    spread(source, vectors)
    left_operand(phased, left)

    def one_step(step, carry):
        term = times(previous[step], left)
        total[step] = term if sums is None else sums[step] + term
        six_rows(step, vectors, out)
        return carry

    lax.fori_loop(0, 4, one_step, 0)


def last_kernel(phased, crossed, sums, theirs, mine, left):
    left_operand(phased, left)
    for out, half in ((theirs, 0), (mine, 1)):
        tails = []
        for part in range(2):
            step = 2 * half + part
            total = sums[step] + times(crossed[step], left)
            out[:, 512 * part : 512 * part + 512] = total[:512].T.astype(out.dtype)
            tails.append(total[512:])
        out[:, 1024:] = jnp.concatenate(tails, 0).T.astype(out.dtype)


def pack_kernel(mine, received, out, total):
    lane = lax.broadcasted_iota(jnp.int32, (8, SITES), 1)
    for tile in range(9):
        lanes = slice(SITES * tile, SITES * tile + SITES)
        total[tile] = mine[:, lanes] + received[:, lanes].astype(jnp.float32)
    for q in range(8):
        for zh in range(4):
            for half in range(2):
                out[8 * zh + 4 * (q % 2) + q // 2, 24 * half : 24 * half + 24, :] = total[
                    2 * zh + half, pl.ds(q, 24, 8), :
                ].astype(jnp.bfloat16)
        tail = total[8, pl.ds(q, 24, 8), :]
        for zh in range(4):
            joined = jnp.zeros((8, SITES), jnp.float32)
            for g in range(3):
                moved = pltpu.roll(tail[8 * g : 8 * g + 8], (32 * (g - zh)) % SITES, 1)
                joined = jnp.where(lane // 32 == g, moved, joined)
            out[8 * zh + 4 * (q % 2) + q // 2, 48:56, :] = joined.astype(jnp.bfloat16)


def final_kernel(parts, out, rows):
    scale = 1.0 / math.sqrt(LX * LY * LZ)
    for t in range(8):
        here = 4 * (t % 2) + t // 2
        total = parts[here].astype(jnp.float32)
        for zh in range(1, 4):
            total += parts[8 * zh + here].astype(jnp.float32)
        total *= scale
        rows[0, pl.ds(t, 24, 8), :] = total[:24]
        rows[1, pl.ds(t, 24, 8), :] = total[24:48]
        for g in range(3):
            tail = total[48:56]
            if g:
                tail = pltpu.roll(tail, SITES - 32 * g, 1)
            rows[2, pl.ds(64 * g + t, 8, 8), :] = tail
    for ri in range(2):
        pieces = [[], [], []]
        for i in range(12):
            at = 8 * (12 * ri + i)
            one, two, three = (rows[part, at : at + 8, :] for part in range(3))
            pieces[0].append(one[:, :96])
            pieces[1].append(one[:, 96:])
            pieces[1].append(two[:, :64])
            pieces[2].append(two[:, 64:])
            pieces[2].append(three[:, :32])
        for r in range(3):
            out[r, :, ri, :] = jnp.concatenate(pieces[r], axis=1)


def vmem():
    return pl.BlockSpec(memory_space=pltpu.VMEM)


def smem():
    return pl.BlockSpec(memory_space=pltpu.SMEM)


def params(mib):
    return pltpu.CompilerParams(vmem_limit_bytes=mib << 20)


def from_y(block, by):
    return lax.ppermute(block, "y", [(i, (i + by) % 4) for i in range(4)])


def on_device(vectors, gauge_links, momentum, direction):
    f32 = jnp.float32
    bf16 = jnp.bfloat16
    swap = [(0, 1), (1, 0)]
    own = jnp.transpose(vectors[0], (1, 2, 0, 3)).reshape(6, NEV, SITES)
    joined = jnp.concatenate(
        [
            own.reshape(6 * NEV, SITES),
            jnp.transpose(gauge_links[0], (0, 2, 3, 1, 4)).reshape(54, SITES),
            jnp.zeros((10, SITES), bf16),
        ]
    )
    outer = lax.ppermute(joined, AXES, ring_pairs(outer_plane))
    other = lax.ppermute(joined, "c", swap)
    before = from_y(own, 1)
    after = from_y(own, 3)
    opposite = from_y(own, 2)
    phased = pl.pallas_call(
        phased_kernel,
        out_shape=jax.ShapeDtypeStruct((6, NEV, SITES), bf16),
        in_specs=[vmem()] * 4,
        out_specs=vmem(),
        scratch_shapes=[pltpu.VMEM((6, NEV, SITES), f32)] * 3,
        compiler_params=params(8),
    )(jnp.concatenate([momentum, direction]), joined, other, outer)
    phased_before = from_y(phased, 1)
    phased_after = from_y(phased, 3)
    phased_opposite = from_y(phased, 2)
    before, after, opposite = lax.optimization_barrier((before, after, opposite))

    crossed_shape = jax.ShapeDtypeStruct((4, 576, DEPTH), bf16)
    sums_shape = jax.ShapeDtypeStruct((4, 576, 192), f32)
    spread_scratch = pltpu.VMEM((12, NEV, SITES), f32)
    left_scratch = pltpu.VMEM((192, DEPTH), bf16)
    short = pl.CostEstimate(flops=0, bytes_accessed=0, transcendentals=0)

    def both(source, phased_plane, previous, *sums):
        return pl.pallas_call(
            both_kernel,
            out_shape=(crossed_shape, sums_shape),
            in_specs=[vmem()] * (3 + len(sums)),
            out_specs=(vmem(), vmem()),
            scratch_shapes=[spread_scratch, left_scratch],
            compiler_params=params(6),
            cost_estimate=short,
        )(source, phased_plane, previous, *sums)

    crossed = pl.pallas_call(
        crossed_kernel,
        out_shape=crossed_shape,
        in_specs=[vmem()],
        out_specs=vmem(),
        scratch_shapes=[spread_scratch],
        compiler_params=params(4),
        cost_estimate=short,
    )(own)
    crossed, sums = both(before, phased, crossed)
    crossed, sums = both(after, phased_before, crossed, sums)
    crossed, sums = both(opposite, phased_after, crossed, sums)
    sent, mine = pl.pallas_call(
        last_kernel,
        out_shape=(
            jax.ShapeDtypeStruct((192, 1152), bf16),
            jax.ShapeDtypeStruct((192, 1152), f32),
        ),
        in_specs=[vmem()] * 3,
        out_specs=(vmem(), vmem()),
        scratch_shapes=[left_scratch],
        compiler_params=params(6),
    )(phased_opposite, crossed, sums)
    received = lax.ppermute(sent, "c", swap)
    packed = pl.pallas_call(
        pack_kernel,
        out_shape=jax.ShapeDtypeStruct((32, 56, SITES), bf16),
        in_specs=[vmem()] * 2,
        out_specs=vmem(),
        scratch_shapes=[pltpu.VMEM((9, 192, SITES), f32)],
        compiler_params=params(16),
    )(mine, received)
    packed = lax.all_to_all(packed, ("zh", "zl", "x"), 0, 0, tiled=True)
    return pl.pallas_call(
        final_kernel,
        out_shape=jax.ShapeDtypeStruct((3, 8, 2, 12 * NEV), f32),
        in_specs=[vmem()],
        out_specs=vmem(),
        scratch_shapes=[pltpu.VMEM((3, 192, SITES), f32)],
        compiler_params=params(16),
    )(packed)


def solution(mesh):
    cut = Mesh(mesh.devices.reshape(SIZES), AXES)
    return jax.shard_map(
        on_device,
        mesh=cut,
        in_specs=(
            P(("x", "zl"), None, None, None, ("y", "zh", "c")),
            P(("x", "zl"), None, None, None, None, ("y", "zh", "c")),
            P(),
            P(("x", "zl")),
        ),
        out_specs=P(("y", "zh", "c"), None, None, ("x", "zl")),
        check_vma=False,
    )
```

```python
import math

import jax
import jax.numpy as jnp
from jax import lax
from jax.experimental import pallas as pl
from jax.experimental.pallas import tpu as pltpu
from jax.sharding import Mesh
from jax.sharding import PartitionSpec as P

NEV = 96
LX = 16
LY = 8
LZ = 32
SITES = 128
AXES = ("x", "zl", "y", "zh", "c")
SIZES = (4, 2, 4, 4, 2)
DEPTH = 6 * SITES


def ring_pairs(target):
    pairs = []
    for x in range(4):
        for zl in range(2):
            for s in range(32):
                to = target(zl, s)
                if to is not None:
                    head = (x * 2 + zl) * 32
                    pairs.append((head + s, head + to))
    return pairs


def outer_plane(zl, s):
    if zl == 1:
        return None
    return (s + 1) % 32 if s % 2 == 1 else (s - 1) % 32


def phased_kernel(numbers, own, other, outer, out, field, ahead, behind):
    links = own[6 * NEV :, :].astype(jnp.float32)
    direction = numbers[3]
    core = lax.axis_index("c")
    plane = (lax.axis_index("y") * 4 + lax.axis_index("zh")) * 2 + core
    lane = lax.broadcasted_iota(jnp.int32, (1, SITES), 1)
    x_coord = lane % LX
    y_coord = lane // LX
    turns = (
        2 * jnp.bitwise_and(numbers[0] * x_coord, LX - 1)
        + 4 * jnp.bitwise_and(numbers[1] * y_coord, LY - 1)
        + jnp.bitwise_and(numbers[2] * plane, LZ - 1)
    )
    angle = (2.0 * math.pi / LZ) * jnp.bitwise_and(turns, LZ - 1).astype(jnp.float32)
    cos_part = jnp.cos(angle)
    sin_part = -jnp.sin(angle)

    @pl.when(direction == 2)
    def _():
        for comp in range(6):
            near = other[NEV * comp : NEV * comp + NEV, :].astype(jnp.float32)
            far = outer[NEV * comp : NEV * comp + NEV, :].astype(jnp.float32)
            ahead[comp] = jnp.where(core == 0, near, far)
            behind[comp] = jnp.where(core == 0, far, near)

    @pl.when(direction != 2)
    def _():
        step = jnp.where(direction == 0, 1, LX)
        last = jnp.logical_and(x_coord == LX - 1, direction == 0)
        first = jnp.logical_and(x_coord == 0, direction == 0)
        for comp in range(6):
            here = own[NEV * comp : NEV * comp + NEV, :].astype(jnp.float32)
            ahead[comp] = jnp.where(
                last, pltpu.roll(here, LX - 1, 1), pltpu.roll(here, SITES - step, 1)
            )
            behind[comp] = jnp.where(
                first, pltpu.roll(here, SITES - LX + 1, 1), pltpu.roll(here, step, 1)
            )

    z_back = jnp.where(
        core == 0,
        outer[6 * NEV :, :].astype(jnp.float32),
        other[6 * NEV :, :].astype(jnp.float32),
    )
    x_roll = jnp.where(
        x_coord == 0, pltpu.roll(links, SITES - LX + 1, 1), pltpu.roll(links, 1, 1)
    )
    y_roll = pltpu.roll(links, LX, 1)

    def matrix(table, part, row, column):
        return table[6 * row + 2 * column + part]

    here_link = []
    back_link = []
    for at in range(18):
        x_at, y_at, z_at = (slice(at + 18 * d, at + 18 * d + 1) for d in range(3))
        here_link.append(
            jnp.where(
                direction == 0, links[x_at], jnp.where(direction == 1, links[y_at], links[z_at])
            )
        )
        back_link.append(
            jnp.where(
                direction == 0,
                x_roll[x_at],
                jnp.where(direction == 1, y_roll[y_at], z_back[z_at]),
            )
        )

    for a in range(3):
        front_re = front_im = rear_re = rear_im = 0.0
        for b in range(3):
            u_re, u_im = matrix(here_link, 0, a, b), matrix(here_link, 1, a, b)
            v_re, v_im = ahead[b], ahead[3 + b]
            front_re += u_re * v_re - u_im * v_im
            front_im += u_re * v_im + u_im * v_re
            w_re, w_im = matrix(back_link, 0, b, a), matrix(back_link, 1, b, a)
            v_re, v_im = behind[b], behind[3 + b]
            rear_re += w_re * v_re + w_im * v_im
            rear_im += w_re * v_im - w_im * v_re
        moved_re = front_re - rear_re
        moved_im = front_im - rear_im
        field[a] = cos_part * moved_re - sin_part * moved_im
        field[3 + a] = cos_part * moved_im + sin_part * moved_re

    for comp in range(6):
        for rows in range(6):
            both = [field[comp, pl.ds(2 * rows + k, 8, 12), :] for k in range(2)]
            out[comp, 16 * rows : 16 * rows + 16, :] = jnp.concatenate(both, 0).astype(
                jnp.bfloat16
            )


def left_operand(phased, left):
    for a in range(3):
        real = phased[a]
        imag = phased[3 + a]
        column = a * SITES
        left[:NEV, column : column + SITES] = real
        left[NEV:, column : column + SITES] = imag
        column += 3 * SITES
        left[:NEV, column : column + SITES] = -imag
        left[NEV:, column : column + SITES] = real


def times(crossed, left):
    return lax.dot_general(
        crossed, left[...], (((1,), (1,)), ((), ())), preferred_element_type=jnp.float32
    )


def six_rows(step, vectors, out):
    core = lax.axis_index("c")
    keeper = jnp.where(step < 2, 1 - core, core)
    first = 24 * lax.axis_index("y") + 12 * (step % 2) + 3 * keeper
    for high in range(2):
        for low in range(3):
            mine = [vectors[comp, pl.ds(first + 6 * high + low, 1), :] for comp in range(9)]
            mine = [jnp.broadcast_to(m, (16, SITES)) for m in mine]
            my_re, my_im, my_sum = mine[:3], mine[3:6], mine[6:]
            for chunk in range(6):
                rows = slice(16 * chunk, 16 * chunk + 16)
                re, total, gap = (
                    [vectors[comp + colour, rows, :] for colour in range(3)]
                    for comp in (0, 6, 9)
                )
                at = 96 * low + 16 * chunk
                at = 256 * high + at if at < 256 else 256 + 32 * high + at
                for a in range(3):
                    b = (a + 1) % 3
                    c = (a + 2) % 3
                    shared = my_sum[b] * re[c] - my_sum[c] * re[b]
                    real = shared - (my_im[b] * total[c] - my_im[c] * total[b])
                    imag = shared + (my_re[b] * gap[c] - my_re[c] * gap[b])
                    column = a * SITES
                    out[step, at : at + 16, column : column + SITES] = real.astype(
                        jnp.bfloat16
                    )
                    column += 3 * SITES
                    out[step, at : at + 16, column : column + SITES] = imag.astype(
                        jnp.bfloat16
                    )


def spread(source, vectors):
    for colour in range(3):
        real = source[colour].astype(jnp.float32)
        imag = source[3 + colour].astype(jnp.float32)
        vectors[colour] = real
        vectors[3 + colour] = imag
        vectors[6 + colour] = real + imag
        vectors[9 + colour] = imag - real


def crossed_kernel(source, out, vectors):
    spread(source, vectors)

    def one_step(step, carry):
        six_rows(step, vectors, out)
        return carry

    lax.fori_loop(0, 4, one_step, 0)


def both_kernel(source, phased, previous, *rest):
    sums = rest[0] if len(rest) == 5 else None
    out, total, vectors, left = rest[-4:]
    spread(source, vectors)
    left_operand(phased, left)

    def one_step(step, carry):
        term = times(previous[step], left)
        total[step] = term if sums is None else sums[step] + term
        six_rows(step, vectors, out)
        return carry

    lax.fori_loop(0, 4, one_step, 0)


def last_kernel(phased, crossed, sums, theirs, mine, left):
    left_operand(phased, left)
    for out, half in ((theirs, 0), (mine, 1)):
        tails = []
        for part in range(2):
            step = 2 * half + part
            total = sums[step] + times(crossed[step], left)
            out[:, 512 * part : 512 * part + 512] = total[:512].T.astype(out.dtype)
            tails.append(total[512:])
        out[:, 1024:] = jnp.concatenate(tails, 0).T.astype(out.dtype)


def pack_kernel(mine, received, out, total):
    lane = lax.broadcasted_iota(jnp.int32, (8, SITES), 1)
    for tile in range(9):
        lanes = slice(SITES * tile, SITES * tile + SITES)
        total[tile] = mine[:, lanes] + received[:, lanes].astype(jnp.float32)
    for q in range(8):
        for zh in range(4):
            for half in range(2):
                out[8 * (q // 2) + 2 * zh + q % 2, 24 * half : 24 * half + 24, :] = total[
                    2 * zh + half, pl.ds(q, 24, 8), :
                ].astype(jnp.bfloat16)
        tail = total[8, pl.ds(q, 24, 8), :]
        for zh in range(4):
            joined = jnp.zeros((8, SITES), jnp.float32)
            for g in range(3):
                moved = pltpu.roll(tail[8 * g : 8 * g + 8], (32 * (g - zh)) % SITES, 1)
                joined = jnp.where(lane // 32 == g, moved, joined)
            out[8 * (q // 2) + 2 * zh + q % 2, 48:56, :] = joined.astype(jnp.bfloat16)


def final_kernel(parts, out, rows):
    scale = 1.0 / math.sqrt(LX * LY * LZ)
    for t in range(8):
        here = 8 * (t // 2) + t % 2
        total = parts[here].astype(jnp.float32)
        for zh in range(1, 4):
            total += parts[here + 2 * zh].astype(jnp.float32)
        total *= scale
        rows[0, pl.ds(t, 24, 8), :] = total[:24]
        rows[1, pl.ds(t, 24, 8), :] = total[24:48]
        for g in range(3):
            tail = total[48:56]
            if g:
                tail = pltpu.roll(tail, SITES - 32 * g, 1)
            rows[2, pl.ds(64 * g + t, 8, 8), :] = tail
    for ri in range(2):
        pieces = [[], [], []]
        for i in range(12):
            at = 8 * (12 * ri + i)
            one, two, three = (rows[part, at : at + 8, :] for part in range(3))
            pieces[0].append(one[:, :96])
            pieces[1].append(one[:, 96:])
            pieces[1].append(two[:, :64])
            pieces[2].append(two[:, 64:])
            pieces[2].append(three[:, :32])
        for r in range(3):
            out[r, :, ri, :] = jnp.concatenate(pieces[r], axis=1)


def vmem():
    return pl.BlockSpec(memory_space=pltpu.VMEM)


def smem():
    return pl.BlockSpec(memory_space=pltpu.SMEM)


def params(mib):
    return pltpu.CompilerParams(vmem_limit_bytes=mib << 20)


def from_y(block, by):
    return lax.ppermute(block, "y", [(i, (i + by) % 4) for i in range(4)])


def on_device(vectors, gauge_links, momentum, direction):
    f32 = jnp.float32
    bf16 = jnp.bfloat16
    swap = [(0, 1), (1, 0)]
    own = jnp.transpose(vectors[0], (1, 2, 0, 3)).reshape(6, NEV, SITES)
    joined = jnp.concatenate(
        [
            own.reshape(6 * NEV, SITES),
            jnp.transpose(gauge_links[0], (0, 2, 3, 1, 4)).reshape(54, SITES),
            jnp.zeros((10, SITES), bf16),
        ]
    )
    outer = lax.ppermute(joined, AXES, ring_pairs(outer_plane))
    other = lax.ppermute(joined, "c", swap)
    before = from_y(own, 1)
    after = from_y(own, 3)
    opposite = from_y(own, 2)
    phased = pl.pallas_call(
        phased_kernel,
        out_shape=jax.ShapeDtypeStruct((6, NEV, SITES), bf16),
        in_specs=[vmem()] * 4,
        out_specs=vmem(),
        scratch_shapes=[pltpu.VMEM((6, NEV, SITES), f32)] * 3,
        compiler_params=params(8),
    )(jnp.concatenate([momentum, direction]), joined, other, outer)
    phased_before = from_y(phased, 1)
    phased_after = from_y(phased, 3)
    phased_opposite = from_y(phased, 2)
    before, after, opposite = lax.optimization_barrier((before, after, opposite))

    crossed_shape = jax.ShapeDtypeStruct((4, 576, DEPTH), bf16)
    sums_shape = jax.ShapeDtypeStruct((4, 576, 192), f32)
    spread_scratch = pltpu.VMEM((12, NEV, SITES), f32)
    left_scratch = pltpu.VMEM((192, DEPTH), bf16)
    short = pl.CostEstimate(flops=0, bytes_accessed=0, transcendentals=0)

    def both(source, phased_plane, previous, *sums):
        return pl.pallas_call(
            both_kernel,
            out_shape=(crossed_shape, sums_shape),
            in_specs=[vmem()] * (3 + len(sums)),
            out_specs=(vmem(), vmem()),
            scratch_shapes=[spread_scratch, left_scratch],
            compiler_params=params(6),
            cost_estimate=short,
        )(source, phased_plane, previous, *sums)

    crossed = pl.pallas_call(
        crossed_kernel,
        out_shape=crossed_shape,
        in_specs=[vmem()],
        out_specs=vmem(),
        scratch_shapes=[spread_scratch],
        compiler_params=params(4),
        cost_estimate=short,
    )(own)
    crossed, sums = both(before, phased, crossed)
    crossed, sums = both(after, phased_before, crossed, sums)
    crossed, sums = both(opposite, phased_after, crossed, sums)
    sent, mine = pl.pallas_call(
        last_kernel,
        out_shape=(
            jax.ShapeDtypeStruct((192, 1152), bf16),
            jax.ShapeDtypeStruct((192, 1152), f32),
        ),
        in_specs=[vmem()] * 3,
        out_specs=(vmem(), vmem()),
        scratch_shapes=[left_scratch],
        compiler_params=params(6),
    )(phased_opposite, crossed, sums)
    received = lax.ppermute(sent, "c", swap)
    packed = pl.pallas_call(
        pack_kernel,
        out_shape=jax.ShapeDtypeStruct((32, 56, SITES), bf16),
        in_specs=[vmem()] * 2,
        out_specs=vmem(),
        scratch_shapes=[pltpu.VMEM((9, 192, SITES), f32)],
        compiler_params=params(16),
    )(mine, received)
    packed = lax.all_to_all(packed, ("x", "zh", "zl"), 0, 0, tiled=True)
    return pl.pallas_call(
        final_kernel,
        out_shape=jax.ShapeDtypeStruct((3, 8, 2, 12 * NEV), f32),
        in_specs=[vmem()],
        out_specs=vmem(),
        scratch_shapes=[pltpu.VMEM((3, 192, SITES), f32)],
        compiler_params=params(16),
    )(packed)


def solution(mesh):
    cut = Mesh(mesh.devices.reshape(SIZES), AXES)
    return jax.shard_map(
        on_device,
        mesh=cut,
        in_specs=(
            P(("x", "zl"), None, None, None, ("y", "zh", "c")),
            P(("x", "zl"), None, None, None, None, ("y", "zh", "c")),
            P(),
            P(("x", "zl")),
        ),
        out_specs=P(("y", "zh", "c"), None, None, ("x", "zl")),
        check_vma=False,
    )
```

```python
import functools
import math

import jax
import jax.numpy as jnp
from jax import lax
from jax.experimental import pallas as pl
from jax.experimental.pallas import tpu as pltpu
from jax.sharding import Mesh
from jax.sharding import PartitionSpec as P

NEV = 96
LX = 16
LY = 8
LZ = 32
SITES = 128
AXES = ("x", "zl", "y", "zh", "c")
SIZES = (4, 2, 4, 4, 2)
DEPTH = 6 * SITES


def ring_pairs(target):
    pairs = []
    for x in range(4):
        for zl in range(2):
            for s in range(32):
                to = target(zl, s)
                if to is not None:
                    head = (x * 2 + zl) * 32
                    pairs.append((head + s, head + to))
    return pairs


def outer_plane(zl, s):
    if zl == 1:
        return None
    return (s + 1) % 32 if s % 2 == 1 else (s - 1) % 32


def phased_kernel(numbers, own, other, outer, out, field, ahead, behind):
    links = own[6 * NEV :, :].astype(jnp.float32)
    direction = numbers[3]
    core = lax.axis_index("c")
    plane = (lax.axis_index("y") * 4 + lax.axis_index("zh")) * 2 + core
    lane = lax.broadcasted_iota(jnp.int32, (1, SITES), 1)
    x_coord = lane % LX
    y_coord = lane // LX
    turns = (
        2 * jnp.bitwise_and(numbers[0] * x_coord, LX - 1)
        + 4 * jnp.bitwise_and(numbers[1] * y_coord, LY - 1)
        + jnp.bitwise_and(numbers[2] * plane, LZ - 1)
    )
    angle = (2.0 * math.pi / LZ) * jnp.bitwise_and(turns, LZ - 1).astype(jnp.float32)
    cos_part = jnp.cos(angle)
    sin_part = -jnp.sin(angle)

    @pl.when(direction == 2)
    def _():
        for comp in range(6):
            near = other[NEV * comp : NEV * comp + NEV, :].astype(jnp.float32)
            far = outer[NEV * comp : NEV * comp + NEV, :].astype(jnp.float32)
            ahead[comp] = jnp.where(core == 0, near, far)
            behind[comp] = jnp.where(core == 0, far, near)

    @pl.when(direction != 2)
    def _():
        step = jnp.where(direction == 0, 1, LX)
        last = jnp.logical_and(x_coord == LX - 1, direction == 0)
        first = jnp.logical_and(x_coord == 0, direction == 0)
        for comp in range(6):
            here = own[NEV * comp : NEV * comp + NEV, :].astype(jnp.float32)
            ahead[comp] = jnp.where(
                last, pltpu.roll(here, LX - 1, 1), pltpu.roll(here, SITES - step, 1)
            )
            behind[comp] = jnp.where(
                first, pltpu.roll(here, SITES - LX + 1, 1), pltpu.roll(here, step, 1)
            )

    z_back = jnp.where(
        core == 0,
        outer[6 * NEV :, :].astype(jnp.float32),
        other[6 * NEV :, :].astype(jnp.float32),
    )
    x_roll = jnp.where(
        x_coord == 0, pltpu.roll(links, SITES - LX + 1, 1), pltpu.roll(links, 1, 1)
    )
    y_roll = pltpu.roll(links, LX, 1)

    def matrix(table, part, row, column):
        return table[6 * row + 2 * column + part]

    here_link = []
    back_link = []
    for at in range(18):
        x_at, y_at, z_at = (slice(at + 18 * d, at + 18 * d + 1) for d in range(3))
        here_link.append(
            jnp.where(
                direction == 0, links[x_at], jnp.where(direction == 1, links[y_at], links[z_at])
            )
        )
        back_link.append(
            jnp.where(
                direction == 0,
                x_roll[x_at],
                jnp.where(direction == 1, y_roll[y_at], z_back[z_at]),
            )
        )

    for a in range(3):
        front_re = front_im = rear_re = rear_im = 0.0
        for b in range(3):
            u_re, u_im = matrix(here_link, 0, a, b), matrix(here_link, 1, a, b)
            v_re, v_im = ahead[b], ahead[3 + b]
            front_re += u_re * v_re - u_im * v_im
            front_im += u_re * v_im + u_im * v_re
            w_re, w_im = matrix(back_link, 0, b, a), matrix(back_link, 1, b, a)
            v_re, v_im = behind[b], behind[3 + b]
            rear_re += w_re * v_re + w_im * v_im
            rear_im += w_re * v_im - w_im * v_re
        moved_re = front_re - rear_re
        moved_im = front_im - rear_im
        field[a] = cos_part * moved_re - sin_part * moved_im
        field[3 + a] = cos_part * moved_im + sin_part * moved_re

    for comp in range(6):
        for rows in range(6):
            both = [field[comp, pl.ds(2 * rows + k, 8, 12), :] for k in range(2)]
            out[comp, 16 * rows : 16 * rows + 16, :] = jnp.concatenate(both, 0).astype(
                jnp.bfloat16
            )


def left_operand(phased, left):
    for a in range(3):
        real = phased[a]
        imag = phased[3 + a]
        column = a * SITES
        left[:NEV, column : column + SITES] = real
        left[NEV:, column : column + SITES] = imag
        column += 3 * SITES
        left[:NEV, column : column + SITES] = -imag
        left[NEV:, column : column + SITES] = real


def times(crossed, left):
    return lax.dot_general(
        crossed, left[...], (((1,), (1,)), ((), ())), preferred_element_type=jnp.float32
    )


def six_rows(step, vectors, out, slot):
    core = lax.axis_index("c")
    keeper = jnp.where(step < 2, 1 - core, core)
    first = 24 * lax.axis_index("y") + 12 * (step % 2) + 3 * keeper
    for high in range(2):
        for low in range(3):
            mine = [vectors[comp, pl.ds(first + 6 * high + low, 1), :] for comp in range(9)]
            mine = [jnp.broadcast_to(m, (16, SITES)) for m in mine]
            my_re, my_im, my_sum = mine[:3], mine[3:6], mine[6:]
            for chunk in range(6):
                rows = slice(16 * chunk, 16 * chunk + 16)
                re, total, gap = (
                    [vectors[comp + colour, rows, :] for colour in range(3)]
                    for comp in (0, 6, 9)
                )
                at = 96 * low + 16 * chunk
                at = 256 * high + at if at < 256 else 256 + 32 * high + at
                for a in range(3):
                    b = (a + 1) % 3
                    c = (a + 2) % 3
                    shared = my_sum[b] * re[c] - my_sum[c] * re[b]
                    real = shared - (my_im[b] * total[c] - my_im[c] * total[b])
                    imag = shared + (my_re[b] * gap[c] - my_re[c] * gap[b])
                    column = a * SITES
                    out[slot, at : at + 16, column : column + SITES] = real.astype(
                        jnp.bfloat16
                    )
                    column += 3 * SITES
                    out[slot, at : at + 16, column : column + SITES] = imag.astype(
                        jnp.bfloat16
                    )


def spread(source, vectors):
    for colour in range(3):
        real = source[colour].astype(jnp.float32)
        imag = source[3 + colour].astype(jnp.float32)
        vectors[colour] = real
        vectors[3 + colour] = imag
        vectors[6 + colour] = real + imag
        vectors[9 + colour] = imag - real


def crossed_kernel(source, out, vectors):
    spread(source, vectors)

    def one_step(step, carry):
        six_rows(step, vectors, out, step)
        return carry

    lax.fori_loop(0, 4, one_step, 0)


def both_kernel(source, phased, previous, *rest):
    sums = rest[0] if len(rest) == 5 else None
    out, total, vectors, left = rest[-4:]
    spread(source, vectors)
    left_operand(phased, left)

    def one_step(step, carry):
        term = times(previous[step], left)
        total[step] = term if sums is None else sums[step] + term
        six_rows(step, vectors, out, step)
        return carry

    lax.fori_loop(0, 4, one_step, 0)


def half_kernel(half, source, phased, previous, sums, out, total, vectors, left):
    spread(source, vectors)
    left_operand(phased, left)

    def one_step(part, carry):
        step = 2 * half + part
        total[part] = sums[step] + times(previous[step], left)
        six_rows(step, vectors, out, part)
        return carry

    lax.fori_loop(0, 2, one_step, 0)


def last_kernel(phased, crossed, sums, out, left):
    left_operand(phased, left)
    tails = []
    for part in range(2):
        total = sums[part] + times(crossed[part], left)
        out[:, 512 * part : 512 * part + 512] = total[:512].T.astype(out.dtype)
        tails.append(total[512:])
    out[:, 1024:] = jnp.concatenate(tails, 0).T.astype(out.dtype)


def pack_kernel(mine, received, out, total):
    lane = lax.broadcasted_iota(jnp.int32, (8, SITES), 1)
    for tile in range(9):
        lanes = slice(SITES * tile, SITES * tile + SITES)
        total[tile] = mine[:, lanes] + received[:, lanes].astype(jnp.float32)
    for q in range(8):
        for zh in range(4):
            for half in range(2):
                out[4 * q + zh, 24 * half : 24 * half + 24, :] = total[
                    2 * zh + half, pl.ds(q, 24, 8), :
                ].astype(jnp.bfloat16)
        tail = total[8, pl.ds(q, 24, 8), :]
        for zh in range(4):
            joined = jnp.zeros((8, SITES), jnp.float32)
            for g in range(3):
                moved = pltpu.roll(tail[8 * g : 8 * g + 8], (32 * (g - zh)) % SITES, 1)
                joined = jnp.where(lane // 32 == g, moved, joined)
            out[4 * q + zh, 48:56, :] = joined.astype(jnp.bfloat16)


def final_kernel(parts, out, rows):
    scale = 1.0 / math.sqrt(LX * LY * LZ)
    for t in range(8):
        total = parts[4 * t].astype(jnp.float32)
        for zh in range(1, 4):
            total += parts[4 * t + zh].astype(jnp.float32)
        total *= scale
        rows[0, pl.ds(t, 24, 8), :] = total[:24]
        rows[1, pl.ds(t, 24, 8), :] = total[24:48]
        for g in range(3):
            tail = total[48:56]
            if g:
                tail = pltpu.roll(tail, SITES - 32 * g, 1)
            rows[2, pl.ds(64 * g + t, 8, 8), :] = tail
    for ri in range(2):
        pieces = [[], [], []]
        for i in range(12):
            at = 8 * (12 * ri + i)
            one, two, three = (rows[part, at : at + 8, :] for part in range(3))
            pieces[0].append(one[:, :96])
            pieces[1].append(one[:, 96:])
            pieces[1].append(two[:, :64])
            pieces[2].append(two[:, 64:])
            pieces[2].append(three[:, :32])
        for r in range(3):
            out[r, :, ri, :] = jnp.concatenate(pieces[r], axis=1)


def vmem():
    return pl.BlockSpec(memory_space=pltpu.VMEM)


def smem():
    return pl.BlockSpec(memory_space=pltpu.SMEM)


def params(mib):
    return pltpu.CompilerParams(vmem_limit_bytes=mib << 20)


def from_y(block, by):
    return lax.ppermute(block, "y", [(i, (i + by) % 4) for i in range(4)])


def on_device(vectors, gauge_links, momentum, direction):
    f32 = jnp.float32
    bf16 = jnp.bfloat16
    swap = [(0, 1), (1, 0)]
    own = jnp.transpose(vectors[0], (1, 2, 0, 3)).reshape(6, NEV, SITES)
    joined = jnp.concatenate(
        [
            own.reshape(6 * NEV, SITES),
            jnp.transpose(gauge_links[0], (0, 2, 3, 1, 4)).reshape(54, SITES),
            jnp.zeros((10, SITES), bf16),
        ]
    )
    outer = lax.ppermute(joined, AXES, ring_pairs(outer_plane))
    other = lax.ppermute(joined, "c", swap)
    before = from_y(own, 1)
    after = from_y(own, 3)
    opposite = from_y(own, 2)
    phased = pl.pallas_call(
        phased_kernel,
        out_shape=jax.ShapeDtypeStruct((6, NEV, SITES), bf16),
        in_specs=[vmem()] * 4,
        out_specs=vmem(),
        scratch_shapes=[pltpu.VMEM((6, NEV, SITES), f32)] * 3,
        compiler_params=params(8),
    )(jnp.concatenate([momentum, direction]), joined, other, outer)
    phased_before = from_y(phased, 1)
    phased_after = from_y(phased, 3)
    phased_opposite = from_y(phased, 2)
    before, after, opposite = lax.optimization_barrier((before, after, opposite))

    crossed_shape = jax.ShapeDtypeStruct((4, 576, DEPTH), bf16)
    sums_shape = jax.ShapeDtypeStruct((4, 576, 192), f32)
    spread_scratch = pltpu.VMEM((12, NEV, SITES), f32)
    left_scratch = pltpu.VMEM((192, DEPTH), bf16)
    short = pl.CostEstimate(flops=0, bytes_accessed=0, transcendentals=0)

    def both(source, phased_plane, previous, *sums):
        return pl.pallas_call(
            both_kernel,
            out_shape=(crossed_shape, sums_shape),
            in_specs=[vmem()] * (3 + len(sums)),
            out_specs=(vmem(), vmem()),
            scratch_shapes=[spread_scratch, left_scratch],
            compiler_params=params(6),
            cost_estimate=short,
        )(source, phased_plane, previous, *sums)

    crossed = pl.pallas_call(
        crossed_kernel,
        out_shape=crossed_shape,
        in_specs=[vmem()],
        out_specs=vmem(),
        scratch_shapes=[spread_scratch],
        compiler_params=params(4),
        cost_estimate=short,
    )(own)
    crossed, sums = both(before, phased, crossed)
    crossed, sums = both(after, phased_before, crossed, sums)

    def last(half, kind, crossed, sums):
        half_crossed, half_sums = pl.pallas_call(
            functools.partial(half_kernel, half),
            out_shape=(
                jax.ShapeDtypeStruct((2, 576, DEPTH), bf16),
                jax.ShapeDtypeStruct((2, 576, 192), f32),
            ),
            in_specs=[vmem()] * 4,
            out_specs=(vmem(), vmem()),
            scratch_shapes=[spread_scratch, left_scratch],
            compiler_params=params(6),
        )(opposite, phased_after, crossed, sums)
        return pl.pallas_call(
            last_kernel,
            out_shape=jax.ShapeDtypeStruct((192, 1152), kind),
            in_specs=[vmem()] * 3,
            out_specs=vmem(),
            scratch_shapes=[left_scratch],
            compiler_params=params(6),
        )(phased_opposite, half_crossed, half_sums)

    sent = last(0, bf16, crossed, sums)
    sent, sums = lax.optimization_barrier((sent, sums))
    received = lax.ppermute(sent, "c", swap)
    mine = last(1, f32, crossed, sums)
    packed = pl.pallas_call(
        pack_kernel,
        out_shape=jax.ShapeDtypeStruct((32, 56, SITES), bf16),
        in_specs=[vmem()] * 2,
        out_specs=vmem(),
        scratch_shapes=[pltpu.VMEM((9, 192, SITES), f32)],
        compiler_params=params(16),
    )(mine, received)
    packed = lax.all_to_all(packed, ("x", "zl", "zh"), 0, 0, tiled=True)
    return pl.pallas_call(
        final_kernel,
        out_shape=jax.ShapeDtypeStruct((3, 8, 2, 12 * NEV), f32),
        in_specs=[vmem()],
        out_specs=vmem(),
        scratch_shapes=[pltpu.VMEM((3, 192, SITES), f32)],
        compiler_params=params(16),
    )(packed)


def solution(mesh):
    cut = Mesh(mesh.devices.reshape(SIZES), AXES)
    return jax.shard_map(
        on_device,
        mesh=cut,
        in_specs=(
            P(("x", "zl"), None, None, None, ("y", "zh", "c")),
            P(("x", "zl"), None, None, None, None, ("y", "zh", "c")),
            P(),
            P(("x", "zl")),
        ),
        out_specs=P(("y", "zh", "c"), None, None, ("x", "zl")),
        check_vma=False,
    )
```

```python
import functools
import math

import jax
import jax.numpy as jnp
from jax import lax
from jax.experimental import pallas as pl
from jax.experimental.pallas import tpu as pltpu
from jax.sharding import Mesh
from jax.sharding import PartitionSpec as P

NEV = 96
LX = 16
LY = 8
LZ = 32
SITES = 128
AXES = ("x", "zl", "y", "zh", "c")
SIZES = (4, 2, 4, 4, 2)
DEPTH = 6 * SITES


def ring_pairs(target):
    pairs = []
    for x in range(4):
        for zl in range(2):
            for s in range(32):
                to = target(zl, s)
                if to is not None:
                    head = (x * 2 + zl) * 32
                    pairs.append((head + s, head + to))
    return pairs


def outer_plane(zl, s):
    if zl == 1:
        return None
    return (s + 1) % 32 if s % 2 == 1 else (s - 1) % 32


def phased_kernel(numbers, own, other, outer, out, field, ahead, behind):
    links = own[6 * NEV :, :].astype(jnp.float32)
    direction = numbers[3]
    core = lax.axis_index("c")
    plane = (lax.axis_index("y") * 4 + lax.axis_index("zh")) * 2 + core
    lane = lax.broadcasted_iota(jnp.int32, (1, SITES), 1)
    x_coord = lane % LX
    y_coord = lane // LX
    turns = (
        2 * jnp.bitwise_and(numbers[0] * x_coord, LX - 1)
        + 4 * jnp.bitwise_and(numbers[1] * y_coord, LY - 1)
        + jnp.bitwise_and(numbers[2] * plane, LZ - 1)
    )
    angle = (2.0 * math.pi / LZ) * jnp.bitwise_and(turns, LZ - 1).astype(jnp.float32)
    cos_part = jnp.cos(angle)
    sin_part = -jnp.sin(angle)

    @pl.when(direction == 2)
    def _():
        for comp in range(6):
            near = other[NEV * comp : NEV * comp + NEV, :].astype(jnp.float32)
            far = outer[NEV * comp : NEV * comp + NEV, :].astype(jnp.float32)
            ahead[comp] = jnp.where(core == 0, near, far)
            behind[comp] = jnp.where(core == 0, far, near)

    @pl.when(direction != 2)
    def _():
        step = jnp.where(direction == 0, 1, LX)
        last = jnp.logical_and(x_coord == LX - 1, direction == 0)
        first = jnp.logical_and(x_coord == 0, direction == 0)
        for comp in range(6):
            here = own[NEV * comp : NEV * comp + NEV, :].astype(jnp.float32)
            ahead[comp] = jnp.where(
                last, pltpu.roll(here, LX - 1, 1), pltpu.roll(here, SITES - step, 1)
            )
            behind[comp] = jnp.where(
                first, pltpu.roll(here, SITES - LX + 1, 1), pltpu.roll(here, step, 1)
            )

    z_back = jnp.where(
        core == 0,
        outer[6 * NEV :, :].astype(jnp.float32),
        other[6 * NEV :, :].astype(jnp.float32),
    )
    x_roll = jnp.where(
        x_coord == 0, pltpu.roll(links, SITES - LX + 1, 1), pltpu.roll(links, 1, 1)
    )
    y_roll = pltpu.roll(links, LX, 1)

    def matrix(table, part, row, column):
        return table[6 * row + 2 * column + part]

    here_link = []
    back_link = []
    for at in range(18):
        x_at, y_at, z_at = (slice(at + 18 * d, at + 18 * d + 1) for d in range(3))
        here_link.append(
            jnp.where(
                direction == 0, links[x_at], jnp.where(direction == 1, links[y_at], links[z_at])
            )
        )
        back_link.append(
            jnp.where(
                direction == 0,
                x_roll[x_at],
                jnp.where(direction == 1, y_roll[y_at], z_back[z_at]),
            )
        )

    for a in range(3):
        front_re = front_im = rear_re = rear_im = 0.0
        for b in range(3):
            u_re, u_im = matrix(here_link, 0, a, b), matrix(here_link, 1, a, b)
            v_re, v_im = ahead[b], ahead[3 + b]
            front_re += u_re * v_re - u_im * v_im
            front_im += u_re * v_im + u_im * v_re
            w_re, w_im = matrix(back_link, 0, b, a), matrix(back_link, 1, b, a)
            v_re, v_im = behind[b], behind[3 + b]
            rear_re += w_re * v_re + w_im * v_im
            rear_im += w_re * v_im - w_im * v_re
        moved_re = front_re - rear_re
        moved_im = front_im - rear_im
        field[a] = cos_part * moved_re - sin_part * moved_im
        field[3 + a] = cos_part * moved_im + sin_part * moved_re

    for comp in range(6):
        for rows in range(6):
            both = [field[comp, pl.ds(2 * rows + k, 8, 12), :] for k in range(2)]
            out[comp, 16 * rows : 16 * rows + 16, :] = jnp.concatenate(both, 0).astype(
                jnp.bfloat16
            )


def left_operand(phased, left):
    for a in range(3):
        real = phased[a]
        imag = phased[3 + a]
        column = a * SITES
        left[:NEV, column : column + SITES] = real
        left[NEV:, column : column + SITES] = imag
        column += 3 * SITES
        left[:NEV, column : column + SITES] = -imag
        left[NEV:, column : column + SITES] = real


def times(crossed, left):
    return lax.dot_general(
        crossed, left[...], (((1,), (1,)), ((), ())), preferred_element_type=jnp.float32
    )


def six_rows(step, vectors, out, slot):
    core = lax.axis_index("c")
    keeper = jnp.where(step < 2, 1 - core, core)
    first = 24 * lax.axis_index("y") + 12 * (step % 2) + 3 * keeper
    for high in range(2):
        for low in range(3):
            mine = [vectors[comp, pl.ds(first + 6 * high + low, 1), :] for comp in range(9)]
            mine = [jnp.broadcast_to(m, (16, SITES)) for m in mine]
            my_re, my_im, my_sum = mine[:3], mine[3:6], mine[6:]
            for chunk in range(6):
                rows = slice(16 * chunk, 16 * chunk + 16)
                re, total, gap = (
                    [vectors[comp + colour, rows, :] for colour in range(3)]
                    for comp in (0, 6, 9)
                )
                at = 96 * low + 16 * chunk
                at = 256 * high + at if at < 256 else 256 + 32 * high + at
                for a in range(3):
                    b = (a + 1) % 3
                    c = (a + 2) % 3
                    shared = my_sum[b] * re[c] - my_sum[c] * re[b]
                    real = shared - (my_im[b] * total[c] - my_im[c] * total[b])
                    imag = shared + (my_re[b] * gap[c] - my_re[c] * gap[b])
                    column = a * SITES
                    out[slot, at : at + 16, column : column + SITES] = real.astype(
                        jnp.bfloat16
                    )
                    column += 3 * SITES
                    out[slot, at : at + 16, column : column + SITES] = imag.astype(
                        jnp.bfloat16
                    )


def spread(source, vectors):
    for colour in range(3):
        real = source[colour].astype(jnp.float32)
        imag = source[3 + colour].astype(jnp.float32)
        vectors[colour] = real
        vectors[3 + colour] = imag
        vectors[6 + colour] = real + imag
        vectors[9 + colour] = imag - real


def crossed_kernel(source, out, vectors):
    spread(source, vectors)

    def one_step(step, carry):
        six_rows(step, vectors, out, step)
        return carry

    lax.fori_loop(0, 4, one_step, 0)


def both_kernel(source, phased, previous, *rest):
    sums = rest[0] if len(rest) == 5 else None
    out, total, vectors, left = rest[-4:]
    spread(source, vectors)
    left_operand(phased, left)

    def one_step(step, carry):
        term = times(previous[step], left)
        total[step] = term if sums is None else sums[step] + term
        six_rows(step, vectors, out, step)
        return carry

    lax.fori_loop(0, 4, one_step, 0)


def half_kernel(half, source, phased, previous, sums, out, total, vectors, left):
    spread(source, vectors)
    left_operand(phased, left)

    def one_step(part, carry):
        step = 2 * half + part
        total[part] = sums[step] + times(previous[step], left)
        six_rows(step, vectors, out, part)
        return carry

    lax.fori_loop(0, 2, one_step, 0)


def last_kernel(phased, crossed, sums, out, left):
    left_operand(phased, left)
    tails = []
    for part in range(2):
        total = sums[part] + times(crossed[part], left)
        out[:, 512 * part : 512 * part + 512] = total[:512].T.astype(out.dtype)
        tails.append(total[512:])
    out[:, 1024:] = jnp.concatenate(tails, 0).T.astype(out.dtype)


def pack_kernel(mine, received, out, total):
    lane = lax.broadcasted_iota(jnp.int32, (8, SITES), 1)
    for tile in range(9):
        lanes = slice(SITES * tile, SITES * tile + SITES)
        total[tile] = mine[:, lanes] + received[:, lanes].astype(jnp.float32)
    for q in range(8):
        for zh in range(4):
            for half in range(2):
                out[4 * q + zh, 24 * half : 24 * half + 24, :] = total[
                    2 * zh + half, pl.ds(q, 24, 8), :
                ].astype(jnp.bfloat16)
        tail = total[8, pl.ds(q, 24, 8), :]
        for zh in range(4):
            joined = jnp.zeros((8, SITES), jnp.float32)
            for g in range(3):
                moved = pltpu.roll(tail[8 * g : 8 * g + 8], (32 * (g - zh)) % SITES, 1)
                joined = jnp.where(lane // 32 == g, moved, joined)
            out[4 * q + zh, 48:56, :] = joined.astype(jnp.bfloat16)


def final_kernel(parts, out, rows):
    scale = 1.0 / math.sqrt(LX * LY * LZ)
    for t in range(8):
        total = parts[4 * t].astype(jnp.float32)
        for zh in range(1, 4):
            total += parts[4 * t + zh].astype(jnp.float32)
        total *= scale
        rows[0, pl.ds(t, 24, 8), :] = total[:24]
        rows[1, pl.ds(t, 24, 8), :] = total[24:48]
        for g in range(3):
            tail = total[48:56]
            if g:
                tail = pltpu.roll(tail, SITES - 32 * g, 1)
            rows[2, pl.ds(64 * g + t, 8, 8), :] = tail
    for ri in range(2):
        pieces = [[], [], []]
        for i in range(12):
            at = 8 * (12 * ri + i)
            one, two, three = (rows[part, at : at + 8, :] for part in range(3))
            pieces[0].append(one[:, :96])
            pieces[1].append(one[:, 96:])
            pieces[1].append(two[:, :64])
            pieces[2].append(two[:, 64:])
            pieces[2].append(three[:, :32])
        for r in range(3):
            out[r, :, ri, :] = jnp.concatenate(pieces[r], axis=1)


def vmem():
    return pl.BlockSpec(memory_space=pltpu.VMEM)


def smem():
    return pl.BlockSpec(memory_space=pltpu.SMEM)


def params(mib):
    return pltpu.CompilerParams(vmem_limit_bytes=mib << 20)


def from_y(block, by):
    return lax.ppermute(block, "y", [(i, (i + by) % 4) for i in range(4)])


def on_device(vectors, gauge_links, momentum, direction):
    f32 = jnp.float32
    bf16 = jnp.bfloat16
    swap = [(0, 1), (1, 0)]
    own = jnp.transpose(vectors[0], (1, 2, 0, 3)).reshape(6, NEV, SITES)
    joined = jnp.concatenate(
        [
            own.reshape(6 * NEV, SITES),
            jnp.transpose(gauge_links[0], (0, 2, 3, 1, 4)).reshape(54, SITES),
            jnp.zeros((10, SITES), bf16),
        ]
    )
    outer = lax.ppermute(joined, AXES, ring_pairs(outer_plane))
    other = lax.ppermute(joined, "c", swap)
    before = from_y(own, 1)
    after = from_y(own, 3)
    opposite = from_y(own, 2)
    phased = pl.pallas_call(
        phased_kernel,
        out_shape=jax.ShapeDtypeStruct((6, NEV, SITES), bf16),
        in_specs=[vmem()] * 4,
        out_specs=vmem(),
        scratch_shapes=[pltpu.VMEM((6, NEV, SITES), f32)] * 3,
        compiler_params=params(8),
    )(jnp.concatenate([momentum, direction]), joined, other, outer)
    phased_before = from_y(phased, 1)
    phased_after = from_y(phased, 3)
    phased_opposite = from_y(phased, 2)
    before, after, opposite = lax.optimization_barrier((before, after, opposite))

    crossed_shape = jax.ShapeDtypeStruct((4, 576, DEPTH), bf16)
    sums_shape = jax.ShapeDtypeStruct((4, 576, 192), f32)
    spread_scratch = pltpu.VMEM((12, NEV, SITES), f32)
    left_scratch = pltpu.VMEM((192, DEPTH), bf16)
    short = pl.CostEstimate(flops=0, bytes_accessed=0, transcendentals=0)

    def both(source, phased_plane, previous, *sums):
        return pl.pallas_call(
            both_kernel,
            out_shape=(crossed_shape, sums_shape),
            in_specs=[vmem()] * (3 + len(sums)),
            out_specs=(vmem(), vmem()),
            scratch_shapes=[spread_scratch, left_scratch],
            compiler_params=params(6),
            cost_estimate=short,
        )(source, phased_plane, previous, *sums)

    crossed = pl.pallas_call(
        crossed_kernel,
        out_shape=crossed_shape,
        in_specs=[vmem()],
        out_specs=vmem(),
        scratch_shapes=[spread_scratch],
        compiler_params=params(4),
        cost_estimate=short,
    )(own)
    crossed, sums = both(before, phased, crossed)
    crossed, sums = both(opposite, phased_before, crossed, sums)

    def last(half, kind, crossed, sums):
        half_crossed, half_sums = pl.pallas_call(
            functools.partial(half_kernel, half),
            out_shape=(
                jax.ShapeDtypeStruct((2, 576, DEPTH), bf16),
                jax.ShapeDtypeStruct((2, 576, 192), f32),
            ),
            in_specs=[vmem()] * 4,
            out_specs=(vmem(), vmem()),
            scratch_shapes=[spread_scratch, left_scratch],
            compiler_params=params(6),
        )(after, phased_opposite, crossed, sums)
        return pl.pallas_call(
            last_kernel,
            out_shape=jax.ShapeDtypeStruct((192, 1152), kind),
            in_specs=[vmem()] * 3,
            out_specs=vmem(),
            scratch_shapes=[left_scratch],
            compiler_params=params(6),
        )(phased_after, half_crossed, half_sums)

    sent = last(0, bf16, crossed, sums)
    sent, sums = lax.optimization_barrier((sent, sums))
    received = lax.ppermute(sent, "c", swap)
    mine = last(1, f32, crossed, sums)
    packed = pl.pallas_call(
        pack_kernel,
        out_shape=jax.ShapeDtypeStruct((32, 56, SITES), bf16),
        in_specs=[vmem()] * 2,
        out_specs=vmem(),
        scratch_shapes=[pltpu.VMEM((9, 192, SITES), f32)],
        compiler_params=params(16),
    )(mine, received)
    packed = lax.all_to_all(packed, ("x", "zl", "zh"), 0, 0, tiled=True)
    return pl.pallas_call(
        final_kernel,
        out_shape=jax.ShapeDtypeStruct((3, 8, 2, 12 * NEV), f32),
        in_specs=[vmem()],
        out_specs=vmem(),
        scratch_shapes=[pltpu.VMEM((3, 192, SITES), f32)],
        compiler_params=params(16),
    )(packed)


def solution(mesh):
    cut = Mesh(mesh.devices.reshape(SIZES), AXES)
    return jax.shard_map(
        on_device,
        mesh=cut,
        in_specs=(
            P(("x", "zl"), None, None, None, ("y", "zh", "c")),
            P(("x", "zl"), None, None, None, None, ("y", "zh", "c")),
            P(),
            P(("x", "zl")),
        ),
        out_specs=P(("y", "zh", "c"), None, None, ("x", "zl")),
        check_vma=False,
    )
```

```python
import functools
import math

import jax
import jax.numpy as jnp
from jax import lax
from jax.experimental import pallas as pl
from jax.experimental.pallas import tpu as pltpu
from jax.sharding import Mesh
from jax.sharding import PartitionSpec as P

NEV = 96
LX = 16
LY = 8
LZ = 32
SITES = 128
AXES = ("x", "zl", "y", "zh", "c")
SIZES = (4, 2, 4, 4, 2)
DEPTH = 6 * SITES


def ring_pairs(target):
    pairs = []
    for x in range(4):
        for zl in range(2):
            for s in range(32):
                to = target(zl, s)
                if to is not None:
                    head = (x * 2 + zl) * 32
                    pairs.append((head + s, head + to))
    return pairs


def outer_plane(zl, s):
    if zl == 1:
        return None
    return (s + 1) % 32 if s % 2 == 1 else (s - 1) % 32


def phased_kernel(numbers, own, other, outer, out, field, ahead, behind):
    links = own[6 * NEV :, :].astype(jnp.float32)
    direction = numbers[3]
    core = lax.axis_index("c")
    plane = (lax.axis_index("y") * 4 + lax.axis_index("zh")) * 2 + core
    lane = lax.broadcasted_iota(jnp.int32, (1, SITES), 1)
    x_coord = lane % LX
    y_coord = lane // LX
    turns = (
        2 * jnp.bitwise_and(numbers[0] * x_coord, LX - 1)
        + 4 * jnp.bitwise_and(numbers[1] * y_coord, LY - 1)
        + jnp.bitwise_and(numbers[2] * plane, LZ - 1)
    )
    angle = (2.0 * math.pi / LZ) * jnp.bitwise_and(turns, LZ - 1).astype(jnp.float32)
    cos_part = jnp.cos(angle)
    sin_part = -jnp.sin(angle)

    @pl.when(direction == 2)
    def _():
        for comp in range(6):
            near = other[NEV * comp : NEV * comp + NEV, :].astype(jnp.float32)
            far = outer[NEV * comp : NEV * comp + NEV, :].astype(jnp.float32)
            ahead[comp] = jnp.where(core == 0, near, far)
            behind[comp] = jnp.where(core == 0, far, near)

    @pl.when(direction != 2)
    def _():
        step = jnp.where(direction == 0, 1, LX)
        last = jnp.logical_and(x_coord == LX - 1, direction == 0)
        first = jnp.logical_and(x_coord == 0, direction == 0)
        for comp in range(6):
            here = own[NEV * comp : NEV * comp + NEV, :].astype(jnp.float32)
            ahead[comp] = jnp.where(
                last, pltpu.roll(here, LX - 1, 1), pltpu.roll(here, SITES - step, 1)
            )
            behind[comp] = jnp.where(
                first, pltpu.roll(here, SITES - LX + 1, 1), pltpu.roll(here, step, 1)
            )

    z_back = jnp.where(
        core == 0,
        outer[6 * NEV :, :].astype(jnp.float32),
        other[6 * NEV :, :].astype(jnp.float32),
    )
    x_roll = jnp.where(
        x_coord == 0, pltpu.roll(links, SITES - LX + 1, 1), pltpu.roll(links, 1, 1)
    )
    y_roll = pltpu.roll(links, LX, 1)

    def matrix(table, part, row, column):
        return table[6 * row + 2 * column + part]

    here_link = []
    back_link = []
    for at in range(18):
        x_at, y_at, z_at = (slice(at + 18 * d, at + 18 * d + 1) for d in range(3))
        here_link.append(
            jnp.where(
                direction == 0, links[x_at], jnp.where(direction == 1, links[y_at], links[z_at])
            )
        )
        back_link.append(
            jnp.where(
                direction == 0,
                x_roll[x_at],
                jnp.where(direction == 1, y_roll[y_at], z_back[z_at]),
            )
        )

    for a in range(3):
        front_re = front_im = rear_re = rear_im = 0.0
        for b in range(3):
            u_re, u_im = matrix(here_link, 0, a, b), matrix(here_link, 1, a, b)
            v_re, v_im = ahead[b], ahead[3 + b]
            front_re += u_re * v_re - u_im * v_im
            front_im += u_re * v_im + u_im * v_re
            w_re, w_im = matrix(back_link, 0, b, a), matrix(back_link, 1, b, a)
            v_re, v_im = behind[b], behind[3 + b]
            rear_re += w_re * v_re + w_im * v_im
            rear_im += w_re * v_im - w_im * v_re
        moved_re = front_re - rear_re
        moved_im = front_im - rear_im
        field[a] = cos_part * moved_re - sin_part * moved_im
        field[3 + a] = cos_part * moved_im + sin_part * moved_re

    for comp in range(6):
        for rows in range(6):
            both = [field[comp, pl.ds(2 * rows + k, 8, 12), :] for k in range(2)]
            out[comp, 16 * rows : 16 * rows + 16, :] = jnp.concatenate(both, 0).astype(
                jnp.bfloat16
            )


def left_operand(phased, left):
    for a in range(3):
        real = phased[a]
        imag = phased[3 + a]
        column = a * SITES
        left[:NEV, column : column + SITES] = real
        left[NEV:, column : column + SITES] = imag
        column += 3 * SITES
        left[:NEV, column : column + SITES] = -imag
        left[NEV:, column : column + SITES] = real


def times(crossed, left):
    return lax.dot_general(
        crossed, left[...], (((1,), (1,)), ((), ())), preferred_element_type=jnp.float32
    )


def six_rows(step, vectors, out, slot):
    core = lax.axis_index("c")
    keeper = jnp.where(step < 2, 1 - core, core)
    first = 24 * lax.axis_index("y") + 12 * (step % 2) + 3 * keeper
    for high in range(2):
        for low in range(3):
            mine = [vectors[comp, pl.ds(first + 6 * high + low, 1), :] for comp in range(9)]
            mine = [jnp.broadcast_to(m, (16, SITES)) for m in mine]
            my_re, my_im, my_sum = mine[:3], mine[3:6], mine[6:]
            for chunk in range(6):
                rows = slice(16 * chunk, 16 * chunk + 16)
                re, total, gap = (
                    [vectors[comp + colour, rows, :] for colour in range(3)]
                    for comp in (0, 6, 9)
                )
                at = 96 * low + 16 * chunk
                at = 256 * high + at if at < 256 else 256 + 32 * high + at
                for a in range(3):
                    b = (a + 1) % 3
                    c = (a + 2) % 3
                    shared = my_sum[b] * re[c] - my_sum[c] * re[b]
                    real = shared - (my_im[b] * total[c] - my_im[c] * total[b])
                    imag = shared + (my_re[b] * gap[c] - my_re[c] * gap[b])
                    column = a * SITES
                    out[slot, at : at + 16, column : column + SITES] = real.astype(
                        jnp.bfloat16
                    )
                    column += 3 * SITES
                    out[slot, at : at + 16, column : column + SITES] = imag.astype(
                        jnp.bfloat16
                    )


def spread(source, vectors):
    for colour in range(3):
        real = source[colour].astype(jnp.float32)
        imag = source[3 + colour].astype(jnp.float32)
        vectors[colour] = real
        vectors[3 + colour] = imag
        vectors[6 + colour] = real + imag
        vectors[9 + colour] = imag - real


def crossed_kernel(source, out, vectors):
    spread(source, vectors)

    def one_step(step, carry):
        six_rows(step, vectors, out, step)
        return carry

    lax.fori_loop(0, 4, one_step, 0)


def both_kernel(source, phased, previous, *rest):
    sums = rest[0] if len(rest) == 5 else None
    out, total, vectors, left = rest[-4:]
    spread(source, vectors)
    left_operand(phased, left)

    def one_step(step, carry):
        term = times(previous[step], left)
        total[step] = term if sums is None else sums[step] + term
        six_rows(step, vectors, out, step)
        return carry

    lax.fori_loop(0, 4, one_step, 0)


def half_kernel(half, source, phased, previous, sums, out, total, vectors, left):
    spread(source, vectors)
    left_operand(phased, left)

    def one_step(part, carry):
        step = 2 * half + part
        total[part] = sums[step] + times(previous[step], left)
        six_rows(step, vectors, out, part)
        return carry

    lax.fori_loop(0, 2, one_step, 0)


def last_kernel(phased, crossed, sums, out, left):
    left_operand(phased, left)
    tails = []
    for part in range(2):
        total = sums[part] + times(crossed[part], left)
        out[:, 512 * part : 512 * part + 512] = total[:512].T.astype(out.dtype)
        tails.append(total[512:])
    out[:, 1024:] = jnp.concatenate(tails, 0).T.astype(out.dtype)


def mine_kernel(source, phased, previous, sums, last, out, crossed, total, vectors, left):
    half_kernel(1, source, phased, previous, sums, crossed, total, vectors, left)
    last_kernel(last, crossed, total, out, left)


def pack_kernel(mine, received, out, total):
    lane = lax.broadcasted_iota(jnp.int32, (8, SITES), 1)
    for tile in range(9):
        lanes = slice(SITES * tile, SITES * tile + SITES)
        total[tile] = mine[:, lanes] + received[:, lanes].astype(jnp.float32)
    for q in range(8):
        for zh in range(4):
            for half in range(2):
                out[4 * q + zh, 24 * half : 24 * half + 24, :] = total[
                    2 * zh + half, pl.ds(q, 24, 8), :
                ].astype(jnp.bfloat16)
        tail = total[8, pl.ds(q, 24, 8), :]
        for zh in range(4):
            joined = jnp.zeros((8, SITES), jnp.float32)
            for g in range(3):
                moved = pltpu.roll(tail[8 * g : 8 * g + 8], (32 * (g - zh)) % SITES, 1)
                joined = jnp.where(lane // 32 == g, moved, joined)
            out[4 * q + zh, 48:56, :] = joined.astype(jnp.bfloat16)


def final_kernel(parts, out, rows):
    scale = 1.0 / math.sqrt(LX * LY * LZ)
    for t in range(8):
        total = parts[4 * t].astype(jnp.float32)
        for zh in range(1, 4):
            total += parts[4 * t + zh].astype(jnp.float32)
        total *= scale
        rows[0, pl.ds(t, 24, 8), :] = total[:24]
        rows[1, pl.ds(t, 24, 8), :] = total[24:48]
        for g in range(3):
            tail = total[48:56]
            if g:
                tail = pltpu.roll(tail, SITES - 32 * g, 1)
            rows[2, pl.ds(64 * g + t, 8, 8), :] = tail
    for ri in range(2):
        pieces = [[], [], []]
        for i in range(12):
            at = 8 * (12 * ri + i)
            one, two, three = (rows[part, at : at + 8, :] for part in range(3))
            pieces[0].append(one[:, :96])
            pieces[1].append(one[:, 96:])
            pieces[1].append(two[:, :64])
            pieces[2].append(two[:, 64:])
            pieces[2].append(three[:, :32])
        for r in range(3):
            out[r, :, ri, :] = jnp.concatenate(pieces[r], axis=1)


def vmem():
    return pl.BlockSpec(memory_space=pltpu.VMEM)


def smem():
    return pl.BlockSpec(memory_space=pltpu.SMEM)


def params(mib):
    return pltpu.CompilerParams(vmem_limit_bytes=mib << 20)


def from_y(block, by):
    return lax.ppermute(block, "y", [(i, (i + by) % 4) for i in range(4)])


def on_device(vectors, gauge_links, momentum, direction):
    f32 = jnp.float32
    bf16 = jnp.bfloat16
    swap = [(0, 1), (1, 0)]
    own = jnp.transpose(vectors[0], (1, 2, 0, 3)).reshape(6, NEV, SITES)
    joined = jnp.concatenate(
        [
            own.reshape(6 * NEV, SITES),
            jnp.transpose(gauge_links[0], (0, 2, 3, 1, 4)).reshape(54, SITES),
            jnp.zeros((10, SITES), bf16),
        ]
    )
    outer = lax.ppermute(joined, AXES, ring_pairs(outer_plane))
    other = lax.ppermute(joined, "c", swap)
    before = from_y(own, 1)
    after = from_y(own, 3)
    opposite = from_y(own, 2)
    phased = pl.pallas_call(
        phased_kernel,
        out_shape=jax.ShapeDtypeStruct((6, NEV, SITES), bf16),
        in_specs=[vmem()] * 4,
        out_specs=vmem(),
        scratch_shapes=[pltpu.VMEM((6, NEV, SITES), f32)] * 3,
        compiler_params=params(8),
    )(jnp.concatenate([momentum, direction]), joined, other, outer)
    phased_before = from_y(phased, 1)
    phased_after = from_y(phased, 3)
    phased_opposite = from_y(phased, 2)
    before, after, opposite = lax.optimization_barrier((before, after, opposite))

    crossed_shape = jax.ShapeDtypeStruct((4, 576, DEPTH), bf16)
    sums_shape = jax.ShapeDtypeStruct((4, 576, 192), f32)
    spread_scratch = pltpu.VMEM((12, NEV, SITES), f32)
    left_scratch = pltpu.VMEM((192, DEPTH), bf16)
    short = pl.CostEstimate(flops=0, bytes_accessed=0, transcendentals=0)

    def both(source, phased_plane, previous, *sums):
        return pl.pallas_call(
            both_kernel,
            out_shape=(crossed_shape, sums_shape),
            in_specs=[vmem()] * (3 + len(sums)),
            out_specs=(vmem(), vmem()),
            scratch_shapes=[spread_scratch, left_scratch],
            compiler_params=params(6),
            cost_estimate=short,
        )(source, phased_plane, previous, *sums)

    crossed = pl.pallas_call(
        crossed_kernel,
        out_shape=crossed_shape,
        in_specs=[vmem()],
        out_specs=vmem(),
        scratch_shapes=[spread_scratch],
        compiler_params=params(4),
        cost_estimate=short,
    )(own)
    crossed, sums = both(before, phased, crossed)
    crossed, sums = both(after, phased_before, crossed, sums)

    def last(half, kind, crossed, sums):
        half_crossed, half_sums = pl.pallas_call(
            functools.partial(half_kernel, half),
            out_shape=(
                jax.ShapeDtypeStruct((2, 576, DEPTH), bf16),
                jax.ShapeDtypeStruct((2, 576, 192), f32),
            ),
            in_specs=[vmem()] * 4,
            out_specs=(vmem(), vmem()),
            scratch_shapes=[spread_scratch, left_scratch],
            compiler_params=params(6),
        )(opposite, phased_after, crossed, sums)
        return pl.pallas_call(
            last_kernel,
            out_shape=jax.ShapeDtypeStruct((192, 1152), kind),
            in_specs=[vmem()] * 3,
            out_specs=vmem(),
            scratch_shapes=[left_scratch],
            compiler_params=params(6),
        )(phased_opposite, half_crossed, half_sums)

    sent = last(0, bf16, crossed, sums)
    sent, sums = lax.optimization_barrier((sent, sums))
    received = lax.ppermute(sent, "c", swap)
    mine = pl.pallas_call(
        mine_kernel,
        out_shape=jax.ShapeDtypeStruct((192, 1152), f32),
        in_specs=[vmem()] * 5,
        out_specs=vmem(),
        scratch_shapes=[
            pltpu.VMEM((2, 576, DEPTH), bf16),
            pltpu.VMEM((2, 576, 192), f32),
            spread_scratch,
            left_scratch,
        ],
        compiler_params=params(10),
    )(opposite, phased_after, crossed, sums, phased_opposite)
    packed = pl.pallas_call(
        pack_kernel,
        out_shape=jax.ShapeDtypeStruct((32, 56, SITES), bf16),
        in_specs=[vmem()] * 2,
        out_specs=vmem(),
        scratch_shapes=[pltpu.VMEM((9, 192, SITES), f32)],
        compiler_params=params(16),
    )(mine, received)
    packed = lax.all_to_all(packed, ("x", "zl", "zh"), 0, 0, tiled=True)
    return pl.pallas_call(
        final_kernel,
        out_shape=jax.ShapeDtypeStruct((3, 8, 2, 12 * NEV), f32),
        in_specs=[vmem()],
        out_specs=vmem(),
        scratch_shapes=[pltpu.VMEM((3, 192, SITES), f32)],
        compiler_params=params(16),
    )(packed)


def solution(mesh):
    cut = Mesh(mesh.devices.reshape(SIZES), AXES)
    return jax.shard_map(
        on_device,
        mesh=cut,
        in_specs=(
            P(("x", "zl"), None, None, None, ("y", "zh", "c")),
            P(("x", "zl"), None, None, None, None, ("y", "zh", "c")),
            P(),
            P(("x", "zl")),
        ),
        out_specs=P(("y", "zh", "c"), None, None, ("x", "zl")),
        check_vma=False,
    )
```
